128 devices in a mesh: seq: 8 (over y, x_lo), fsdp: 16 (over z, x_hi, core).
Axes of the slice: x: 4 (x_hi: 2, x_lo: 2; x = x_hi * 2 + x_lo), y: 4, z: 4, core: 2. Of those that a mesh axis runs over, the one named last changes fastest.
Arguments:
- tokens: bfloat16 [16, 1024, 1536], P('fsdp', 'seq'), may hold values from -6 to 6
- segments: int32 [16, 1024], P('fsdp', 'seq'), may hold values from 0 to 2, as said below
- out_grad: bfloat16 [16, 1024, 1536], P('fsdp', 'seq'), may hold values from -6 to 6
- attn_gain: bfloat16 [1536], P('fsdp'), may hold values from 0.5 to 1.5
- w_query: bfloat16 [1536, 1536], P('fsdp'), may hold values from -0.15625 to 0.15625
- key_projection: bfloat16 [1536, 512], P('fsdp'), may hold values from -0.15625 to 0.15625
- value_projection: bfloat16 [1536, 512], P('fsdp'), may hold values from -0.15625 to 0.15625
- query_gain: bfloat16 [64], P('fsdp'), may hold values from 0.5 to 1.5
- key_norm_gain: bfloat16 [64], P('fsdp'), may hold values from 0.5 to 1.5
- w_out: bfloat16 [1536, 1536], P(None, 'fsdp'), may hold values from -0.875 to 0.875
- mlp_gain: bfloat16 [1536], P('fsdp'), may hold values from 0.5 to 1.5
- w_gate: bfloat16 [1536, 6912], P('fsdp', 'seq'), may hold values from -0.15625 to 0.15625
- w_up: bfloat16 [1536, 6912], P('fsdp', 'seq'), may hold values from -0.15625 to 0.15625
- w_down: bfloat16 [6912, 1536], P('seq', 'fsdp'), may hold values from -0.15625 to 0.15625
Outputs:
- layer_out: bfloat16 [16, 1024, 1536], P('fsdp', 'seq')
- grad_tokens: float32 [16, 1024, 1536], P('fsdp', 'seq')
- grad_attn_gain: float32 [1536], P('fsdp')
- grad_w_query: float32 [1536, 1536], P('fsdp')
- grad_w_key: float32 [1536, 512], P('fsdp')
- grad_w_value: float32 [1536, 512], P('fsdp')
- grad_query_gain: float32 [64], P('fsdp')
- grad_key_gain: float32 [64], P('fsdp')
- grad_w_out: float32 [1536, 1536], P(None, 'fsdp')
- grad_mlp_gain: float32 [1536], P('fsdp')
- grad_w_gate: float32 [1536, 6912], P('fsdp', 'seq')
- grad_w_up: float32 [1536, 6912], P('fsdp', 'seq')
- grad_w_down: float32 [6912, 1536], P('seq', 'fsdp')
The draws below stay inside these ranges and needn't reach their ends.
Inputs may be any that keep to these rules, and one draw needn't show every extreme that they name: `segments`: within a sequence segment numbers start at 0, never fall and rise by one where a document starts; a sequence holds at most three documents, each of 64 tokens or more; of the 1 sequence of each index of fsdp, one drawn from the seed has three documents, the middle one starting within the first 128 tokens and ending within the last 128.
All inputs are finite; a program needn't handle non-finite values.
Results may differ from the reference program's by a relative error of at most 0.02.
Values may be sent and summed in bfloat16 or wider, within the bound.
No kernel may reach another device: no remote copies, remote signals or barrier semaphores. Data moves between devices by JAX's collectives and lax.ppermute only.
A program may use at most 192 MiB of HBM per device.

```python
import math
import jax
import jax.numpy as jnp
from jax import lax

MODEL_WIDTH = 1536
HQ = 24
KEY_VALUE_HEADS = 8
HEAD_SIZE = 64
FF = 6912
SEQ_LEN = 1024
SEQS = 1
BATCH = 16


def draw_segments(key, part):
    key = jax.random.fold_in(key, 11)
    cut_key, keep_key, first_key, last_key, pick_key = jax.random.split(key, 5)
    eighth = SEQ_LEN // 8
    jitter = SEQ_LEN // 32
    places = jnp.arange(SEQ_LEN, dtype=jnp.int32)
    grid_cuts = jnp.arange(1, 8, dtype=jnp.int32) * eighth
    offsets = jax.random.randint(cut_key, (BATCH, 7), -jitter, jitter + 1)
    keep_flags = jax.random.randint(keep_key, (BATCH, 7), 0, 2)
    cuts = grid_cuts[None, :] + offsets
    regular = jnp.sum(keep_flags[:, :, None] * (places[None, None, :] >= cuts[:, :, None]).astype(jnp.int32), axis=1)
    regular = jnp.minimum(regular, 2)
    first_cut = jax.random.randint(first_key, (BATCH,), SEQ_LEN // 16, eighth)
    last_cut = jax.random.randint(last_key, (BATCH,), SEQ_LEN - eighth + 1, SEQ_LEN - SEQ_LEN // 16 + 1)
    spanning = (places[None, :] >= first_cut[:, None]).astype(jnp.int32) + (places[None, :] >= last_cut[:, None]).astype(jnp.int32)
    picked = jax.random.randint(pick_key, (BATCH // SEQS,), 0, SEQS)
    chosen = jnp.arange(BATCH, dtype=jnp.int32) % SEQS == jnp.repeat(picked, SEQS)
    return jnp.where(chosen[:, None], spanning, regular).astype(jnp.int32)


def steps_of(key, extent, cuts, smallest, high):
    def one(axis_at, blocks):
        draws = jax.random.uniform(jax.random.fold_in(jax.random.fold_in(key, 6), axis_at), (blocks,), jnp.float32, smallest / len(cuts), high / len(cuts))
        return jnp.repeat(jnp.exp(draws), extent[axis_at] // blocks).reshape((-1,) + (1,) * (len(extent) - axis_at - 1))

    loudness = one(*cuts[0])
    for cut in cuts[1:]:
        loudness = loudness * one(*cut)
    return loudness


def scatter_about(own_key, extent, scale, most, shards=(), held_as=jnp.bfloat16):
    level = steps_of(own_key, extent, shards, -0.22, 0.18) if shards else 1.0
    values = jax.random.normal(own_key, extent, jnp.float32) * scale * level
    return jnp.minimum(jnp.maximum(values, -most), most).astype(held_as)


def setup_inputs(seed: int = 0) -> dict:
    keys = jax.random.split(jax.random.key(seed), 15)
    return {
        "tokens": scatter_about(keys[0], (BATCH, SEQ_LEN, MODEL_WIDTH), 1.0, 6.0, ((0, 16), (1, 8))),
        "segments": draw_segments(jax.random.fold_in(keys[14], 71), 0),
        "out_grad": scatter_about(keys[2], (BATCH, SEQ_LEN, MODEL_WIDTH), 1.0, 6.0, ((0, 16), (1, 8))),
        "attn_gain": jnp.clip(0.5 + 1.0 * jax.random.uniform(keys[3], (MODEL_WIDTH,), jnp.float32) ** steps_of(keys[3], (MODEL_WIDTH,), ((0, 16),), -0.2, 0.2), 0.5, 1.5).astype(jnp.bfloat16),
        "w_query": scatter_about(keys[4], (MODEL_WIDTH, HQ * HEAD_SIZE), MODEL_WIDTH ** -0.5, 0.15625, ((0, 16),)),
        "key_projection": scatter_about(keys[5], (MODEL_WIDTH, KEY_VALUE_HEADS * HEAD_SIZE), MODEL_WIDTH ** -0.5, 0.15625, ((0, 16),)),
        "value_projection": scatter_about(keys[6], (MODEL_WIDTH, KEY_VALUE_HEADS * HEAD_SIZE), MODEL_WIDTH ** -0.5, 0.15625, ((0, 16),)),
        "query_gain": jnp.clip(0.5 + 1.0 * jax.random.uniform(keys[7], (HEAD_SIZE,), jnp.float32) ** steps_of(keys[7], (HEAD_SIZE,), ((0, 16),), -0.2, 0.2), 0.5, 1.5).astype(jnp.bfloat16),
        "key_norm_gain": jnp.clip(0.5 + 1.0 * jax.random.uniform(keys[8], (HEAD_SIZE,), jnp.float32) ** steps_of(keys[8], (HEAD_SIZE,), ((0, 16),), -0.2, 0.2), 0.5, 1.5).astype(jnp.bfloat16),
        "w_out": scatter_about(keys[9], (HQ * HEAD_SIZE, MODEL_WIDTH), (HQ * HEAD_SIZE // 32) ** -0.5, 0.875, ((1, 16),)),
        "mlp_gain": jnp.clip(0.5 + 1.0 * jax.random.uniform(keys[10], (MODEL_WIDTH,), jnp.float32) ** steps_of(keys[10], (MODEL_WIDTH,), ((0, 16),), -0.2, 0.2), 0.5, 1.5).astype(jnp.bfloat16),
        "w_gate": scatter_about(keys[11], (MODEL_WIDTH, FF), MODEL_WIDTH ** -0.5, 0.15625, ((0, 16), (1, 8))),
        "w_up": scatter_about(keys[12], (MODEL_WIDTH, FF), MODEL_WIDTH ** -0.5, 0.15625, ((0, 16), (1, 8))),
        "w_down": scatter_about(keys[13], (FF, MODEL_WIDTH), (FF // 4) ** -0.5, 0.15625, ((0, 8), (1, 16))),
    }


@jax.custom_vjp
def reduced_precision(v):
    return lax.optimization_barrier(v.astype(jnp.bfloat16)).astype(jnp.float32)

@jax.custom_vjp
def reduced_precision_backward(v):
    return v

def low_keep(v):
    return (reduced_precision(v), None)

def low_pass(kept, grad):
    return (grad,)

def back_keep(v):
    return (v, None)

def back_low(kept, grad):
    return (reduced_precision(grad),)
reduced_precision.defvjp(low_keep, low_pass)
reduced_precision_backward.defvjp(back_keep, back_low)
eps = 1e-05
rope_base = 1000000.0
highest = lax.Precision.HIGHEST

def matmul(left, right):
    return jnp.einsum('...i,ij->...j', left, right, precision=highest)

def apply_norm(values, norm_gain):
    inverse = lax.rsqrt(lax.optimization_barrier(jnp.mean(values * values, axis=-1, keepdims=True)) + eps)
    return values * inverse * norm_gain

def apply_rotary(values, token_position):
    halfway = values.shape[-1] // 2
    frequency = rope_base ** (-2.0 * jnp.arange(halfway, dtype=jnp.float32) / values.shape[-1])
    angles = token_position[..., None, None] * frequency
    cosine = jnp.cos(angles)
    sine_part = jnp.sin(angles)
    leading = values[..., :halfway]
    trailing = values[..., halfway:]
    return jnp.concatenate([leading * cosine - trailing * sine_part, trailing * cosine + leading * sine_part], axis=-1)

def doc_positions(seg_ids):
    earlier = lax.optimization_barrier(jnp.sum((seg_ids[..., None, :] < seg_ids[..., :, None]).astype(jnp.int32), axis=-1))
    indices = jnp.arange(seg_ids.shape[-1], dtype=jnp.int32)
    return (indices - earlier).astype(jnp.float32)

def attend(inputs):
    queries, key_head_rows, value_heads, seg_ids = inputs
    length_total = queries.shape[0]
    head_groups = key_head_rows.shape[1] // HEAD_SIZE
    grouped = queries.reshape(length_total, head_groups, -1, HEAD_SIZE)
    key_split = key_head_rows.reshape(length_total, head_groups, HEAD_SIZE)
    value_split = value_heads.reshape(length_total, head_groups, HEAD_SIZE)
    scores = reduced_precision_backward(jnp.einsum('qhgd,khd->hgqk', grouped, key_split, precision=highest) * HEAD_SIZE ** (-0.5))
    indices = jnp.arange(length_total)
    allowed = (indices[None, :] <= indices[:, None]) & (seg_ids[None, :] == seg_ids[:, None])
    scores = jnp.where(allowed, scores, -1e+30)
    weights = reduced_precision(jax.nn.softmax(scores, axis=-1))
    mixed_out = jnp.einsum('hgqk,khd->qhgd', weights, value_split, precision=highest)
    return mixed_out.reshape(length_total, -1)

def block_layer(tokens_f, seg_ids, attn_gain, w_query, key_projection, value_projection, query_gain, key_norm_gain, w_out, mlp_gain, w_gate, w_up, w_down):
    sequence_rows = tokens_f.shape[0]
    length_total = tokens_f.shape[1]
    token_position = doc_positions(seg_ids)
    normed_input = reduced_precision(apply_norm(tokens_f, attn_gain))
    query_unnormed = reduced_precision_backward(matmul(normed_input, w_query))
    key_unnormed = reduced_precision_backward(matmul(normed_input, key_projection))
    value_all = reduced_precision_backward(reduced_precision(matmul(normed_input, value_projection)))
    query_heads = apply_rotary(apply_norm(query_unnormed.reshape(sequence_rows, length_total, HQ, HEAD_SIZE), query_gain), token_position)
    key_head_rows = apply_rotary(apply_norm(key_unnormed.reshape(sequence_rows, length_total, KEY_VALUE_HEADS, HEAD_SIZE), key_norm_gain), token_position)
    query_send = reduced_precision_backward(reduced_precision(query_heads.reshape(sequence_rows, length_total, HQ * HEAD_SIZE)))
    key_outgoing = reduced_precision_backward(reduced_precision(key_head_rows.reshape(sequence_rows, length_total, KEY_VALUE_HEADS * HEAD_SIZE)))
    attended = lax.map(jax.checkpoint(attend), (query_send, key_outgoing, value_all, seg_ids))
    attended = reduced_precision_backward(reduced_precision(attended))
    branch_output = reduced_precision_backward(matmul(attended, w_out))
    middle = tokens_f + branch_output
    second = reduced_precision(apply_norm(middle, mlp_gain))
    gate_before_activation = reduced_precision_backward(matmul(second, w_gate))
    upward_projection = reduced_precision_backward(matmul(second, w_up))
    hidden = reduced_precision(jax.nn.silu(gate_before_activation) * upward_projection)
    return middle + matmul(hidden, w_down)

def reference(tokens, segments, out_grad, attn_gain, w_query, key_projection, value_projection, query_gain, key_norm_gain, w_out, mlp_gain, w_gate, w_up, w_down):
    weights = (attn_gain, w_query, key_projection, value_projection, query_gain, key_norm_gain, w_out, mlp_gain, w_gate, w_up, w_down)
    weights = tuple((matrix.astype(jnp.float32) for matrix in weights))
    together = math.gcd(BATCH, max(1, 4096 // SEQ_LEN))
    blocks = BATCH // together
    inputs = (tokens.astype(jnp.float32).reshape(blocks, together, SEQ_LEN, MODEL_WIDTH), segments.reshape(blocks, together, SEQ_LEN), out_grad.astype(jnp.float32).reshape(blocks, together, SEQ_LEN, MODEL_WIDTH))

    def advance(totals, element):
        block_tokens, block_ids, block_grad = element

        def forward(tokens_f, *params):
            return block_layer(tokens_f, block_ids, *params)
        result, backward = jax.vjp(forward, block_tokens, *weights)
        gradients = backward(block_grad)
        totals = tuple((running + fresh_grad for running, fresh_grad in zip(totals, gradients[1:])))
        return (totals, (result.astype(jnp.bfloat16), gradients[0]))
    initial = tuple((jnp.zeros_like(matrix) for matrix in weights))
    totals, (results, input_grads) = lax.scan(advance, initial, inputs)
    return (results.reshape(BATCH, SEQ_LEN, MODEL_WIDTH), input_grads.reshape(BATCH, SEQ_LEN, MODEL_WIDTH), totals[0], totals[1], totals[2], totals[3], totals[4], totals[5], totals[6], totals[7], totals[8], totals[9], totals[10])
```

```python
from functools import partial

import jax
import jax.numpy as jnp
from jax import lax
from jax.sharding import PartitionSpec as P

HEAD = 64
EPS = 1e-05
ROPE_BASE = 1000000.0
F32 = jnp.float32
BF16 = jnp.bfloat16
PAD = 896


def rms_norm(values, gain):
    inverse = lax.rsqrt(jnp.mean(values * values, axis=-1, keepdims=True) + EPS)
    return values * inverse * gain


def shift(size, by):
    return [(i, (i + by) % size) for i in range(size)]


def gather_seq(block):
    n = lax.axis_size("seq")
    me = lax.axis_index("seq")
    whole = jnp.zeros((n,) + block.shape, block.dtype)
    whole = lax.dynamic_update_index_in_dim(whole, block, me, 0)
    for by in range(1, n):
        got = lax.ppermute(block, "seq", shift(n, by))
        whole = lax.dynamic_update_index_in_dim(whole, got, (me - by) % n, 0)
    return whole


def scatter_sum_seq(blocks):
    n = lax.axis_size("seq")
    me = lax.axis_index("seq")
    got = [
        lax.ppermute(
            lax.dynamic_index_in_dim(blocks, (me + by) % n, 0, keepdims=False), "seq", shift(n, by)
        )
        for by in range(1, n)
    ]
    total = lax.dynamic_index_in_dim(blocks, me, 0, keepdims=False).astype(F32)
    for block in got:
        total = total + block.astype(F32)
    return total


def gather_fsdp(block):
    n = lax.axis_size("fsdp")
    me = lax.axis_index("fsdp")
    held = block[None]
    for bit in (1, 2):
        other = lax.ppermute(held, "fsdp", [(i, i ^ bit) for i in range(n)])
        low = (me & bit) == 0
        held = jnp.concatenate([jnp.where(low, held, other), jnp.where(low, other, held)], axis=0)
    quad = held.shape[0]
    whole = jnp.zeros((n,) + block.shape, block.dtype)
    whole = lax.dynamic_update_slice_in_dim(whole, held, me // quad * quad, 0)
    for by in range(quad, n, quad):
        got = lax.ppermute(held, "fsdp", shift(n, by))
        whole = lax.dynamic_update_slice_in_dim(whole, got, (me - by) % n // quad * quad, 0)
    return whole.reshape((n * block.shape[0],) + block.shape[1:])


def rotary(values, cosine, sine):
    half = values.shape[-1] // 2
    a, b = values[..., :half], values[..., half:]
    return jnp.concatenate([a * cosine - b * sine, b * cosine + a * sine], axis=-1)


def prep(raw, gain, cosine, sine):
    shaped = raw.reshape(raw.shape[0], -1, HEAD)
    return rotary(rms_norm(shaped, gain), cosine[:, None, :], sine[:, None, :]).reshape(raw.shape)


def mm(a, b):
    return jnp.dot(a, b, preferred_element_type=F32)


def mm_nt(a, b):
    return lax.dot_general(a, b, (((1,), (1,)), ((), ())), preferred_element_type=F32)


def mm_tn(a, b):
    return lax.dot_general(a, b, (((0,), (0,)), ((), ())), preferred_element_type=F32)


def masked_scores(q, k, allowed):
    scores = jnp.einsum("qhd,kd->hqk", q, k, preferred_element_type=F32) * HEAD**-0.5
    return jnp.where(allowed, scores, -1e30)


def attend(q, k, v, allowed):
    grouped = q.reshape(q.shape[0], -1, HEAD)
    scores = masked_scores(grouped, k, allowed)
    peak = jnp.max(scores, axis=-1, keepdims=True)
    exps = jnp.exp(scores - peak)
    total = jnp.sum(exps, axis=-1, keepdims=True)
    probs = (exps / total).astype(BF16)
    mixed = jnp.einsum("hqk,kd->qhd", probs, v, preferred_element_type=F32)
    return mixed.reshape(q.shape).astype(BF16), peak + jnp.log(total)


def attend_back(q, k, v, allowed, lse, grad):
    grouped = q.reshape(q.shape[0], -1, HEAD)
    probs = jnp.exp(masked_scores(grouped, k, allowed) - lse)
    grads = grad.reshape(grouped.shape)
    grad_probs = jnp.einsum("qhd,kd->hqk", grads, v, preferred_element_type=F32)
    inner = jnp.sum(probs * grad_probs, axis=-1, keepdims=True)
    grad_scores = (probs * (grad_probs - inner)).astype(BF16)
    gq = jnp.einsum("hqk,kd->qhd", grad_scores, k, preferred_element_type=F32) * HEAD**-0.5
    gk = jnp.einsum("hqk,qhd->kd", grad_scores, grouped, preferred_element_type=F32) * HEAD**-0.5
    gv = jnp.einsum("hqk,qhd->kd", probs.astype(BF16), grads, preferred_element_type=F32)
    return gq.reshape(q.shape).astype(BF16), gk.astype(BF16), gv.astype(BF16)


def lanes(array, width):
    return jnp.pad(array, ((0, 0), (0, width - array.shape[1])))


def rows(vector, count):
    return jnp.pad(vector, (0, count - vector.shape[0]))


def on_device(
    tokens,
    segments,
    out_grad,
    attn_gain,
    w_query,
    w_key,
    w_value,
    query_gain,
    key_gain,
    w_out,
    mlp_gain,
    w_gate,
    w_up,
    w_down,
):
    n_seq = lax.axis_size("seq")
    n_fsdp = lax.axis_size("fsdp")
    me = lax.axis_index("seq")
    local, width = tokens.shape[1:]
    length = local * n_seq
    shard = attn_gain.shape[0]
    q_all, kv_all = w_query.shape[1], w_key.shape[1]
    q_own, kv_own = q_all // n_seq, kv_all // n_seq
    hidden_own = w_gate.shape[1]
    gain_own = query_gain.shape[0]

    mlp_pack = jnp.concatenate(
        [w_out.T, lanes(w_gate, PAD), lanes(w_up, PAD), lanes(w_down.T, PAD)], axis=1
    )
    mlp_full = lax.all_gather(mlp_pack, "fsdp", axis=0, tiled=True)
    own = lax.dynamic_slice_in_dim
    head_pack = jnp.concatenate(
        [
            own(w_query, me * q_own, q_own, 1),
            own(w_key, me * kv_own, kv_own, 1),
            own(w_value, me * kv_own, kv_own, 1),
            attn_gain[:, None],
            mlp_gain[:, None],
            rows(query_gain, shard)[:, None],
            rows(key_gain, shard)[:, None],
        ],
        axis=1,
    )
    qkv_own = q_own + 2 * kv_own
    head_pack = lanes(head_pack, 384)

    segs = gather_seq(segments).reshape(length)
    x = tokens[0]
    x_all = gather_seq(x).reshape(length, width)
    head_full = gather_fsdp(head_pack)
    g_all = gather_seq(out_grad[0]).reshape(length, width)

    w_own = head_full[:, :qkv_own]
    gains = head_full[:, qkv_own : qkv_own + 4].astype(F32)
    attn_g, mlp_g = gains[:, 0], gains[:, 1]
    query_g = gains[:, 2].reshape(n_fsdp, shard)[:, :gain_own].reshape(-1)
    key_g = gains[:, 3].reshape(n_fsdp, shard)[:, :gain_own].reshape(-1)

    index = jnp.arange(length, dtype=jnp.int32)
    first = jnp.sum((segs == 0).astype(jnp.int32))
    second_ = jnp.sum((segs == 1).astype(jnp.int32))
    earlier = jnp.where(segs >= 1, first, 0) + jnp.where(segs >= 2, second_, 0)
    position = (index - earlier).astype(F32)
    frequency = ROPE_BASE ** (-2.0 * jnp.arange(HEAD // 2, dtype=F32) / HEAD)
    angles = position[:, None] * frequency
    cosine, sine = jnp.cos(angles), jnp.sin(angles)
    allowed = (index[None, :] <= index[:, None]) & (segs[None, :] == segs[:, None])

    normed_all = rms_norm(x_all.astype(F32), attn_g).astype(BF16)
    raw = mm(normed_all, w_own)
    q_raw, k_raw = raw[:, :q_own], raw[:, q_own : q_own + kv_own]
    v = raw[:, q_own + kv_own :].astype(BF16)
    prep_pos = partial(prep, cosine=cosine, sine=sine)
    q_f, q_back = jax.vjp(prep_pos, q_raw, query_g)
    k_f, k_back = jax.vjp(prep_pos, k_raw, key_g)
    q, k = q_f.astype(BF16), k_f.astype(BF16)
    attended, lse = attend(q, k, v, allowed)

    att_all = gather_seq(attended).transpose(1, 0, 2).reshape(length, q_all)
    w_out_t = mlp_full[:, :q_all]
    gate_w = mlp_full[:, q_all : q_all + PAD]
    up_w = mlp_full[:, q_all + PAD : q_all + 2 * PAD]
    down_t = mlp_full[:, q_all + 2 * PAD :]
    middle = x_all.astype(F32) + mm_nt(att_all, w_out_t)
    second = rms_norm(middle, mlp_g).astype(BF16)
    middle_own = lax.dynamic_slice_in_dim(middle, me * local, local, 0)

    gate_pre = mm(second, gate_w)
    upward = mm(second, up_w)
    sig = jax.nn.sigmoid(gate_pre)
    hidden = (gate_pre * sig * upward).astype(BF16)
    grad_hidden = mm(g_all, down_t)
    grad_gate = (grad_hidden * upward * sig * (1.0 + gate_pre * (1.0 - sig))).astype(BF16)
    grad_up = (grad_hidden * gate_pre * sig).astype(BF16)
    second_part = (mm_nt(grad_gate, gate_w) + mm_nt(grad_up, up_w)).astype(BF16)
    grad_second = scatter_sum_seq(second_part.reshape(n_seq, local, width))
    out_part = mm_nt(hidden, down_t).astype(BF16)
    mlp_out = scatter_sum_seq(out_part.reshape(n_seq, local, width))
    layer_out = (middle_own + mlp_out).astype(BF16)

    mlp_grads = jnp.concatenate(
        [mm_tn(second, grad_gate), mm_tn(second, grad_up), mm_tn(g_all, hidden)], axis=1
    ).astype(BF16)
    mlp_owned = lax.psum_scatter(mlp_grads, "fsdp", scatter_dimension=0, tiled=True).astype(F32)
    proj = lax.all_gather(
        jnp.concatenate([w_query, w_key, w_value], axis=1), "fsdp", axis=0, tiled=True
    )

    _, mlp_back = jax.vjp(rms_norm, middle_own, mlp_g)
    grad_middle_norm, grad_mlp_g = mlp_back(grad_second)
    grad_middle = out_grad[0].astype(F32) + grad_middle_norm
    branch = grad_middle.astype(BF16)
    grad_att = mm(branch, w_out_t).astype(BF16)
    grad_att_h = lax.all_to_all(
        grad_att.reshape(local, n_seq, q_own), "seq", split_axis=1, concat_axis=0, tiled=True
    ).reshape(length, q_own)
    branch_all = gather_seq(branch).reshape(length, width)
    gq, gk, gv = attend_back(q, k, v, allowed, lse, grad_att_h)
    gq_raw, grad_query_g = q_back(gq.astype(F32))
    gk_raw, grad_key_g = k_back(gk.astype(F32))
    g_qkv = jnp.concatenate([gq_raw.astype(BF16), gk_raw.astype(BF16), gv], axis=1)

    tok_qkv = lax.all_to_all(
        g_qkv.reshape(n_seq, local, qkv_own), "seq", split_axis=0, concat_axis=0, tiled=True
    )
    cut = (q_own, q_own + kv_own)
    tok_g = jnp.concatenate(
        [
            tok_qkv[:, :, : cut[0]].transpose(1, 0, 2).reshape(local, q_all),
            tok_qkv[:, :, cut[0] : cut[1]].transpose(1, 0, 2).reshape(local, kv_all),
            tok_qkv[:, :, cut[1] :].transpose(1, 0, 2).reshape(local, kv_all),
        ],
        axis=1,
    )
    grad_normed = mm_nt(tok_g, proj)
    _, attn_back = jax.vjp(rms_norm, x.astype(F32), attn_g)
    grad_x_norm, grad_attn_g = attn_back(grad_normed)
    grad_tokens = grad_middle + grad_x_norm

    def spread(vector):
        grid = vector.reshape(n_fsdp, gain_own)
        return jnp.pad(grid, ((0, 0), (0, shard - gain_own))).reshape(-1)

    att_grads = jnp.concatenate(
        [
            mm_tn(normed_all, g_qkv),
            mm_tn(branch_all, attended),
            grad_attn_g[:, None],
            grad_mlp_g[:, None],
            spread(grad_query_g)[:, None],
            spread(grad_key_g)[:, None],
        ],
        axis=1,
    )
    att_grads = lanes(att_grads.astype(BF16), 640)
    got = lax.all_to_all(
        att_grads.reshape(n_fsdp, shard, 640), "fsdp", split_axis=0, concat_axis=0, tiled=True
    )
    att_owned = jnp.sum(got.astype(F32), axis=0).astype(BF16)
    att_seq = gather_seq(att_owned).astype(F32)

    def side(start, stop):
        return att_seq[:, :, start:stop].transpose(1, 0, 2).reshape(shard, -1)

    gain_at = qkv_own + q_own
    gain_sums = jnp.sum(att_seq[:, :, gain_at : gain_at + 4], axis=0)
    return (
        layer_out[None],
        grad_tokens[None],
        gain_sums[:, 0],
        side(0, cut[0]),
        side(cut[0], cut[1]),
        side(cut[1], qkv_own),
        gain_sums[:gain_own, 2],
        gain_sums[:gain_own, 3],
        side(qkv_own, gain_at).T,
        gain_sums[:, 1],
        mlp_owned[:, :hidden_own],
        mlp_owned[:, PAD : PAD + hidden_own],
        mlp_owned[:, 2 * PAD : 2 * PAD + hidden_own].T,
    )


def solution(mesh):
    in_specs = (
        P("fsdp", "seq", None),
        P("fsdp", "seq"),
        P("fsdp", "seq", None),
        P("fsdp"),
        P("fsdp", None),
        P("fsdp", None),
        P("fsdp", None),
        P("fsdp"),
        P("fsdp"),
        P(None, "fsdp"),
        P("fsdp"),
        P("fsdp", "seq"),
        P("fsdp", "seq"),
        P("seq", "fsdp"),
    )
    out_specs = (
        P("fsdp", "seq", None),
        P("fsdp", "seq", None),
        P("fsdp"),
        P("fsdp", None),
        P("fsdp", None),
        P("fsdp", None),
        P("fsdp"),
        P("fsdp"),
        P(None, "fsdp"),
        P("fsdp"),
        P("fsdp", "seq"),
        P("fsdp", "seq"),
        P("seq", "fsdp"),
    )
    return jax.shard_map(
        on_device, mesh=mesh, in_specs=in_specs, out_specs=out_specs, check_vma=False
    )
```

```python
import functools

import jax
import jax.numpy as jnp
from jax import lax
from jax.experimental import pallas as pl
from jax.experimental.pallas import tpu as pltpu
from jax.sharding import PartitionSpec as P

HEAD = 64
EPS = 1e-05
ROPE_BASE = 1000000.0
F32 = jnp.float32
BF16 = jnp.bfloat16
PAD = 896
HALVES = 2
VMEM = 56 * 2**20


def dot(a, b, ca, cb):
    return lax.dot_general(a, b, (((ca,), (cb,)), ((), ())), preferred_element_type=F32)


def shape(*dims, dtype=BF16):
    return jax.ShapeDtypeStruct(dims, dtype)


def cost(micros):
    return pl.CostEstimate(flops=int(micros * 1.15e9), bytes_accessed=2**10, transcendentals=0)


def angles_of(freq_ref, position):
    turn = freq_ref[...] * position
    return jnp.cos(turn), jnp.sin(turn)


def mask_of(rows, start, index, heads):
    row = lax.broadcasted_iota(jnp.int32, (rows, start.shape[1]), 0).astype(F32)
    allowed = (row >= start) & (row <= index)
    return jnp.concatenate([allowed] * heads, axis=1)


PIECES = (
    (0, 0, 0, 1),
    (0, 1, 0, 1),
    (-1, 0, 0, 1),
    (1, 0, 0, 1),
    (-1, 1, 0, 1),
    (1, 1, 0, 1),
    (2, 0, 0, 2),
    (2, 0, 1, 2),
    (2, 1, 0, 2),
    (2, 1, 1, 2),
)


STEPS = (0, -1, 1, 2)


def block_at(me_ref, dy, dx, n_seq):
    y, x = me_ref[0] // 2, me_ref[0] % 2
    return (y + dy + n_seq // 2) % (n_seq // 2) * 2 + (x + dx) % 2


def first_row(me_ref, piece, n_seq, rows):
    dy, dx, part, parts = piece
    block = block_at(me_ref, dy, dx, n_seq)
    return pl.multiple_of(block * rows + part * (rows // parts), rows // parts)


def owners(width, per):
    lane = lax.broadcasted_iota(jnp.int32, (HEAD, width), 1)
    row = lax.broadcasted_iota(jnp.int32, (HEAD, width), 0)
    shard = width * per // HEAD
    owner, place = lane // shard, lane % shard
    return jnp.where((place < per) & (owner * per + place == row), 1.0, 0.0).astype(BF16)


def forward_kernel(
    me_ref, *refs, pieces, heads, block, n_seq, per,
):
    x_refs, refs = refs[:pieces], refs[pieces:]
    w_ref, freq_ref = refs[:2]
    (
        x_ref, normed_ref, raw_ref, qt_ref, kt_ref, vt_ref, att_ref, parts_ref, lse_ref, pos_ref,
        rows_ref, gains_ref, k_rows, segs_ref,
    ) = refs[2:]
    local = x_refs[0].shape[0]
    width = w_ref.shape[0]
    at = (heads + 2) * HEAD
    slab = w_ref[:, at // 128 * 128 :]
    rows = slab.astype(F32).T
    at = at % 128
    rows_ref[...] = rows[at : at + 8]
    gain = rows[at : at + 1]
    gains_ref[...] = dot(owners(width, per), slab, 1, 0)
    qg, kg = gains_ref[:, at + 2 : at + 3], gains_ref[:, at + 3 : at + 4]
    length = n_seq * local
    q_own = heads * HEAD
    for piece, ref in zip(PIECES, x_refs):
        at = first_row(me_ref, piece, n_seq, local)
        here = pl.ds(at, ref.shape[0])
        x = ref[:, :width]
        x_ref[here, :] = x
        x = x.astype(F32)
        inverse = lax.rsqrt(jnp.mean(x * x, axis=1, keepdims=True) + EPS)
        normed_ref[here, :] = (x * inverse * gain).astype(BF16)
        if piece[2] == 0:
            segs_ref[0:1, pl.ds(pl.multiple_of(at, 128), local)] = ref[
                0:1, width : width + local
            ].astype(F32)
    segs = segs_ref[0:1, :]
    index = lax.broadcasted_iota(jnp.int32, (1, length), 1).astype(F32)
    first = jnp.sum(jnp.where(segs == 0.0, 1.0, 0.0), axis=1, keepdims=True)
    middle = jnp.sum(jnp.where(segs == 1.0, 1.0, 0.0), axis=1, keepdims=True)
    start = jnp.where(segs >= 1.0, first, 0.0) + jnp.where(segs >= 2.0, middle, 0.0)
    position = index - start
    pos_ref[0:1, :] = position
    cosine, sine = angles_of(freq_ref, position)
    raw = dot(normed_ref[...], w_ref[...], 1, 0).T
    raw_ref[...] = raw[: q_own + HEAD]
    for h in range(heads + 1):
        values = raw[h * HEAD : (h + 1) * HEAD]
        inverse = lax.rsqrt(jnp.mean(values * values, axis=0, keepdims=True) + EPS)
        values = values * inverse * (qg if h < heads else kg)
        a, b = values[: HEAD // 2], values[HEAD // 2 :]
        turned = jnp.concatenate([a * cosine - b * sine, b * cosine + a * sine], axis=0)
        if h < heads:
            qt_ref[h * HEAD : (h + 1) * HEAD, :] = turned.astype(BF16)
        else:
            kt_ref[...] = turned.astype(BF16)
            k_rows[...] = turned.T.astype(BF16)
    vt_ref[...] = raw[q_own + HEAD : q_own + 2 * HEAD].astype(BF16)
    part = local // HALVES
    for c in range(length // block):
        stop = (c + 1) * block
        lanes = slice(c * block, stop)
        q = jnp.concatenate(
            [qt_ref[h * HEAD : (h + 1) * HEAD, lanes] for h in range(heads)], axis=1
        )
        scores = dot(k_rows[:stop, :], q, 1, 0) * HEAD**-0.5
        allowed = mask_of(stop, start[:, lanes], index[:, lanes], heads)
        scores = jnp.where(allowed, scores, -1e30)
        peak = jnp.max(scores, axis=0, keepdims=True)
        exps = jnp.exp(scores - peak)
        total = jnp.sum(exps, axis=0, keepdims=True)
        probs = (exps * (1.0 / total)).astype(BF16)
        mixed = dot(vt_ref[:, :stop], probs, 1, 0).astype(BF16)
        lse = peak + jnp.log(total)
        for h in range(heads):
            own = mixed[:, h * block : (h + 1) * block]
            rows = slice(h * HEAD, (h + 1) * HEAD)
            att_ref[rows, lanes] = own
            lse_ref[h : h + 1, lanes] = lse[:, h * block : (h + 1) * block]
            for k in range(HALVES):
                cut = [
                    own[:, t * local + k * part : t * local + (k + 1) * part]
                    for t in range(block // local)
                ]
                at = c * (block // HALVES)
                parts_ref[k, rows, at : at + block // HALVES] = jnp.concatenate(cut, axis=1)


def smem():
    return pl.BlockSpec(memory_space=pltpu.SMEM)


def vmem(count):
    return [pl.BlockSpec(memory_space=pltpu.VMEM)] * count


def attend_forward(me, x_pieces, w_own, freq, heads, n_seq, per, block=256):
    local = x_pieces[0].shape[0]
    width = w_own.shape[0]
    length = n_seq * local
    q_own = heads * HEAD
    return pl.pallas_call(
        functools.partial(
            forward_kernel,
            pieces=len(x_pieces),
            heads=heads,
            block=block,
            n_seq=n_seq,
            per=per,
        ),
        in_specs=[smem()] + vmem(len(x_pieces) + 2),
        out_shape=(
            shape(length, width),
            shape(length, width),
            shape(q_own + HEAD, length, dtype=F32),
            shape(q_own, length),
            shape(HEAD, length),
            shape(HEAD, length),
            shape(q_own, length),
            shape(HALVES, q_own, length // HALVES),
            shape(8, length, dtype=F32),
            shape(8, length, dtype=F32),
            shape(8, width, dtype=F32),
            shape(HEAD, 128, dtype=F32),
        ),
        scratch_shapes=[pltpu.VMEM((length, HEAD), BF16), pltpu.VMEM((8, length), F32)],
        compiler_params=pltpu.CompilerParams(vmem_limit_bytes=VMEM),
        cost_estimate=cost(0.1),
        name="attend_forward",
    )(me, *x_pieces, w_own, freq)


def backward_kernel(
    me_ref, qt_ref, kt_ref, vt_ref, raw_ref, lse_ref, pos_ref, g_ref, gains_ref, freq_ref, w_ref,
    gt_ref, back0_ref, back1_ref, back2_ref, back3_ref, gain_ref,
    k_rows, v_rows, q_rows, g_rows, dk, dv, dq, *, heads, block,
):
    length = kt_ref.shape[1]
    blocks, _, local = g_ref.shape
    q_own = heads * HEAD
    at = (heads + 2) * HEAD % 128 + 2
    qg, kg = gains_ref[:, at : at + 1], gains_ref[:, at + 1 : at + 2]
    position = pos_ref[0:1, :]
    index = lax.broadcasted_iota(jnp.int32, (1, length), 1).astype(F32)
    start = index - position
    cosine, sine = angles_of(freq_ref, position)
    k_rows[...] = kt_ref[...].astype(F32).T.astype(BF16)
    v_rows[...] = vt_ref[...].astype(F32).T.astype(BF16)
    dk[...] = jnp.zeros_like(dk)
    dv[...] = jnp.zeros_like(dv)
    scale = HEAD**-0.5
    per = block // local
    for c in range(length // block):
        stop = (c + 1) * block
        lanes = slice(c * block, stop)
        q = jnp.concatenate(
            [qt_ref[h * HEAD : (h + 1) * HEAD, lanes] for h in range(heads)], axis=1
        )
        g = jnp.concatenate(
            [
                g_ref[c * per + t, h * HEAD : (h + 1) * HEAD, :]
                for h in range(heads)
                for t in range(per)
            ],
            axis=1,
        )
        lse = jnp.concatenate([lse_ref[h : h + 1, lanes] for h in range(heads)], axis=1)
        q_rows[...] = q.astype(F32).T.astype(BF16)
        g_rows[...] = g.astype(F32).T.astype(BF16)
        scores = dot(k_rows[:stop, :], q, 1, 0) * scale
        allowed = mask_of(stop, start[:, lanes], index[:, lanes], heads)
        probs = jnp.where(allowed, jnp.exp(scores - lse), 0.0)
        grad_probs = dot(v_rows[:stop, :], g, 1, 0)
        inner = jnp.sum(probs * grad_probs, axis=0, keepdims=True)
        grad_scores = (probs * (grad_probs - inner)).astype(BF16)
        dv[:stop, :] += dot(probs.astype(BF16), g_rows[...], 1, 0)
        dk[:stop, :] += dot(grad_scores, q_rows[...], 1, 0)
        part = dot(kt_ref[:, :stop], grad_scores, 1, 0) * scale
        for h in range(heads):
            dq[h * HEAD : (h + 1) * HEAD, lanes] = part[:, h * block : (h + 1) * block]

    def back(grad, raw, gain):
        grad = grad.astype(BF16).astype(F32)
        a, b = grad[: HEAD // 2], grad[HEAD // 2 :]
        grad = jnp.concatenate([a * cosine + b * sine, b * cosine - a * sine], axis=0)
        inverse = lax.rsqrt(jnp.mean(raw * raw, axis=0, keepdims=True) + EPS)
        u = grad * gain
        pull = jnp.mean(u * raw, axis=0, keepdims=True)
        out = inverse * u - raw * (inverse * inverse * inverse) * pull
        return out.astype(BF16), jnp.sum(grad * raw * inverse, axis=1, keepdims=True)

    gain_q = jnp.zeros((HEAD, 1), F32)
    for h in range(heads):
        rows = slice(h * HEAD, (h + 1) * HEAD)
        gt_ref[rows, :], more = back(dq[rows, :], raw_ref[rows, :], qg)
        gain_q += more
    k_at = slice(q_own, q_own + HEAD)
    gt_ref[k_at, :], gain_k = back((dk[...] * scale).T, raw_ref[k_at, :], kg)
    gt_ref[q_own + HEAD : q_own + 2 * HEAD, :] = dv[...].T.astype(BF16)
    w = w_ref[:, : q_own + 2 * HEAD]
    for dy, ref in zip(STEPS, (back0_ref, back1_ref, back2_ref, back3_ref)):
        for dx in range(2):
            at = pl.multiple_of(block_at(me_ref, dy, dx, blocks) * local, local)
            ref[dx] = dot(gt_ref[:, pl.ds(at, local)], w, 0, 1).astype(BF16)
    lane = lax.broadcasted_iota(jnp.int32, (HEAD, 128), 1)
    gain_ref[...] = jnp.where(lane == 0, gain_q, jnp.where(lane == 1, gain_k, 0.0))


def attend_backward(me, qt, kt, vt, raw, lse, pos, grads, gains, freq, w_own, block=256):
    blocks, q_own, local = grads.shape
    length = blocks * local
    heads = q_own // HEAD
    rows = q_own + 2 * HEAD
    return pl.pallas_call(
        functools.partial(backward_kernel, heads=heads, block=block),
        out_shape=(
            shape(rows, length),
            *[shape(2, local, w_own.shape[0])] * 4,
            shape(HEAD, 128, dtype=F32),
        ),
        in_specs=[smem()] + vmem(10),
        scratch_shapes=[
            pltpu.VMEM((length, HEAD), BF16),
            pltpu.VMEM((length, HEAD), BF16),
            pltpu.VMEM((heads * block, HEAD), BF16),
            pltpu.VMEM((heads * block, HEAD), BF16),
            pltpu.VMEM((length, HEAD), F32),
            pltpu.VMEM((length, HEAD), F32),
            pltpu.VMEM((q_own, length), F32),
        ],
        compiler_params=pltpu.CompilerParams(vmem_limit_bytes=VMEM),
        cost_estimate=cost(0.1),
        name="attend_backward",
    )(me, qt, kt, vt, raw, lse, pos, grads, gains, freq, w_own)


def mlp_kernel(me_ref, *refs, pieces, width, pad, n_seq):
    att_refs, refs = refs[:pieces], refs[pieces:]
    x_ref, g_ref, gain_ref, w_ref = refs[:4]
    (
        mid_ref, second_ref, hid_ref, gate_grad_ref, up_grad_ref, back_ref, out_ref,
        w_out, w_gate, w_up, w_down, sems, att_all,
    ) = refs[4:]
    places = (
        (0, width, w_out),
        (width, pad, w_gate),
        (width + pad, pad, w_up),
        (width + 2 * pad, pad, w_down),
    )
    copies = [
        pltpu.make_async_copy(w_ref.at[:, at : at + n], to, sems.at[i])
        for i, (at, n, to) in enumerate(places)
    ]
    first = pl.program_id(0) == 0

    @pl.when(first)
    def _():
        for copy in copies:
            copy.start()

    def ready(i):
        @pl.when(first)
        def _():
            copies[i].wait()

    n, rows, _ = g_ref.shape
    count = n * rows
    x = x_ref[...].reshape(count, width).astype(F32)
    if pieces == 1:
        att = att_refs[0][...].reshape(width, count)
    else:
        part = width // n_seq
        for dy, ref in zip(STEPS, att_refs):
            for dx in range(2):
                at = pl.multiple_of(block_at(me_ref, dy, dx, n_seq) * part, part)
                att_all[pl.ds(at, part), :] = ref[dx]
        att = att_all[...]
    ready(0)
    middle = x + dot(att, w_out[...], 0, 1)
    mid_ref[...] = middle.reshape(n, rows, width)
    inverse = lax.rsqrt(jnp.mean(middle * middle, axis=1, keepdims=True) + EPS)
    second = (middle * inverse * gain_ref[1:2, :]).astype(BF16)
    second_ref[...] = second
    ready(1)
    gate = dot(second, w_gate[...], 1, 0)
    ready(2)
    up = dot(second, w_up[...], 1, 0)
    sig = lax.logistic(gate)
    act = gate * sig
    hidden = (act * up).astype(BF16)
    hid_ref[...] = hidden
    ready(3)
    grad_hidden = dot(g_ref[...].reshape(count, width), w_down[...], 1, 0)
    gate_grad = (grad_hidden * up * sig * (1.0 + gate * (1.0 - sig))).astype(BF16)
    up_grad = (grad_hidden * act).astype(BF16)
    gate_grad_ref[...] = gate_grad
    up_grad_ref[...] = up_grad
    back = dot(gate_grad, w_gate[...], 1, 1) + dot(up_grad, w_up[...], 1, 1)
    back_ref[...] = back.astype(BF16).reshape(n, rows, width)
    out_ref[...] = dot(hidden, w_down[...], 1, 1).astype(BF16).reshape(n, rows, width)


def mlp(me, att, x_all, g_all, gain, weights, half, per=4):
    count = att[0].shape[-1]
    n_seq, local, width = x_all.shape
    rows = local // HALVES
    pad = (weights.shape[1] - width) // 3
    step = per * rows
    spec = pl.BlockSpec
    flat = spec((step, pad), lambda i: (i, 0))
    stack = spec((per, rows, width), lambda i: (i, 0, 0))
    return pl.pallas_call(
        functools.partial(mlp_kernel, pieces=len(att), width=width, pad=pad, n_seq=n_seq),
        grid=(n_seq // per,),
        in_specs=[smem()]
        + [
            spec(a.shape[:-1] + (step,), lambda i, lead=(0,) * (a.ndim - 1): lead + (i,))
            for a in att
        ]
        + [
            spec((per, rows, width), lambda i: (i, half, 0)),
            spec((per, rows, width), lambda i: (i, half, 0)),
            spec((8, width), lambda i: (0, 0)),
            spec(memory_space=pl.ANY),
        ],
        out_specs=[
            stack,
            spec((step, width), lambda i: (i, 0)),
            flat,
            flat,
            flat,
            stack,
            stack,
        ],
        out_shape=(
            shape(n_seq, rows, width, dtype=F32),
            shape(count, width),
            shape(count, pad),
            shape(count, pad),
            shape(count, pad),
            shape(n_seq, rows, width),
            shape(n_seq, rows, width),
        ),
        scratch_shapes=[
            pltpu.VMEM((width, width), BF16),
            pltpu.VMEM((width, pad), BF16),
            pltpu.VMEM((width, pad), BF16),
            pltpu.VMEM((width, pad), BF16),
            pltpu.SemaphoreType.DMA((4,)),
            pltpu.VMEM((width, step), BF16),
        ],
        compiler_params=pltpu.CompilerParams(vmem_limit_bytes=VMEM),
        cost_estimate=cost(1),
        name="mlp_part",
    )(me, *att, x_all, g_all, gain, weights)


def mlp_grads_kernel(core_ref, *refs, shard):
    seconds, cotangents = refs[:HALVES], refs[HALVES : 2 * HALVES]
    rest, own_ref, other_ref = refs[2 * HALVES : -2], refs[-2], refs[-1]
    pad = rest[0].shape[1]
    core = core_ref[0]
    for k in range(3):
        total = None
        for h in range(HALVES):
            left = (seconds if k < 2 else cotangents)[h][...]
            left = left.reshape(-1, left.shape[-1])
            term = dot(left, rest[k * HALVES + h][...], 0, 0)
            total = term if total is None else total + term
        total = total.astype(BF16)
        lanes = slice(k * pad, (k + 1) * pad)
        for i in range(total.shape[0] // shard):
            part = total[i * shard : (i + 1) * shard]

            @pl.when(core == i % 2)
            def _(part=part, i=i, lanes=lanes):
                own_ref[i // 2, :, lanes] = part

            @pl.when(core != i % 2)
            def _(part=part, i=i, lanes=lanes):
                other_ref[i // 2, :, lanes] = part


def mlp_grads(core, seconds, g_all, gates, ups, hiddens, shard, tile=384):
    count, width = seconds[0].shape
    pad = gates[0].shape[1]
    n_seq, local, _ = g_all.shape
    rows = local // HALVES
    spec = pl.BlockSpec
    return pl.pallas_call(
        functools.partial(mlp_grads_kernel, shard=shard),
        grid=(width // tile,),
        in_specs=[smem()]
        + [spec((count, tile), lambda r: (0, r))] * HALVES
        + [spec((n_seq, rows, tile), lambda r, h=h: (0, h, r)) for h in range(HALVES)]
        + [spec((count, pad), lambda r: (0, 0))] * (3 * HALVES),
        out_specs=[spec((tile // shard // 2, shard, 3 * pad), lambda r: (r, 0, 0))] * 2,
        out_shape=(shape(width // shard // 2, shard, 3 * pad),) * 2,
        compiler_params=pltpu.CompilerParams(vmem_limit_bytes=VMEM),
        cost_estimate=cost(0.1),
        name="mlp_grads",
    )(core, *seconds, *([g_all] * HALVES), *gates, *ups, *hiddens)


def middle_kernel(
    me_ref, back0_ref, back1_ref, mid0_ref, mid1_ref, g_ref, gain_ref, w_ref,
    branch_ref, grad_ref, att_ref, gain_grad_ref, mid_out_ref,
    mid, w, sems, *, width,
):
    half = back0_ref.shape[1]
    me = me_ref[0]
    copies = [
        pltpu.make_async_copy(mid0_ref.at[me], mid.at[pl.ds(0, half)], sems.at[0]),
        pltpu.make_async_copy(mid1_ref.at[me], mid.at[pl.ds(half, half)], sems.at[1]),
        pltpu.make_async_copy(w_ref.at[:, :width], w, sems.at[2]),
    ]
    for copy in copies:
        copy.start()
    grad = jnp.concatenate(
        [jnp.sum(ref[...].astype(F32), axis=0) for ref in (back0_ref, back1_ref)], axis=0
    )
    copies[0].wait()
    copies[1].wait()
    middle = mid[...]
    mid_out_ref[...] = middle
    inverse = lax.rsqrt(jnp.mean(middle * middle, axis=1, keepdims=True) + EPS)
    u = grad * gain_ref[1:2, :]
    pull = jnp.mean(u * middle, axis=1, keepdims=True)
    grad_middle = (
        g_ref[...].astype(F32) + inverse * u - middle * (inverse * inverse * inverse) * pull
    )
    gain_grad_ref[...] = jnp.sum(grad * middle * inverse, axis=0, keepdims=True)
    grad_ref[...] = grad_middle
    branch = grad_middle.astype(BF16)
    branch_ref[...] = branch
    copies[2].wait()
    att_ref[...] = dot(branch, w[...], 1, 0).T.astype(BF16)


def middle_back(me, backs, mids, g_own, gain, weights):
    local, width = g_own.shape
    anywhere = pl.BlockSpec(memory_space=pl.ANY)
    return pl.pallas_call(
        functools.partial(middle_kernel, width=width),
        in_specs=[smem()] + vmem(2) + [anywhere] * 2 + vmem(2) + [anywhere],
        out_shape=(
            shape(local, width),
            shape(local, width, dtype=F32),
            shape(width, local),
            shape(1, width, dtype=F32),
            shape(local, width, dtype=F32),
        ),
        scratch_shapes=[
            pltpu.VMEM((local, width), F32),
            pltpu.VMEM((width, width), BF16),
            pltpu.SemaphoreType.DMA((3,)),
        ],
        compiler_params=pltpu.CompilerParams(vmem_limit_bytes=VMEM),
        cost_estimate=cost(0.1),
        name="middle_back",
    )(me, *backs, *mids, g_own, gain, weights)


def qkv_grads_kernel(gt_ref, normed_ref, gains_ref, mlp_gain_ref, out_ref, *, per):
    qkv = dot(gt_ref[...], normed_ref[...], 1, 0)
    width = normed_ref.shape[1]
    gains = dot(gains_ref[:, :HEAD].astype(BF16), owners(width, per), 0, 0)
    row = lax.broadcasted_iota(jnp.int32, gains.shape, 0)
    gains = jnp.where(row == 2, mlp_gain_ref[...], gains)
    out_ref[...] = jnp.concatenate([qkv, gains], axis=0).T.astype(BF16)


def qkv_grads(gt, normed, gains, mlp_gain, per):
    count, width = normed.shape
    return pl.pallas_call(
        functools.partial(qkv_grads_kernel, per=per),
        out_shape=shape(width, gt.shape[0] + HEAD),
        compiler_params=pltpu.CompilerParams(vmem_limit_bytes=VMEM),
        cost_estimate=cost(0.1),
        name="qkv_grads",
    )(gt, normed, gains, mlp_gain)


def out_grads_kernel(me_ref, att_ref, *refs, n_seq):
    branch_refs, out_ref, whole = refs[:-2], refs[-2], refs[-1]
    local = branch_refs[0].shape[1]
    for dy, ref in zip(STEPS, branch_refs):
        for dx in range(2):
            at = pl.multiple_of(block_at(me_ref, dy, dx, n_seq) * local, local)
            whole[pl.ds(at, local), :] = ref[dx]
    out_ref[...] = dot(att_ref[...], whole[...], 1, 0).T.astype(BF16)


def out_grads(me, att, branch, n_seq):
    q_own, length = att.shape
    width = branch[0].shape[2]
    return pl.pallas_call(
        functools.partial(out_grads_kernel, n_seq=n_seq),
        in_specs=[smem()] + vmem(1 + len(branch)),
        out_shape=shape(width, q_own),
        scratch_shapes=[pltpu.VMEM((length, width), BF16)],
        compiler_params=pltpu.CompilerParams(vmem_limit_bytes=VMEM),
        cost_estimate=cost(1),
        name="out_grads",
    )(me, att, *branch)


def shards_kernel(
    in_ref, wq_ref, wk_ref, wv_ref, gain_ref,
    gq_ref, gk_ref, gv_ref, go_ref, gains_ref, *, q_own, kv_own,
):
    n = in_ref.shape[0]

    def side(start, stop):
        return jnp.concatenate([in_ref[j][:, start:stop] for j in range(n)], axis=1).astype(F32)

    k_at, v_at, end = q_own, q_own + kv_own, q_own + 2 * kv_own
    gq, gk, gv = side(0, k_at), side(k_at, v_at), side(v_at, end)
    gq_ref[...], gk_ref[...], gv_ref[...] = gq, gk, gv
    go_ref[...] = side(end + HEAD, end + HEAD + q_own)
    attn = sum(
        jnp.sum(w[...].astype(F32) * g, axis=1, keepdims=True)
        for w, g in ((wq_ref, gq), (wk_ref, gk), (wv_ref, gv))
    ) / gain_ref[...].astype(F32)
    sums = jnp.sum(in_ref[:, :, 256:384].astype(F32), axis=0)
    lane = lax.broadcasted_iota(jnp.int32, sums.shape, 1)
    gains_ref[...] = jnp.where(lane == 0, attn, sums)


def own_shards(parts, w_query, w_key, w_value, attn_gain, q_own, kv_own):
    shard, q_all = w_query.shape
    return pl.pallas_call(
        functools.partial(shards_kernel, q_own=q_own, kv_own=kv_own),
        out_shape=(
            shape(shard, q_all, dtype=F32),
            shape(shard, w_key.shape[1], dtype=F32),
            shape(shard, w_value.shape[1], dtype=F32),
            shape(shard, q_all, dtype=F32),
            shape(shard, 128, dtype=F32),
        ),
        compiler_params=pltpu.CompilerParams(vmem_limit_bytes=VMEM),
        cost_estimate=cost(200),
        name="own_shards",
    )(parts, w_query, w_key, w_value, attn_gain)


def mlp_shards_kernel(x_ref, grads_ref, got_ref, gate_ref, up_ref, down_ref):
    width = gate_ref.shape[1]
    total = grads_ref[x_ref[0]].astype(F32) + got_ref[...].astype(F32)
    for k, ref in enumerate((gate_ref, up_ref, down_ref)):
        ref[...] = total[:, k * PAD : k * PAD + width]


def mlp_shards(x_hi, grads, got, width):
    return pl.pallas_call(
        mlp_shards_kernel,
        in_specs=[smem()] + vmem(2),
        out_shape=(shape(got.shape[0], width, dtype=F32),) * 3,
        compiler_params=pltpu.CompilerParams(vmem_limit_bytes=VMEM),
        cost_estimate=cost(1),
        name="mlp_shards",
    )(x_hi, grads, got)


def shift(size, by):
    return [(i, (i + by) % size) for i in range(size)]


def to_all(block):
    n = lax.axis_size("seq")
    return lax.all_to_all(jnp.broadcast_to(block[None], (n,) + block.shape), "seq", 0, 0, tiled=True)


def exchange(blocks):
    return lax.all_to_all(blocks, "seq", 0, 0, tiled=True)


def total_of(blocks):
    return jnp.sum(blocks.astype(F32), axis=0)


def step_seq(block, dy, dx=0):
    n = lax.axis_size("seq")
    to = [(i, (i + 2 * dy) % n ^ dx) for i in range(n)]
    return lax.ppermute(block, "seq", to)


def gather_pieces(block):
    half = block.shape[0] // 2
    up, down = step_seq(block, 1), step_seq(block, -1)
    beside = step_seq(block, 0, 1)
    beside_up, beside_down = step_seq(beside, 1), step_seq(beside, -1)
    return (
        block,
        beside,
        up,
        down,
        beside_up,
        beside_down,
        step_seq(up[:half], 1),
        step_seq(down[half:], -1),
        step_seq(beside_up[:half], 1),
        step_seq(beside_down[half:], -1),
    )


def along_y(pair):
    return (pair,) + tuple(step_seq(pair, -dy) for dy in STEPS[1:])


def send_along(parts):
    return (parts[0],) + tuple(step_seq(part, dy) for dy, part in zip(STEPS[1:], parts[1:]))


def sum_pairs(pairs):
    total = sum(pair.astype(F32) for pair in pairs)
    return total[0] + step_seq(total[1].astype(pairs[0].dtype), 0, 1).astype(F32)


def pairs_for(blocks):
    n = lax.axis_size("seq")
    me = lax.axis_index("seq")
    y, x = me // 2, me % 2
    grid = blocks.reshape((n // 2, 2) + blocks.shape[1:])
    grid = jnp.where(x == 0, grid, grid[:, ::-1])
    pick = functools.partial(lax.dynamic_index_in_dim, grid, axis=0, keepdims=False)
    return [pick((y + dy) % (n // 2)) for dy in STEPS]


def in_order_kernel(me_ref, *refs, n_seq):
    out_ref = refs[-1]
    for dy, ref in zip(STEPS, refs[:-1]):
        for dx in range(2):
            out_ref[block_at(me_ref, dy, dx, n_seq)] = ref[dx]


def in_order(me, pairs, n_seq):
    return pl.pallas_call(
        functools.partial(in_order_kernel, n_seq=n_seq),
        in_specs=[smem()] + vmem(len(pairs)),
        out_shape=shape(n_seq, *pairs[0].shape[1:]),
        compiler_params=pltpu.CompilerParams(vmem_limit_bytes=VMEM),
        cost_estimate=cost(0.1),
        name="in_order",
    )(me, *pairs)


def swap(held, bit):
    n = lax.axis_size("fsdp")
    return lax.ppermute(held, "fsdp", [(i, i ^ bit) for i in range(n)])


def scatter_sum_fsdp(blocks):
    n = lax.axis_size("fsdp")
    me = lax.axis_index("fsdp")
    core, x_hi, z = me % 2, me // 2 % 2, me // 4
    rest = blocks.shape[1:]
    grid = blocks.reshape((n // 2, 2) + rest)
    pick = lax.dynamic_index_in_dim
    got = swap(pick(grid, 1 - core, 1, keepdims=False), 1)
    held = (pick(grid, core, 1, keepdims=False).astype(F32) + got.astype(F32)).astype(blocks.dtype)
    grid = held.reshape((n // 4, 2) + rest)
    got = [
        lax.ppermute(pick(grid, (z + by) % (n // 4), 0, keepdims=False), "fsdp", shift(n, 4 * by))
        for by in range(1, n // 4)
    ]
    held = pick(grid, z, 0, keepdims=False).astype(F32)
    for block in got:
        held = held + block.astype(F32)
    held = held.astype(blocks.dtype)
    got = swap(pick(held, 1 - x_hi, 0, keepdims=False), 2)
    return pick(held, x_hi, 0, keepdims=False).astype(F32) + got.astype(F32)


def pair(mine, other, low):
    return jnp.concatenate([jnp.where(low, mine, other), jnp.where(low, other, mine)], axis=0)


def gather_fsdp(block, first, second):
    n = lax.axis_size("fsdp")
    me = lax.axis_index("fsdp")
    held = block[None]
    held = pair(held, swap(held, 2), me // 2 % 2 == 0)
    held, _ = lax.optimization_barrier((held, first))
    other = swap(held, 1)
    low = me % 2 == 0
    held = jnp.stack([jnp.where(low, held, other), jnp.where(low, other, held)], axis=1)
    held = held.reshape((1, 4) + block.shape)
    held, _ = lax.optimization_barrier((held, second))
    whole = jnp.zeros((n // 4,) + held.shape[1:], block.dtype)
    z = me // 4
    whole = lax.dynamic_update_slice_in_dim(whole, held, z, 0)
    for by in range(1, n // 4):
        got = lax.ppermute(held, "fsdp", shift(n, 4 * by))
        whole = lax.dynamic_update_slice_in_dim(whole, got, (z - by) % (n // 4), 0)
    return whole.reshape((n * block.shape[0],) + block.shape[1:])


def lanes(array, width):
    return jnp.pad(array, ((0, 0), (0, width - array.shape[1])))


def rows(vector, count):
    return jnp.pad(vector, (0, count - vector.shape[0]))


def on_device(
    tokens,
    segments,
    out_grad,
    attn_gain,
    w_query,
    w_key,
    w_value,
    query_gain,
    key_gain,
    w_out,
    mlp_gain,
    w_gate,
    w_up,
    w_down,
):
    n_seq = lax.axis_size("seq")
    n_fsdp = lax.axis_size("fsdp")
    me = lax.axis_index("seq")
    here = me.astype(jnp.int32).reshape(1)
    core = (lax.axis_index("fsdp") % 2).astype(jnp.int32).reshape(1)
    x_hi = (lax.axis_index("fsdp") // 2 % 2).astype(jnp.int32).reshape(1)
    local, width = tokens.shape[1:]
    shard = attn_gain.shape[0]
    q_all, kv_all = w_query.shape[1], w_key.shape[1]
    q_own, kv_own = q_all // n_seq, kv_all // n_seq
    heads = q_own // HEAD
    qkv_own = q_own + 2 * kv_own
    hidden_own = w_gate.shape[1]
    gain_own = query_gain.shape[0]

    x = tokens[0]
    numbers = lax.pad(
        segments.astype(BF16), jnp.zeros((), BF16), ((0, local - 1, 0), (0, 128 - local, 0))
    )
    x_pieces = gather_pieces(jnp.concatenate([x, numbers], axis=1))

    mlp_pack = jnp.concatenate(
        [w_out.T, lanes(w_gate, PAD), lanes(w_up, PAD), lanes(w_down.T, PAD)], axis=1
    )
    mlp_full = lax.all_gather(mlp_pack, "fsdp", axis=0, tiled=True)

    mlp_pack = jnp.concatenate(
        [w_out.T, lanes(w_gate, PAD), lanes(w_up, PAD), lanes(w_down.T, PAD)], axis=1
    )
    mlp_full = lax.all_gather(mlp_pack, "fsdp", axis=0, tiled=True)

    own = lax.dynamic_slice_in_dim
    head_pack = jnp.concatenate(
        [
            own(w_query, me * q_own, q_own, 1),
            own(w_key, me * kv_own, kv_own, 1),
            own(w_value, me * kv_own, kv_own, 1),
            attn_gain[:, None],
            mlp_gain[:, None],
            rows(query_gain, shard)[:, None],
            rows(key_gain, shard)[:, None],
        ],
        axis=1,
    )
    head_full = gather_fsdp(lanes(head_pack, 384), x_pieces[1], x_pieces[2:4])

    freq = (ROPE_BASE ** (-2.0 * jnp.arange(HEAD // 2, dtype=F32) / HEAD)).reshape(-1, 1)

    after = lax.optimization_barrier
    g_pair = jnp.stack([out_grad[0], step_seq(out_grad[0], 0, 1)])
    g_pair, x_pieces = after((g_pair, x_pieces))
    g_pairs = along_y(g_pair)

    x_all, normed, raw, qt, kt, vt, att, att_parts, lse, pos, gain_rows, gains = attend_forward(
        here, x_pieces, head_full, freq, heads, n_seq, gain_own
    )
    x_all = x_all.reshape(n_seq, local, width)
    att_beside = step_seq(att_parts, 0, 1)
    att_pair, g_pairs = after((jnp.stack([att_parts[0], att_beside[0]]), g_pairs))
    att_first = along_y(att_pair)
    att_sent, att_first = after((att_parts[1], att_first))
    att_second = (to_all(att_sent),)
    g_all = in_order(here, g_pairs, n_seq)
    done = [mlp(here, att_first, x_all, g_all, gain_rows, mlp_full, 0)]
    back_first = exchange(done[0][5])
    att_second, done[0] = after((att_second, done[0]))
    done.append(mlp(here, att_second, x_all, g_all, gain_rows, mlp_full, 1))
    middle_parts, seconds, hiddens, gate_grads, up_grads, back_parts, out_parts = zip(*done)
    back_sent, back_first = after((back_parts[1], back_first))
    backs = (back_first, exchange(back_sent))
    mine, other = mlp_grads(core, seconds, g_all, gate_grads, up_grads, hiddens, shard)
    mine, other, backs = after((mine, other, backs))
    got = swap(other, 1)
    out_sent = pairs_for(jnp.concatenate(out_parts, axis=1))
    out_near = [step_seq(pair, dy) for pair, dy in zip(out_sent[1:3], STEPS[1:3])]
    backs, out_near = after((backs, out_near))

    branch, grad_middle, grad_att, grad_mlp_g, middle = middle_back(
        here, backs, middle_parts, out_grad[0], gain_rows, mlp_full
    )
    mine, got, branch = after((mine, got, branch))
    chip_sums = (mine.astype(F32) + got.astype(F32)).astype(BF16)
    mlp_sums = lax.psum_scatter(
        chip_sums.reshape(n_fsdp // 4, 2, shard, -1),
        "fsdp",
        scatter_dimension=0,
        tiled=True,
        axis_index_groups=[list(range(i, n_fsdp, 4)) for i in range(4)],
    ).reshape(2, shard, -1)
    grad_heads = exchange(grad_att.reshape(n_seq, q_own, local))
    branch_pair = jnp.stack([branch, step_seq(branch, 0, 1)])
    branch_pair, grad_heads, _ = after((branch_pair, grad_heads, chip_sums))
    branch_pairs = along_y(branch_pair)

    gt, *back, gain_grads = attend_backward(
        here, qt, kt, vt, raw, lse, pos, grad_heads, gains, freq, head_full
    )
    back, branch_pairs = after((back, branch_pairs))
    back_pairs = send_along(back)
    grad_normed = sum_pairs(back_pairs)
    out_far, back_pairs = after((out_sent[3], back_pairs))
    out_pairs = [out_sent[0], *out_near, step_seq(out_far, STEPS[3])]
    layer_out = (middle + sum_pairs(out_pairs)).astype(BF16)
    xf = x.astype(F32)
    inverse_x = lax.rsqrt(jnp.mean(xf * xf, axis=-1, keepdims=True) + EPS)
    ux = grad_normed * gain_rows[:1]
    grad_tokens = (
        grad_middle
        + inverse_x * ux
        - xf * inverse_x**3 * jnp.mean(ux * xf, axis=-1, keepdims=True)
    )

    own_grads = jnp.concatenate(
        [
            qkv_grads(gt, normed, gain_grads, grad_mlp_g, gain_own),
            out_grads(here, att, branch_pairs, n_seq),
        ],
        axis=1,
    )
    att_owned = scatter_sum_fsdp(own_grads.reshape(n_fsdp, shard, -1)).astype(BF16)
    att_owned, grad_normed = after((att_owned, grad_normed))
    gw_query, gw_key, gw_value, gw_out, gain_sums = own_shards(
        to_all(att_owned), w_query, w_key, w_value, attn_gain[:, None], q_own, kv_own
    )
    far = lax.dynamic_index_in_dim(mlp_sums, 1 - x_hi[0], 0, keepdims=False)
    gw_gate, gw_up, gw_down = mlp_shards(x_hi, mlp_sums, swap(far, 2), hidden_own)
    at = qkv_own - 256
    return (
        layer_out[None],
        grad_tokens[None],
        gain_sums[:, 0],
        gw_query,
        gw_key,
        gw_value,
        gain_sums[:gain_own, at],
        gain_sums[:gain_own, at + 1],
        gw_out.T,
        gain_sums[:, at + 2],
        gw_gate,
        gw_up,
        gw_down.T,
    )


def solution(mesh):
    in_specs = (
        P("fsdp", "seq", None),
        P("fsdp", "seq"),
        P("fsdp", "seq", None),
        P("fsdp"),
        P("fsdp", None),
        P("fsdp", None),
        P("fsdp", None),
        P("fsdp"),
        P("fsdp"),
        P(None, "fsdp"),
        P("fsdp"),
        P("fsdp", "seq"),
        P("fsdp", "seq"),
        P("seq", "fsdp"),
    )
    out_specs = (
        P("fsdp", "seq", None),
        P("fsdp", "seq", None),
        P("fsdp"),
        P("fsdp", None),
        P("fsdp", None),
        P("fsdp", None),
        P("fsdp"),
        P("fsdp"),
        P(None, "fsdp"),
        P("fsdp"),
        P("fsdp", "seq"),
        P("fsdp", "seq"),
        P("seq", "fsdp"),
    )
    return jax.shard_map(
        on_device, mesh=mesh, in_specs=in_specs, out_specs=out_specs, check_vma=False
    )
```

```python
import functools

import jax
import jax.numpy as jnp
from jax import lax
from jax.experimental import pallas as pl
from jax.experimental.pallas import tpu as pltpu
from jax.sharding import PartitionSpec as P

HEAD = 64
EPS = 1e-05
ROPE_BASE = 1000000.0
F32 = jnp.float32
BF16 = jnp.bfloat16
PAD = 896
HALVES = 2
VMEM = 56 * 2**20


def dot(a, b, ca, cb):
    return lax.dot_general(a, b, (((ca,), (cb,)), ((), ())), preferred_element_type=F32)


def shape(*dims, dtype=BF16):
    return jax.ShapeDtypeStruct(dims, dtype)


def cost(micros):
    return pl.CostEstimate(flops=int(micros * 1.15e9), bytes_accessed=2**10, transcendentals=0)


def angles_of(freq_ref, position):
    turn = freq_ref[...] * position
    return jnp.cos(turn), jnp.sin(turn)


def mask_of(rows, start, index, heads):
    row = lax.broadcasted_iota(jnp.int32, (rows, start.shape[1]), 0).astype(F32)
    allowed = (row >= start) & (row <= index)
    return jnp.concatenate([allowed] * heads, axis=1)


PIECES = (
    (0, 0, 0, 1),
    (0, 1, 0, 1),
    (-1, 0, 0, 1),
    (1, 0, 0, 1),
    (-1, 1, 0, 1),
    (1, 1, 0, 1),
    (2, 0, 0, 2),
    (2, 0, 1, 2),
    (2, 1, 0, 2),
    (2, 1, 1, 2),
)


STEPS = (0, -1, 1, 2)


def block_at(me_ref, dy, dx, n_seq):
    y, x = me_ref[0] // 2, me_ref[0] % 2
    return (y + dy + n_seq // 2) % (n_seq // 2) * 2 + (x + dx) % 2


def first_row(me_ref, piece, n_seq, rows):
    dy, dx, part, parts = piece
    block = block_at(me_ref, dy, dx, n_seq)
    return pl.multiple_of(block * rows + part * (rows // parts), rows // parts)


def owners(width, per):
    lane = lax.broadcasted_iota(jnp.int32, (HEAD, width), 1)
    row = lax.broadcasted_iota(jnp.int32, (HEAD, width), 0)
    shard = width * per // HEAD
    owner, place = lane // shard, lane % shard
    return jnp.where((place < per) & (owner * per + place == row), 1.0, 0.0).astype(BF16)


def forward_kernel(
    me_ref, *refs, pieces, heads, block, n_seq, per,
):
    x_refs, refs = refs[:pieces], refs[pieces:]
    w_ref, freq_ref = refs[:2]
    (
        x_ref, normed_ref, raw_ref, qt_ref, kt_ref, vt_ref, att_ref, parts_ref, lse_ref, pos_ref,
        rows_ref, gains_ref, k_rows, segs_ref,
    ) = refs[2:]
    local = x_refs[0].shape[0]
    width = w_ref.shape[0]
    at = (heads + 2) * HEAD
    slab = w_ref[:, at // 128 * 128 :]
    rows = slab.astype(F32).T
    at = at % 128
    rows_ref[...] = rows[at : at + 8]
    gain = rows[at : at + 1]
    gains_ref[...] = dot(owners(width, per), slab, 1, 0)
    qg, kg = gains_ref[:, at + 2 : at + 3], gains_ref[:, at + 3 : at + 4]
    length = n_seq * local
    q_own = heads * HEAD
    for piece, ref in zip(PIECES, x_refs):
        at = first_row(me_ref, piece, n_seq, local)
        here = pl.ds(at, ref.shape[0])
        x = ref[:, :width]
        x_ref[here, :] = x
        x = x.astype(F32)
        inverse = lax.rsqrt(jnp.mean(x * x, axis=1, keepdims=True) + EPS)
        normed_ref[here, :] = (x * inverse * gain).astype(BF16)
        if piece[2] == 0:
            segs_ref[0:1, pl.ds(pl.multiple_of(at, 128), local)] = ref[
                0:1, width : width + local
            ].astype(F32)
    segs = segs_ref[0:1, :]
    index = lax.broadcasted_iota(jnp.int32, (1, length), 1).astype(F32)
    first = jnp.sum(jnp.where(segs == 0.0, 1.0, 0.0), axis=1, keepdims=True)
    middle = jnp.sum(jnp.where(segs == 1.0, 1.0, 0.0), axis=1, keepdims=True)
    start = jnp.where(segs >= 1.0, first, 0.0) + jnp.where(segs >= 2.0, middle, 0.0)
    position = index - start
    pos_ref[0:1, :] = position
    cosine, sine = angles_of(freq_ref, position)
    raw = dot(normed_ref[...], w_ref[...], 1, 0).T
    raw_ref[...] = raw[: q_own + HEAD]
    for h in range(heads + 1):
        values = raw[h * HEAD : (h + 1) * HEAD]
        inverse = lax.rsqrt(jnp.mean(values * values, axis=0, keepdims=True) + EPS)
        values = values * inverse * (qg if h < heads else kg)
        a, b = values[: HEAD // 2], values[HEAD // 2 :]
        turned = jnp.concatenate([a * cosine - b * sine, b * cosine + a * sine], axis=0)
        if h < heads:
            qt_ref[h * HEAD : (h + 1) * HEAD, :] = turned.astype(BF16)
        else:
            kt_ref[...] = turned.astype(BF16)
            k_rows[...] = turned.T.astype(BF16)
    vt_ref[...] = raw[q_own + HEAD : q_own + 2 * HEAD].astype(BF16)
    part = local // HALVES
    for c in range(length // block):
        stop = (c + 1) * block
        lanes = slice(c * block, stop)
        q = jnp.concatenate(
            [qt_ref[h * HEAD : (h + 1) * HEAD, lanes] for h in range(heads)], axis=1
        )
        scores = dot(k_rows[:stop, :], q, 1, 0) * HEAD**-0.5
        allowed = mask_of(stop, start[:, lanes], index[:, lanes], heads)
        scores = jnp.where(allowed, scores, -1e30)
        peak = jnp.max(scores, axis=0, keepdims=True)
        exps = jnp.exp(scores - peak)
        total = jnp.sum(exps, axis=0, keepdims=True)
        probs = (exps * (1.0 / total)).astype(BF16)
        mixed = dot(vt_ref[:, :stop], probs, 1, 0).astype(BF16)
        lse = peak + jnp.log(total)
        for h in range(heads):
            own = mixed[:, h * block : (h + 1) * block]
            rows = slice(h * HEAD, (h + 1) * HEAD)
            att_ref[rows, lanes] = own
            lse_ref[h : h + 1, lanes] = lse[:, h * block : (h + 1) * block]
            for k in range(HALVES):
                cut = [
                    own[:, t * local + k * part : t * local + (k + 1) * part]
                    for t in range(block // local)
                ]
                at = c * (block // HALVES)
                parts_ref[k, rows, at : at + block // HALVES] = jnp.concatenate(cut, axis=1)


def smem():
    return pl.BlockSpec(memory_space=pltpu.SMEM)


def vmem(count):
    return [pl.BlockSpec(memory_space=pltpu.VMEM)] * count


def attend_forward(me, x_pieces, w_own, freq, heads, n_seq, per, block=256):
    local = x_pieces[0].shape[0]
    width = w_own.shape[0]
    length = n_seq * local
    q_own = heads * HEAD
    return pl.pallas_call(
        functools.partial(
            forward_kernel,
            pieces=len(x_pieces),
            heads=heads,
            block=block,
            n_seq=n_seq,
            per=per,
        ),
        in_specs=[smem()] + vmem(len(x_pieces) + 2),
        out_shape=(
            shape(length, width),
            shape(length, width),
            shape(q_own + HEAD, length, dtype=F32),
            shape(q_own, length),
            shape(HEAD, length),
            shape(HEAD, length),
            shape(q_own, length),
            shape(HALVES, q_own, length // HALVES),
            shape(8, length, dtype=F32),
            shape(8, length, dtype=F32),
            shape(8, width, dtype=F32),
            shape(HEAD, 128, dtype=F32),
        ),
        scratch_shapes=[pltpu.VMEM((length, HEAD), BF16), pltpu.VMEM((8, length), F32)],
        compiler_params=pltpu.CompilerParams(vmem_limit_bytes=VMEM),
        cost_estimate=cost(0.1),
        name="attend_forward",
    )(me, *x_pieces, w_own, freq)


def backward_kernel(
    me_ref, qt_ref, kt_ref, vt_ref, raw_ref, lse_ref, pos_ref, g_ref, gains_ref, freq_ref, w_ref,
    gt_ref, back0_ref, back1_ref, back2_ref, back3_ref, gain_ref,
    k_rows, v_rows, q_rows, g_rows, dk, dv, dq, *, heads, block,
):
    length = kt_ref.shape[1]
    blocks, _, local = g_ref.shape
    q_own = heads * HEAD
    at = (heads + 2) * HEAD % 128 + 2
    qg, kg = gains_ref[:, at : at + 1], gains_ref[:, at + 1 : at + 2]
    position = pos_ref[0:1, :]
    index = lax.broadcasted_iota(jnp.int32, (1, length), 1).astype(F32)
    start = index - position
    cosine, sine = angles_of(freq_ref, position)
    k_rows[...] = kt_ref[...].astype(F32).T.astype(BF16)
    v_rows[...] = vt_ref[...].astype(F32).T.astype(BF16)
    dk[...] = jnp.zeros_like(dk)
    dv[...] = jnp.zeros_like(dv)
    scale = HEAD**-0.5
    per = block // local
    for c in range(length // block):
        stop = (c + 1) * block
        lanes = slice(c * block, stop)
        q = jnp.concatenate(
            [qt_ref[h * HEAD : (h + 1) * HEAD, lanes] for h in range(heads)], axis=1
        )
        g = jnp.concatenate(
            [
                g_ref[c * per + t, h * HEAD : (h + 1) * HEAD, :]
                for h in range(heads)
                for t in range(per)
            ],
            axis=1,
        )
        lse = jnp.concatenate([lse_ref[h : h + 1, lanes] for h in range(heads)], axis=1)
        q_rows[...] = q.astype(F32).T.astype(BF16)
        g_rows[...] = g.astype(F32).T.astype(BF16)
        scores = dot(k_rows[:stop, :], q, 1, 0) * scale
        allowed = mask_of(stop, start[:, lanes], index[:, lanes], heads)
        probs = jnp.where(allowed, jnp.exp(scores - lse), 0.0)
        grad_probs = dot(v_rows[:stop, :], g, 1, 0)
        inner = jnp.sum(probs * grad_probs, axis=0, keepdims=True)
        grad_scores = (probs * (grad_probs - inner)).astype(BF16)
        dv[:stop, :] += dot(probs.astype(BF16), g_rows[...], 1, 0)
        dk[:stop, :] += dot(grad_scores, q_rows[...], 1, 0)
        part = dot(kt_ref[:, :stop], grad_scores, 1, 0) * scale
        for h in range(heads):
            dq[h * HEAD : (h + 1) * HEAD, lanes] = part[:, h * block : (h + 1) * block]

    def back(grad, raw, gain):
        grad = grad.astype(BF16).astype(F32)
        a, b = grad[: HEAD // 2], grad[HEAD // 2 :]
        grad = jnp.concatenate([a * cosine + b * sine, b * cosine - a * sine], axis=0)
        inverse = lax.rsqrt(jnp.mean(raw * raw, axis=0, keepdims=True) + EPS)
        u = grad * gain
        pull = jnp.mean(u * raw, axis=0, keepdims=True)
        out = inverse * u - raw * (inverse * inverse * inverse) * pull
        return out.astype(BF16), jnp.sum(grad * raw * inverse, axis=1, keepdims=True)

    gain_q = jnp.zeros((HEAD, 1), F32)
    for h in range(heads):
        rows = slice(h * HEAD, (h + 1) * HEAD)
        gt_ref[rows, :], more = back(dq[rows, :], raw_ref[rows, :], qg)
        gain_q += more
    k_at = slice(q_own, q_own + HEAD)
    gt_ref[k_at, :], gain_k = back((dk[...] * scale).T, raw_ref[k_at, :], kg)
    gt_ref[q_own + HEAD : q_own + 2 * HEAD, :] = dv[...].T.astype(BF16)
    w = w_ref[:, : q_own + 2 * HEAD]
    for dy, ref in zip(STEPS, (back0_ref, back1_ref, back2_ref, back3_ref)):
        for dx in range(2):
            at = pl.multiple_of(block_at(me_ref, dy, dx, blocks) * local, local)
            ref[dx] = dot(gt_ref[:, pl.ds(at, local)], w, 0, 1).astype(BF16)
    lane = lax.broadcasted_iota(jnp.int32, (HEAD, 128), 1)
    gain_ref[...] = jnp.where(lane == 0, gain_q, jnp.where(lane == 1, gain_k, 0.0))


def attend_backward(me, qt, kt, vt, raw, lse, pos, grads, gains, freq, w_own, block=256):
    blocks, q_own, local = grads.shape
    length = blocks * local
    heads = q_own // HEAD
    rows = q_own + 2 * HEAD
    return pl.pallas_call(
        functools.partial(backward_kernel, heads=heads, block=block),
        out_shape=(
            shape(rows, length),
            *[shape(2, local, w_own.shape[0])] * 4,
            shape(HEAD, 128, dtype=F32),
        ),
        in_specs=[smem()] + vmem(10),
        scratch_shapes=[
            pltpu.VMEM((length, HEAD), BF16),
            pltpu.VMEM((length, HEAD), BF16),
            pltpu.VMEM((heads * block, HEAD), BF16),
            pltpu.VMEM((heads * block, HEAD), BF16),
            pltpu.VMEM((length, HEAD), F32),
            pltpu.VMEM((length, HEAD), F32),
            pltpu.VMEM((q_own, length), F32),
        ],
        compiler_params=pltpu.CompilerParams(vmem_limit_bytes=VMEM),
        cost_estimate=cost(0.1),
        name="attend_backward",
    )(me, qt, kt, vt, raw, lse, pos, grads, gains, freq, w_own)


def mlp_kernel(me_ref, *refs, pieces, width, pad, n_seq):
    att_refs, refs = refs[:pieces], refs[pieces:]
    x_ref, g_ref, gain_ref, w_ref = refs[:4]
    (
        mid_ref, second_ref, hid_ref, gate_grad_ref, up_grad_ref, back_ref, out_ref, own_ref,
        w_out, w_gate, w_up, w_down, sems, att_all,
    ) = refs[4:]
    places = (
        (0, width, w_out),
        (width, pad, w_gate),
        (width + pad, pad, w_up),
        (width + 2 * pad, pad, w_down),
    )
    copies = [
        pltpu.make_async_copy(w_ref.at[:, at : at + n], to, sems.at[i])
        for i, (at, n, to) in enumerate(places)
    ]
    first = pl.program_id(0) == 0

    @pl.when(first)
    def _():
        for copy in copies:
            copy.start()

    def ready(i):
        @pl.when(first)
        def _():
            copies[i].wait()

    n, rows, _ = g_ref.shape
    count = n * rows
    x = x_ref[...].reshape(count, width).astype(F32)
    if pieces == 1:
        att = att_refs[0][...].reshape(width, count)
    else:
        part = width // n_seq
        for dy, ref in zip(STEPS, att_refs):
            for dx in range(2):
                at = pl.multiple_of(block_at(me_ref, dy, dx, n_seq) * part, part)
                att_all[pl.ds(at, part), :] = ref[dx]
        att = att_all[...]
    for i in range(n):

        @pl.when(me_ref[0] == n * pl.program_id(0) + i)
        def _(i=i):
            own_ref[...] = att[:, i * rows : (i + 1) * rows]

    ready(0)
    middle = x + dot(att, w_out[...], 0, 1)
    mid_ref[...] = middle.reshape(n, rows, width)
    inverse = lax.rsqrt(jnp.mean(middle * middle, axis=1, keepdims=True) + EPS)
    second = (middle * inverse * gain_ref[1:2, :]).astype(BF16)
    second_ref[...] = second
    ready(1)
    gate = dot(second, w_gate[...], 1, 0)
    ready(2)
    up = dot(second, w_up[...], 1, 0)
    sig = lax.logistic(gate)
    act = gate * sig
    hidden = (act * up).astype(BF16)
    hid_ref[...] = hidden
    ready(3)
    grad_hidden = dot(g_ref[...].reshape(count, width), w_down[...], 1, 0)
    gate_grad = (grad_hidden * up * sig * (1.0 + gate * (1.0 - sig))).astype(BF16)
    up_grad = (grad_hidden * act).astype(BF16)
    gate_grad_ref[...] = gate_grad
    up_grad_ref[...] = up_grad
    back = dot(gate_grad, w_gate[...], 1, 1) + dot(up_grad, w_up[...], 1, 1)
    back_ref[...] = back.astype(BF16).reshape(n, rows, width)
    out_ref[...] = dot(hidden, w_down[...], 1, 1).astype(BF16).reshape(n, rows, width)


def mlp(me, att, x_all, g_all, gain, weights, half, per=4):
    count = att[0].shape[-1]
    n_seq, local, width = x_all.shape
    rows = local // HALVES
    pad = (weights.shape[1] - width) // 3
    step = per * rows
    spec = pl.BlockSpec
    flat = spec((step, pad), lambda i: (i, 0))
    stack = spec((per, rows, width), lambda i: (i, 0, 0))
    return pl.pallas_call(
        functools.partial(mlp_kernel, pieces=len(att), width=width, pad=pad, n_seq=n_seq),
        grid=(n_seq // per,),
        in_specs=[smem()]
        + [
            spec(a.shape[:-1] + (step,), lambda i, lead=(0,) * (a.ndim - 1): lead + (i,))
            for a in att
        ]
        + [
            spec((per, rows, width), lambda i: (i, half, 0)),
            spec((per, rows, width), lambda i: (i, half, 0)),
            spec((8, width), lambda i: (0, 0)),
            spec(memory_space=pl.ANY),
        ],
        out_specs=[
            stack,
            spec((step, width), lambda i: (i, 0)),
            flat,
            flat,
            flat,
            stack,
            stack,
            spec((width, rows), lambda i: (0, 0)),
        ],
        out_shape=(
            shape(n_seq, rows, width, dtype=F32),
            shape(count, width),
            shape(count, pad),
            shape(count, pad),
            shape(count, pad),
            shape(n_seq, rows, width),
            shape(n_seq, rows, width),
            shape(width, rows),
        ),
        scratch_shapes=[
            pltpu.VMEM((width, width), BF16),
            pltpu.VMEM((width, pad), BF16),
            pltpu.VMEM((width, pad), BF16),
            pltpu.VMEM((width, pad), BF16),
            pltpu.SemaphoreType.DMA((4,)),
            pltpu.VMEM((width, step), BF16),
        ],
        compiler_params=pltpu.CompilerParams(vmem_limit_bytes=VMEM),
        cost_estimate=cost(1),
        name="mlp_part",
    )(me, *att, x_all, g_all, gain, weights)


def mlp_grads_kernel(core_ref, *refs, shard):
    seconds, cotangents = refs[:HALVES], refs[HALVES : 2 * HALVES]
    rest, own_ref, other_ref = refs[2 * HALVES : -2], refs[-2], refs[-1]
    pad = rest[0].shape[1]
    core = core_ref[0]
    for k in range(3):
        total = None
        for h in range(HALVES):
            left = (seconds if k < 2 else cotangents)[h][...]
            left = left.reshape(-1, left.shape[-1])
            term = dot(left, rest[k * HALVES + h][...], 0, 0)
            total = term if total is None else total + term
        total = total.astype(BF16)
        lanes = slice(k * pad, (k + 1) * pad)
        for i in range(total.shape[0] // shard):
            part = total[i * shard : (i + 1) * shard]

            @pl.when(core == i % 2)
            def _(part=part, i=i, lanes=lanes):
                own_ref[i // 2, :, lanes] = part

            @pl.when(core != i % 2)
            def _(part=part, i=i, lanes=lanes):
                other_ref[i // 2, :, lanes] = part


def mlp_grads(core, seconds, g_all, gates, ups, hiddens, shard, tile=384):
    count, width = seconds[0].shape
    pad = gates[0].shape[1]
    n_seq, local, _ = g_all.shape
    rows = local // HALVES
    spec = pl.BlockSpec
    return pl.pallas_call(
        functools.partial(mlp_grads_kernel, shard=shard),
        grid=(width // tile,),
        in_specs=[smem()]
        + [spec((count, tile), lambda r: (0, r))] * HALVES
        + [spec((n_seq, rows, tile), lambda r, h=h: (0, h, r)) for h in range(HALVES)]
        + [spec((count, pad), lambda r: (0, 0))] * (3 * HALVES),
        out_specs=[spec((tile // shard // 2, shard, 3 * pad), lambda r: (r, 0, 0))] * 2,
        out_shape=(shape(width // shard // 2, shard, 3 * pad),) * 2,
        compiler_params=pltpu.CompilerParams(vmem_limit_bytes=VMEM),
        cost_estimate=cost(0.1),
        name="mlp_grads",
    )(core, *seconds, *([g_all] * HALVES), *gates, *ups, *hiddens)


def core_sums_kernel(mine_ref, got_ref, out_ref):
    out_ref[...] = (mine_ref[...].astype(F32) + got_ref[...].astype(F32)).astype(BF16)


def core_sums(mine, got):
    spec = pl.BlockSpec((2,) + mine.shape[1:], lambda i: (i, 0, 0))
    return pl.pallas_call(
        core_sums_kernel,
        grid=(mine.shape[0] // 2,),
        in_specs=[spec] * 2,
        out_specs=spec,
        out_shape=shape(*mine.shape),
        compiler_params=pltpu.CompilerParams(vmem_limit_bytes=VMEM),
        cost_estimate=cost(0.1),
        name="core_sums",
    )(mine, got)


def middle_kernel(
    me_ref, back0_ref, back1_ref, mid0_ref, mid1_ref, g_ref, gain_ref, w_ref,
    branch_ref, grad_ref, att_ref, gain_grad_ref, mid_out_ref,
    mid, w, sems, *, width,
):
    half = back0_ref.shape[1]
    me = me_ref[0]
    copies = [
        pltpu.make_async_copy(mid0_ref.at[me], mid.at[pl.ds(0, half)], sems.at[0]),
        pltpu.make_async_copy(mid1_ref.at[me], mid.at[pl.ds(half, half)], sems.at[1]),
        pltpu.make_async_copy(w_ref.at[:, :width], w, sems.at[2]),
    ]
    for copy in copies:
        copy.start()
    grad = jnp.concatenate(
        [jnp.sum(ref[...].astype(F32), axis=0) for ref in (back0_ref, back1_ref)], axis=0
    )
    copies[0].wait()
    copies[1].wait()
    middle = mid[...]
    mid_out_ref[...] = middle
    inverse = lax.rsqrt(jnp.mean(middle * middle, axis=1, keepdims=True) + EPS)
    u = grad * gain_ref[1:2, :]
    pull = jnp.mean(u * middle, axis=1, keepdims=True)
    grad_middle = (
        g_ref[...].astype(F32) + inverse * u - middle * (inverse * inverse * inverse) * pull
    )
    gain_grad_ref[...] = jnp.sum(grad * middle * inverse, axis=0, keepdims=True)
    grad_ref[...] = grad_middle
    branch = grad_middle.astype(BF16)
    branch_ref[...] = branch
    copies[2].wait()
    att_ref[...] = dot(branch, w[...], 1, 0).T.astype(BF16)


def middle_back(me, backs, mids, g_own, gain, weights):
    local, width = g_own.shape
    anywhere = pl.BlockSpec(memory_space=pl.ANY)
    return pl.pallas_call(
        functools.partial(middle_kernel, width=width),
        in_specs=[smem()] + vmem(2) + [anywhere] * 2 + vmem(2) + [anywhere],
        out_shape=(
            shape(local, width),
            shape(local, width, dtype=F32),
            shape(width, local),
            shape(1, width, dtype=F32),
            shape(local, width, dtype=F32),
        ),
        scratch_shapes=[
            pltpu.VMEM((local, width), F32),
            pltpu.VMEM((width, width), BF16),
            pltpu.SemaphoreType.DMA((3,)),
        ],
        compiler_params=pltpu.CompilerParams(vmem_limit_bytes=VMEM),
        cost_estimate=cost(0.1),
        name="middle_back",
    )(me, *backs, *mids, g_own, gain, weights)


def head_grads_kernel(
    core_ref, gt_ref, normed_ref, gains_ref, mlp_gain_ref, branch_ref, *refs, per, shard,
):
    att_refs, (own_ref, other_ref) = refs[:-2], refs[-2:]
    att = jnp.concatenate([ref[...] for ref in att_refs], axis=1)
    out = dot(branch_ref[...], att, 0, 1).astype(BF16)
    qkv = dot(gt_ref[...], normed_ref[...], 1, 0)
    width = normed_ref.shape[1]
    gains = dot(gains_ref[:, :HEAD].astype(BF16), owners(width, per), 0, 0)
    row = lax.broadcasted_iota(jnp.int32, gains.shape, 0)
    gains = jnp.where(row == 2, mlp_gain_ref[...], gains)
    qkv = jnp.concatenate([qkv, gains], axis=0).T.astype(BF16)
    core = core_ref[0]
    cut = qkv.shape[1]
    for i in range(width // shard):
        rows = slice(i * shard, (i + 1) * shard)

        def put(ref, rows=rows, i=i):
            ref[i // 2, :, :cut] = qkv[rows]
            ref[i // 2, :, cut:] = out[rows]

        pl.when(core == i % 2)(functools.partial(put, own_ref))
        pl.when(core != i % 2)(functools.partial(put, other_ref))


def head_grads(core, gt, normed, gains, mlp_gain, branch, atts, per, shard):
    width = normed.shape[1]
    columns = gt.shape[0] + HEAD + atts[0].shape[0]
    return pl.pallas_call(
        functools.partial(head_grads_kernel, per=per, shard=shard),
        in_specs=[smem()] + vmem(5 + len(atts)),
        out_shape=(shape(width // shard // 2, shard, columns),) * 2,
        compiler_params=pltpu.CompilerParams(vmem_limit_bytes=VMEM),
        cost_estimate=cost(0.1),
        name="head_grads",
    )(core, gt, normed, gains, mlp_gain, branch, *atts)


def out_blocks_kernel(sums_ref, got_ref, qkv_ref, out_ref):
    total = sums_ref[...] + got_ref[...].astype(F32)
    cut, part = qkv_ref.shape[1], out_ref.shape[2]
    qkv_ref[...] = total[:, :cut].astype(BF16)
    for j in range(out_ref.shape[0]):
        out_ref[j] = total[:, cut + j * part : cut + (j + 1) * part].astype(BF16)


def out_blocks(sums, got, n_seq, cut):
    shard, columns = got.shape
    return pl.pallas_call(
        out_blocks_kernel,
        out_shape=(shape(shard, cut), shape(n_seq, shard, (columns - cut) // n_seq)),
        compiler_params=pltpu.CompilerParams(vmem_limit_bytes=VMEM),
        cost_estimate=cost(0.1),
        name="out_blocks",
    )(sums, got)


def shards_kernel(
    in_ref, wq_ref, wk_ref, wv_ref, gain_ref,
    gq_ref, gk_ref, gv_ref, go_ref, gains_ref, *, q_own, kv_own,
):
    n = in_ref.shape[0]

    def side(start, stop):
        return jnp.concatenate([in_ref[j][:, start:stop] for j in range(n)], axis=1).astype(F32)

    k_at, v_at, end = q_own, q_own + kv_own, q_own + 2 * kv_own
    gq, gk, gv = side(0, k_at), side(k_at, v_at), side(v_at, end)
    gq_ref[...], gk_ref[...], gv_ref[...] = gq, gk, gv
    go_ref[...] = side(end + HEAD, end + HEAD + q_own)
    attn = sum(
        jnp.sum(w[...].astype(F32) * g, axis=1, keepdims=True)
        for w, g in ((wq_ref, gq), (wk_ref, gk), (wv_ref, gv))
    ) / gain_ref[...].astype(F32)
    sums = jnp.sum(in_ref[:, :, 256:384].astype(F32), axis=0)
    lane = lax.broadcasted_iota(jnp.int32, sums.shape, 1)
    gains_ref[...] = jnp.where(lane == 0, attn, sums).T


def own_shards(parts, w_query, w_key, w_value, attn_gain, q_own, kv_own):
    shard, q_all = w_query.shape
    return pl.pallas_call(
        functools.partial(shards_kernel, q_own=q_own, kv_own=kv_own),
        out_shape=(
            shape(shard, q_all, dtype=F32),
            shape(shard, w_key.shape[1], dtype=F32),
            shape(shard, w_value.shape[1], dtype=F32),
            shape(shard, q_all, dtype=F32),
            shape(128, shard, dtype=F32),
        ),
        compiler_params=pltpu.CompilerParams(vmem_limit_bytes=VMEM),
        cost_estimate=cost(1),
        name="own_shards",
    )(parts, w_query, w_key, w_value, attn_gain)


def mlp_shards_kernel(x_ref, grads_ref, got_ref, gate_ref, up_ref, down_ref):
    width = gate_ref.shape[1]
    total = grads_ref[x_ref[0]].astype(F32) + got_ref[...].astype(F32)
    for k, ref in enumerate((gate_ref, up_ref, down_ref)):
        ref[...] = total[:, k * PAD : k * PAD + width]


def mlp_shards(x_hi, grads, got, width):
    return pl.pallas_call(
        mlp_shards_kernel,
        in_specs=[smem()] + vmem(2),
        out_shape=(shape(got.shape[0], width, dtype=F32),) * 3,
        compiler_params=pltpu.CompilerParams(vmem_limit_bytes=VMEM),
        cost_estimate=cost(1),
        name="mlp_shards",
    )(x_hi, grads, got)


def shift(size, by):
    return [(i, (i + by) % size) for i in range(size)]


def to_all(block):
    n = lax.axis_size("seq")
    return lax.all_to_all(jnp.broadcast_to(block[None], (n,) + block.shape), "seq", 0, 0, tiled=True)


def exchange(blocks):
    return lax.all_to_all(blocks, "seq", 0, 0, tiled=True)


def total_of(blocks):
    return jnp.sum(blocks.astype(F32), axis=0)


def step_seq(block, dy, dx=0):
    n = lax.axis_size("seq")
    to = [(i, (i + 2 * dy) % n ^ dx) for i in range(n)]
    return lax.ppermute(block, "seq", to)


def gather_pieces(block):
    half = block.shape[0] // 2
    up, down = step_seq(block, 1), step_seq(block, -1)
    beside = step_seq(block, 0, 1)
    beside_up, beside_down = step_seq(beside, 1), step_seq(beside, -1)
    return (
        block,
        beside,
        up,
        down,
        beside_up,
        beside_down,
        step_seq(up[:half], 1),
        step_seq(down[half:], -1),
        step_seq(beside_up[:half], 1),
        step_seq(beside_down[half:], -1),
    )


def along_y(pair):
    return (pair,) + tuple(step_seq(pair, -dy) for dy in STEPS[1:])


def near_of(parts, sign=1):
    return tuple(step_seq(parts[i], sign * STEPS[i]) for i in (1, 2))


def sum_pairs(pairs):
    total = sum(pair.astype(F32) for pair in pairs)
    return total[0] + step_seq(total[1].astype(pairs[0].dtype), 0, 1).astype(F32)


def pairs_for(blocks):
    n = lax.axis_size("seq")
    me = lax.axis_index("seq")
    y, x = me // 2, me % 2
    grid = blocks.reshape((n // 2, 2) + blocks.shape[1:])
    grid = jnp.where(x == 0, grid, grid[:, ::-1])
    pick = functools.partial(lax.dynamic_index_in_dim, grid, axis=0, keepdims=False)
    return [pick((y + dy) % (n // 2)) for dy in STEPS]


def in_order_kernel(me_ref, *refs, n_seq):
    out_ref = refs[-1]
    for dy, ref in zip(STEPS, refs[:-1]):
        for dx in range(2):
            out_ref[block_at(me_ref, dy, dx, n_seq)] = ref[dx]


def in_order(me, pairs, n_seq):
    return pl.pallas_call(
        functools.partial(in_order_kernel, n_seq=n_seq),
        in_specs=[smem()] + vmem(len(pairs)),
        out_shape=shape(n_seq, *pairs[0].shape[1:]),
        compiler_params=pltpu.CompilerParams(vmem_limit_bytes=VMEM),
        cost_estimate=cost(0.1),
        name="in_order",
    )(me, *pairs)


def swap(held, bit):
    n = lax.axis_size("fsdp")
    return lax.ppermute(held, "fsdp", [(i, i ^ bit) for i in range(n)])


def along_z(grid):
    n = lax.axis_size("fsdp")
    z = lax.axis_index("fsdp") // 4
    grid = grid.reshape((n // 4, 2) + grid.shape[1:])
    pick = functools.partial(lax.dynamic_index_in_dim, grid, axis=0, keepdims=False)
    got = [lax.ppermute(pick((z + by) % (n // 4)), "fsdp", shift(n, 4 * by)) for by in range(1, 4)]
    return [pick(z)] + got


def sum_z(pairs):
    x_hi = lax.axis_index("fsdp") // 2 % 2
    pick = functools.partial(lax.dynamic_index_in_dim, axis=0, keepdims=False)
    held = sum(pair.astype(F32) for pair in pairs)
    return pick(held, x_hi), pick(held, 1 - x_hi).astype(pairs[0].dtype)


def pair(mine, other, low):
    return jnp.concatenate([jnp.where(low, mine, other), jnp.where(low, other, mine)], axis=0)


def gather_fsdp(block, first, second):
    n = lax.axis_size("fsdp")
    me = lax.axis_index("fsdp")
    held = block[None]
    held = pair(held, swap(held, 2), me // 2 % 2 == 0)
    held, _ = lax.optimization_barrier((held, first))
    other = swap(held, 1)
    low = me % 2 == 0
    held = jnp.stack([jnp.where(low, held, other), jnp.where(low, other, held)], axis=1)
    held = held.reshape((1, 4) + block.shape)
    held, _ = lax.optimization_barrier((held, second))
    whole = jnp.zeros((n // 4,) + held.shape[1:], block.dtype)
    z = me // 4
    whole = lax.dynamic_update_slice_in_dim(whole, held, z, 0)
    for by in range(1, n // 4):
        got = lax.ppermute(held, "fsdp", shift(n, 4 * by))
        whole = lax.dynamic_update_slice_in_dim(whole, got, (z - by) % (n // 4), 0)
    return whole.reshape((n * block.shape[0],) + block.shape[1:])


def lanes(array, width):
    return jnp.pad(array, ((0, 0), (0, width - array.shape[1])))


def rows(vector, count):
    return jnp.pad(vector, (0, count - vector.shape[0]))


def on_device(
    tokens,
    segments,
    out_grad,
    attn_gain,
    w_query,
    w_key,
    w_value,
    query_gain,
    key_gain,
    w_out,
    mlp_gain,
    w_gate,
    w_up,
    w_down,
):
    n_seq = lax.axis_size("seq")
    n_fsdp = lax.axis_size("fsdp")
    me = lax.axis_index("seq")
    here = me.astype(jnp.int32).reshape(1)
    core = (lax.axis_index("fsdp") % 2).astype(jnp.int32).reshape(1)
    x_hi = (lax.axis_index("fsdp") // 2 % 2).astype(jnp.int32).reshape(1)
    local, width = tokens.shape[1:]
    shard = attn_gain.shape[0]
    q_all, kv_all = w_query.shape[1], w_key.shape[1]
    q_own, kv_own = q_all // n_seq, kv_all // n_seq
    heads = q_own // HEAD
    qkv_own = q_own + 2 * kv_own
    hidden_own = w_gate.shape[1]
    gain_own = query_gain.shape[0]

    x = tokens[0]
    numbers = lax.pad(
        segments.astype(BF16), jnp.zeros((), BF16), ((0, local - 1, 0), (0, 128 - local, 0))
    )
    x_pieces = gather_pieces(jnp.concatenate([x, numbers], axis=1))

    mlp_pack = jnp.concatenate(
        [w_out.T, lanes(w_gate, PAD), lanes(w_up, PAD), lanes(w_down.T, PAD)], axis=1
    )
    mlp_full = lax.all_gather(mlp_pack, "fsdp", axis=0, tiled=True)

    mlp_pack = jnp.concatenate(
        [w_out.T, lanes(w_gate, PAD), lanes(w_up, PAD), lanes(w_down.T, PAD)], axis=1
    )
    mlp_full = lax.all_gather(mlp_pack, "fsdp", axis=0, tiled=True)

    own = lax.dynamic_slice_in_dim
    head_pack = jnp.concatenate(
        [
            own(w_query, me * q_own, q_own, 1),
            own(w_key, me * kv_own, kv_own, 1),
            own(w_value, me * kv_own, kv_own, 1),
            attn_gain[:, None],
            mlp_gain[:, None],
            rows(query_gain, shard)[:, None],
            rows(key_gain, shard)[:, None],
        ],
        axis=1,
    )
    head_full = gather_fsdp(lanes(head_pack, 384), x_pieces[1], x_pieces[2:4])

    freq = (ROPE_BASE ** (-2.0 * jnp.arange(HEAD // 2, dtype=F32) / HEAD)).reshape(-1, 1)

    after = lax.optimization_barrier
    g_pair = jnp.stack([out_grad[0], step_seq(out_grad[0], 0, 1)])
    g_pair, x_pieces = after((g_pair, x_pieces))
    g_pairs = along_y(g_pair)

    x_all, normed, raw, qt, kt, vt, att, att_parts, lse, pos, gain_rows, gains = attend_forward(
        here, x_pieces, head_full, freq, heads, n_seq, gain_own
    )
    x_all = x_all.reshape(n_seq, local, width)
    att_beside = step_seq(att_parts, 0, 1)
    att_pair, g_pairs = after((jnp.stack([att_parts[0], att_beside[0]]), g_pairs))
    att_first = along_y(att_pair)
    att_sent, att_first = after((att_parts[1], att_first))
    att_second = (to_all(att_sent),)
    g_all = in_order(here, g_pairs, n_seq)
    done = [mlp(here, att_first, x_all, g_all, gain_rows, mlp_full, 0)]
    back_first = exchange(done[0][5])
    att_second, done[0] = after((att_second, done[0]))
    done.append(mlp(here, att_second, x_all, g_all, gain_rows, mlp_full, 1))
    middle_parts, seconds, hiddens, gate_grads, up_grads, back_parts, out_parts, att_own = zip(*done)
    back_sent, back_first = after((back_parts[1], back_first))
    backs = (back_first, exchange(back_sent))
    mine, other = mlp_grads(core, seconds, g_all, gate_grads, up_grads, hiddens, shard)
    mine, other, backs = after((mine, other, backs))
    got = swap(other, 1)

    def sum_fsdp(core_sum):
        parts = lax.psum_scatter(
            core_sum.reshape(n_fsdp // 4, 2, shard, -1),
            "fsdp",
            scatter_dimension=0,
            tiled=True,
            axis_index_groups=[list(range(i, n_fsdp, 4)) for i in range(4)],
        ).reshape(2, shard, -1)
        far = lax.dynamic_index_in_dim(parts, 1 - x_hi[0], 0, keepdims=False)
        return parts, far

    branch, grad_middle, grad_att, grad_mlp_g, middle = middle_back(
        here, backs, middle_parts, out_grad[0], gain_rows, mlp_full
    )
    grad_heads = exchange(grad_att.reshape(n_seq, q_own, local))
    mine, got, out_parts, branch = after((mine, got, out_parts, branch))
    chip_sums = core_sums(mine, got)
    out = pairs_for(jnp.concatenate(out_parts, axis=1))
    out, grad_heads, chip_sums = after((out, grad_heads, chip_sums))
    mlp_sums, mlp_far = sum_fsdp(chip_sums)

    out_pairs = (out[0], *near_of(out), step_seq(out[3], STEPS[3]))
    gt, *back, gain_grads = attend_backward(
        here, qt, kt, vt, raw, lse, pos, grad_heads, gains, freq, head_full
    )
    head_mine, head_other = head_grads(
        core, gt, normed, gain_grads, grad_mlp_g, branch, att_own, gain_own, shard
    )
    back, head_mine, head_other, out_pairs = after((back, head_mine, head_other, out_pairs))
    back_pairs = (back[0], *near_of(back), step_seq(back[3], STEPS[3]))
    z_pairs = along_z(core_sums(head_mine, swap(head_other, 1)))
    mlp_got = swap(mlp_far, 2)
    z_pairs, back_pairs, mlp_got = after((z_pairs, back_pairs, mlp_got))
    head_own, head_far = sum_z(z_pairs)
    qkv_owned, out_blocks_own = out_blocks(
        head_own, swap(head_far, 2), n_seq, qkv_own + HEAD
    )
    out_owned = total_of(exchange(out_blocks_own)).astype(BF16)
    att_owned = jnp.concatenate([qkv_owned, out_owned], axis=1)
    grad_normed = sum_pairs(back_pairs)
    layer_out = (middle + sum_pairs(out_pairs)).astype(BF16)
    xf = x.astype(F32)
    inverse_x = lax.rsqrt(jnp.mean(xf * xf, axis=-1, keepdims=True) + EPS)
    ux = grad_normed * gain_rows[:1]
    grad_tokens = (
        grad_middle
        + inverse_x * ux
        - xf * inverse_x**3 * jnp.mean(ux * xf, axis=-1, keepdims=True)
    )

    mlp_owned = mlp_shards(x_hi, mlp_sums, mlp_got, hidden_own)
    att_seq, (gw_gate, gw_up, gw_down) = after((to_all(att_owned), mlp_owned))
    gw_query, gw_key, gw_value, gw_out, gain_sums = own_shards(
        att_seq, w_query, w_key, w_value, attn_gain[:, None], q_own, kv_own
    )
    at = qkv_own - 256
    return (
        layer_out[None],
        grad_tokens[None],
        gain_sums[0],
        gw_query,
        gw_key,
        gw_value,
        gain_sums[at, :gain_own],
        gain_sums[at + 1, :gain_own],
        gw_out.T,
        gain_sums[at + 2],
        gw_gate,
        gw_up,
        gw_down.T,
    )


def solution(mesh):
    in_specs = (
        P("fsdp", "seq", None),
        P("fsdp", "seq"),
        P("fsdp", "seq", None),
        P("fsdp"),
        P("fsdp", None),
        P("fsdp", None),
        P("fsdp", None),
        P("fsdp"),
        P("fsdp"),
        P(None, "fsdp"),
        P("fsdp"),
        P("fsdp", "seq"),
        P("fsdp", "seq"),
        P("seq", "fsdp"),
    )
    out_specs = (
        P("fsdp", "seq", None),
        P("fsdp", "seq", None),
        P("fsdp"),
        P("fsdp", None),
        P("fsdp", None),
        P("fsdp", None),
        P("fsdp"),
        P("fsdp"),
        P(None, "fsdp"),
        P("fsdp"),
        P("fsdp", "seq"),
        P("fsdp", "seq"),
        P("seq", "fsdp"),
    )
    return jax.shard_map(
        on_device, mesh=mesh, in_specs=in_specs, out_specs=out_specs, check_vma=False
    )
```

```python
import functools

import jax
import jax.numpy as jnp
from jax import lax
from jax.experimental import pallas as pl
from jax.experimental.pallas import tpu as pltpu
from jax.sharding import PartitionSpec as P

HEAD = 64
EPS = 1e-05
ROPE_BASE = 1000000.0
F32 = jnp.float32
BF16 = jnp.bfloat16
PAD = 896
HALVES = 2
VMEM = 56 * 2**20


def dot(a, b, ca, cb):
    return lax.dot_general(a, b, (((ca,), (cb,)), ((), ())), preferred_element_type=F32)


def shape(*dims, dtype=BF16):
    return jax.ShapeDtypeStruct(dims, dtype)


def cost(micros):
    return pl.CostEstimate(flops=int(micros * 1.15e9), bytes_accessed=2**10, transcendentals=0)


def angles_of(freq_ref, position):
    turn = freq_ref[...] * position
    return jnp.cos(turn), jnp.sin(turn)


def mask_of(rows, start, index, heads):
    row = lax.broadcasted_iota(jnp.int32, (rows, start.shape[1]), 0).astype(F32)
    allowed = (row >= start) & (row <= index)
    return jnp.concatenate([allowed] * heads, axis=1)


PIECES = (
    (0, 0, 0, 1),
    (0, 1, 0, 1),
    (-1, 0, 0, 1),
    (1, 0, 0, 1),
    (-1, 1, 0, 1),
    (1, 1, 0, 1),
    (2, 0, 0, 2),
    (2, 0, 1, 2),
    (2, 1, 0, 2),
    (2, 1, 1, 2),
)


STEPS = (0, -1, 1, 2)


def block_at(me_ref, dy, dx, n_seq):
    y, x = me_ref[0] // 2, me_ref[0] % 2
    return (y + dy + n_seq // 2) % (n_seq // 2) * 2 + (x + dx) % 2


def first_row(me_ref, piece, n_seq, rows):
    dy, dx, part, parts = piece
    block = block_at(me_ref, dy, dx, n_seq)
    return pl.multiple_of(block * rows + part * (rows // parts), rows // parts)


def owners(width, per):
    lane = lax.broadcasted_iota(jnp.int32, (HEAD, width), 1)
    row = lax.broadcasted_iota(jnp.int32, (HEAD, width), 0)
    shard = width * per // HEAD
    owner, place = lane // shard, lane % shard
    return jnp.where((place < per) & (owner * per + place == row), 1.0, 0.0).astype(BF16)


def forward_kernel(
    me_ref, *refs, pieces, heads, block, n_seq, per,
):
    x_refs, refs = refs[:pieces], refs[pieces:]
    w_ref, freq_ref = refs[:2]
    (
        x_ref, normed_ref, raw_ref, qt_ref, kt_ref, vt_ref, att_ref, parts_ref, lse_ref, pos_ref,
        rows_ref, gains_ref, k_rows, segs_ref,
    ) = refs[2:]
    local = x_refs[0].shape[0]
    width = w_ref.shape[0]
    at = (heads + 2) * HEAD
    slab = w_ref[:, at // 128 * 128 :]
    rows = slab.astype(F32).T
    at = at % 128
    rows_ref[...] = rows[at : at + 8]
    gain = rows[at : at + 1]
    gains_ref[...] = dot(owners(width, per), slab, 1, 0)
    qg, kg = gains_ref[:, at + 2 : at + 3], gains_ref[:, at + 3 : at + 4]
    length = n_seq * local
    q_own = heads * HEAD
    for piece, ref in zip(PIECES, x_refs):
        at = first_row(me_ref, piece, n_seq, local)
        here = pl.ds(at, ref.shape[0])
        x = ref[:, :width]
        x_ref[here, :] = x
        x = x.astype(F32)
        inverse = lax.rsqrt(jnp.mean(x * x, axis=1, keepdims=True) + EPS)
        normed_ref[here, :] = (x * inverse * gain).astype(BF16)
        if piece[2] == 0:
            segs_ref[0:1, pl.ds(pl.multiple_of(at, 128), local)] = ref[
                0:1, width : width + local
            ].astype(F32)
    segs = segs_ref[0:1, :]
    index = lax.broadcasted_iota(jnp.int32, (1, length), 1).astype(F32)
    first = jnp.sum(jnp.where(segs == 0.0, 1.0, 0.0), axis=1, keepdims=True)
    middle = jnp.sum(jnp.where(segs == 1.0, 1.0, 0.0), axis=1, keepdims=True)
    start = jnp.where(segs >= 1.0, first, 0.0) + jnp.where(segs >= 2.0, middle, 0.0)
    position = index - start
    pos_ref[0:1, :] = position
    cosine, sine = angles_of(freq_ref, position)
    raw = dot(normed_ref[...], w_ref[...], 1, 0).T
    raw_ref[...] = raw[: q_own + HEAD]
    for h in range(heads + 1):
        values = raw[h * HEAD : (h + 1) * HEAD]
        inverse = lax.rsqrt(jnp.mean(values * values, axis=0, keepdims=True) + EPS)
        values = values * inverse * (qg if h < heads else kg)
        a, b = values[: HEAD // 2], values[HEAD // 2 :]
        turned = jnp.concatenate([a * cosine - b * sine, b * cosine + a * sine], axis=0)
        if h < heads:
            qt_ref[h * HEAD : (h + 1) * HEAD, :] = turned.astype(BF16)
        else:
            kt_ref[...] = turned.astype(BF16)
            k_rows[...] = turned.T.astype(BF16)
    vt_ref[...] = raw[q_own + HEAD : q_own + 2 * HEAD].astype(BF16)
    part = local // HALVES
    for c in range(length // block):
        stop = (c + 1) * block
        lanes = slice(c * block, stop)
        q = jnp.concatenate(
            [qt_ref[h * HEAD : (h + 1) * HEAD, lanes] for h in range(heads)], axis=1
        )
        scores = dot(k_rows[:stop, :], q, 1, 0) * HEAD**-0.5
        allowed = mask_of(stop, start[:, lanes], index[:, lanes], heads)
        scores = jnp.where(allowed, scores, -1e30)
        peak = jnp.max(scores, axis=0, keepdims=True)
        exps = jnp.exp(scores - peak)
        total = jnp.sum(exps, axis=0, keepdims=True)
        probs = (exps * (1.0 / total)).astype(BF16)
        mixed = dot(vt_ref[:, :stop], probs, 1, 0).astype(BF16)
        lse = peak + jnp.log(total)
        for h in range(heads):
            own = mixed[:, h * block : (h + 1) * block]
            rows = slice(h * HEAD, (h + 1) * HEAD)
            att_ref[rows, lanes] = own
            lse_ref[h : h + 1, lanes] = lse[:, h * block : (h + 1) * block]
            for k in range(HALVES):
                cut = [
                    own[:, t * local + k * part : t * local + (k + 1) * part]
                    for t in range(block // local)
                ]
                at = c * (block // HALVES)
                parts_ref[k, rows, at : at + block // HALVES] = jnp.concatenate(cut, axis=1)


def smem():
    return pl.BlockSpec(memory_space=pltpu.SMEM)


def vmem(count):
    return [pl.BlockSpec(memory_space=pltpu.VMEM)] * count


def attend_forward(me, x_pieces, w_own, freq, heads, n_seq, per, block=256):
    local = x_pieces[0].shape[0]
    width = w_own.shape[0]
    length = n_seq * local
    q_own = heads * HEAD
    return pl.pallas_call(
        functools.partial(
            forward_kernel,
            pieces=len(x_pieces),
            heads=heads,
            block=block,
            n_seq=n_seq,
            per=per,
        ),
        in_specs=[smem()] + vmem(len(x_pieces) + 2),
        out_shape=(
            shape(length, width),
            shape(length, width),
            shape(q_own + HEAD, length, dtype=F32),
            shape(q_own, length),
            shape(HEAD, length),
            shape(HEAD, length),
            shape(q_own, length),
            shape(HALVES, q_own, length // HALVES),
            shape(8, length, dtype=F32),
            shape(8, length, dtype=F32),
            shape(8, width, dtype=F32),
            shape(HEAD, 128, dtype=F32),
        ),
        scratch_shapes=[pltpu.VMEM((length, HEAD), BF16), pltpu.VMEM((8, length), F32)],
        compiler_params=pltpu.CompilerParams(vmem_limit_bytes=VMEM),
        cost_estimate=cost(0.1),
        name="attend_forward",
    )(me, *x_pieces, w_own, freq)


def backward_kernel(
    me_ref, qt_ref, kt_ref, vt_ref, raw_ref, lse_ref, pos_ref, g_ref, gains_ref, freq_ref, w_ref,
    gt_ref, back0_ref, back1_ref, back2_ref, back3_ref, gain_ref,
    k_rows, v_rows, q_rows, g_rows, dk, dv, dq, *, heads, block,
):
    length = kt_ref.shape[1]
    blocks, _, local = g_ref.shape
    q_own = heads * HEAD
    at = (heads + 2) * HEAD % 128 + 2
    qg, kg = gains_ref[:, at : at + 1], gains_ref[:, at + 1 : at + 2]
    position = pos_ref[0:1, :]
    index = lax.broadcasted_iota(jnp.int32, (1, length), 1).astype(F32)
    start = index - position
    cosine, sine = angles_of(freq_ref, position)
    k_rows[...] = kt_ref[...].astype(F32).T.astype(BF16)
    v_rows[...] = vt_ref[...].astype(F32).T.astype(BF16)
    dk[...] = jnp.zeros_like(dk)
    dv[...] = jnp.zeros_like(dv)
    scale = HEAD**-0.5
    per = block // local
    for c in range(length // block):
        stop = (c + 1) * block
        lanes = slice(c * block, stop)
        q = jnp.concatenate(
            [qt_ref[h * HEAD : (h + 1) * HEAD, lanes] for h in range(heads)], axis=1
        )
        g = jnp.concatenate(
            [
                g_ref[c * per + t, h * HEAD : (h + 1) * HEAD, :]
                for h in range(heads)
                for t in range(per)
            ],
            axis=1,
        )
        lse = jnp.concatenate([lse_ref[h : h + 1, lanes] for h in range(heads)], axis=1)
        q_rows[...] = q.astype(F32).T.astype(BF16)
        g_rows[...] = g.astype(F32).T.astype(BF16)
        scores = dot(k_rows[:stop, :], q, 1, 0) * scale
        allowed = mask_of(stop, start[:, lanes], index[:, lanes], heads)
        probs = jnp.where(allowed, jnp.exp(scores - lse), 0.0)
        grad_probs = dot(v_rows[:stop, :], g, 1, 0)
        inner = jnp.sum(probs * grad_probs, axis=0, keepdims=True)
        grad_scores = (probs * (grad_probs - inner)).astype(BF16)
        dv[:stop, :] += dot(probs.astype(BF16), g_rows[...], 1, 0)
        dk[:stop, :] += dot(grad_scores, q_rows[...], 1, 0)
        part = dot(kt_ref[:, :stop], grad_scores, 1, 0) * scale
        for h in range(heads):
            dq[h * HEAD : (h + 1) * HEAD, lanes] = part[:, h * block : (h + 1) * block]

    def back(grad, raw, gain):
        grad = grad.astype(BF16).astype(F32)
        a, b = grad[: HEAD // 2], grad[HEAD // 2 :]
        grad = jnp.concatenate([a * cosine + b * sine, b * cosine - a * sine], axis=0)
        inverse = lax.rsqrt(jnp.mean(raw * raw, axis=0, keepdims=True) + EPS)
        u = grad * gain
        pull = jnp.mean(u * raw, axis=0, keepdims=True)
        out = inverse * u - raw * (inverse * inverse * inverse) * pull
        return out.astype(BF16), jnp.sum(grad * raw * inverse, axis=1, keepdims=True)

    gain_q = jnp.zeros((HEAD, 1), F32)
    for h in range(heads):
        rows = slice(h * HEAD, (h + 1) * HEAD)
        gt_ref[rows, :], more = back(dq[rows, :], raw_ref[rows, :], qg)
        gain_q += more
    k_at = slice(q_own, q_own + HEAD)
    gt_ref[k_at, :], gain_k = back((dk[...] * scale).T, raw_ref[k_at, :], kg)
    gt_ref[q_own + HEAD : q_own + 2 * HEAD, :] = dv[...].T.astype(BF16)
    w = w_ref[:, : q_own + 2 * HEAD]
    for dy, ref in zip(STEPS, (back0_ref, back1_ref, back2_ref, back3_ref)):
        for dx in range(2):
            at = pl.multiple_of(block_at(me_ref, dy, dx, blocks) * local, local)
            ref[dx] = dot(gt_ref[:, pl.ds(at, local)], w, 0, 1).astype(BF16)
    lane = lax.broadcasted_iota(jnp.int32, (HEAD, 128), 1)
    gain_ref[...] = jnp.where(lane == 0, gain_q, jnp.where(lane == 1, gain_k, 0.0))


def attend_backward(me, qt, kt, vt, raw, lse, pos, grads, gains, freq, w_own, block=256):
    blocks, q_own, local = grads.shape
    length = blocks * local
    heads = q_own // HEAD
    rows = q_own + 2 * HEAD
    return pl.pallas_call(
        functools.partial(backward_kernel, heads=heads, block=block),
        out_shape=(
            shape(rows, length),
            *[shape(2, local, w_own.shape[0])] * 4,
            shape(HEAD, 128, dtype=F32),
        ),
        in_specs=[smem()] + vmem(10),
        scratch_shapes=[
            pltpu.VMEM((length, HEAD), BF16),
            pltpu.VMEM((length, HEAD), BF16),
            pltpu.VMEM((heads * block, HEAD), BF16),
            pltpu.VMEM((heads * block, HEAD), BF16),
            pltpu.VMEM((length, HEAD), F32),
            pltpu.VMEM((length, HEAD), F32),
            pltpu.VMEM((q_own, length), F32),
        ],
        compiler_params=pltpu.CompilerParams(vmem_limit_bytes=VMEM),
        cost_estimate=cost(0.1),
        name="attend_backward",
    )(me, qt, kt, vt, raw, lse, pos, grads, gains, freq, w_own)


def mlp_kernel(me_ref, *refs, pieces, width, pad, n_seq):
    att_refs, refs = refs[:pieces], refs[pieces:]
    x_ref, g_ref, gain_ref, w_ref = refs[:4]
    (
        mid_ref, second_ref, hid_ref, gate_grad_ref, up_grad_ref, back_ref, out_ref, own_ref,
        w_out, w_gate, w_up, w_down, sems, att_all,
    ) = refs[4:]
    places = (
        (0, width, w_out),
        (width, pad, w_gate),
        (width + pad, pad, w_up),
        (width + 2 * pad, pad, w_down),
    )
    copies = [
        pltpu.make_async_copy(w_ref.at[:, at : at + n], to, sems.at[i])
        for i, (at, n, to) in enumerate(places)
    ]
    first = pl.program_id(0) == 0

    @pl.when(first)
    def _():
        for copy in copies:
            copy.start()

    def ready(i):
        @pl.when(first)
        def _():
            copies[i].wait()

    n, rows, _ = g_ref.shape
    count = n * rows
    x = x_ref[...].reshape(count, width).astype(F32)
    if pieces == 1:
        att = att_refs[0][...].reshape(width, count)
    else:
        part = width // n_seq
        for dy, ref in zip(STEPS, att_refs):
            for dx in range(2):
                at = pl.multiple_of(block_at(me_ref, dy, dx, n_seq) * part, part)
                att_all[pl.ds(at, part), :] = ref[dx]
        att = att_all[...]
    for i in range(n):

        @pl.when(me_ref[0] == n * pl.program_id(0) + i)
        def _(i=i):
            own_ref[...] = att[:, i * rows : (i + 1) * rows]

    ready(0)
    middle = x + dot(att, w_out[...], 0, 1)
    for i in range(n):

        @pl.when(me_ref[0] == n * pl.program_id(0) + i)
        def _(i=i):
            mid_ref[...] = middle[i * rows : (i + 1) * rows]

    inverse = lax.rsqrt(jnp.mean(middle * middle, axis=1, keepdims=True) + EPS)
    second = (middle * inverse * gain_ref[1:2, :]).astype(BF16)
    second_ref[...] = second
    ready(1)
    gate = dot(second, w_gate[...], 1, 0)
    ready(2)
    up = dot(second, w_up[...], 1, 0)
    sig = lax.logistic(gate)
    act = gate * sig
    hidden = (act * up).astype(BF16)
    hid_ref[...] = hidden
    ready(3)
    grad_hidden = dot(g_ref[...].reshape(count, width), w_down[...], 1, 0)
    gate_grad = (grad_hidden * up * sig * (1.0 + gate * (1.0 - sig))).astype(BF16)
    up_grad = (grad_hidden * act).astype(BF16)
    gate_grad_ref[...] = gate_grad
    up_grad_ref[...] = up_grad
    back = dot(gate_grad, w_gate[...], 1, 1) + dot(up_grad, w_up[...], 1, 1)
    back_ref[...] = back.astype(BF16).reshape(n, rows, width)
    out_ref[...] = dot(hidden, w_down[...], 1, 1).astype(BF16).reshape(n, rows, width)


def mlp(me, att, x_all, g_all, gain, weights, half, per=4):
    count = att[0].shape[-1]
    n_seq, local, width = x_all.shape
    rows = local // HALVES
    pad = (weights.shape[1] - width) // 3
    step = per * rows
    spec = pl.BlockSpec
    flat = spec((step, pad), lambda i: (i, 0))
    stack = spec((per, rows, width), lambda i: (i, 0, 0))
    return pl.pallas_call(
        functools.partial(mlp_kernel, pieces=len(att), width=width, pad=pad, n_seq=n_seq),
        grid=(n_seq // per,),
        in_specs=[smem()]
        + [
            spec(a.shape[:-1] + (step,), lambda i, lead=(0,) * (a.ndim - 1): lead + (i,))
            for a in att
        ]
        + [
            spec((per, rows, width), lambda i: (i, half, 0)),
            spec((per, rows, width), lambda i: (i, half, 0)),
            spec((8, width), lambda i: (0, 0)),
            spec(memory_space=pl.ANY),
        ],
        out_specs=[
            spec((rows, width), lambda i: (0, 0)),
            spec((step, width), lambda i: (i, 0)),
            flat,
            flat,
            flat,
            stack,
            stack,
            spec((width, rows), lambda i: (0, 0)),
        ],
        out_shape=(
            shape(rows, width, dtype=F32),
            shape(count, width),
            shape(count, pad),
            shape(count, pad),
            shape(count, pad),
            shape(n_seq, rows, width),
            shape(n_seq, rows, width),
            shape(width, rows),
        ),
        scratch_shapes=[
            pltpu.VMEM((width, width), BF16),
            pltpu.VMEM((width, pad), BF16),
            pltpu.VMEM((width, pad), BF16),
            pltpu.VMEM((width, pad), BF16),
            pltpu.SemaphoreType.DMA((4,)),
            pltpu.VMEM((width, step), BF16),
        ],
        compiler_params=pltpu.CompilerParams(vmem_limit_bytes=VMEM),
        cost_estimate=cost(1),
        name="mlp_part",
    )(me, *att, x_all, g_all, gain, weights)


def mlp_grads_kernel(core_ref, *refs, shard):
    seconds, cotangents = refs[:HALVES], refs[HALVES : 2 * HALVES]
    rest, own_ref, other_ref = refs[2 * HALVES : -2], refs[-2], refs[-1]
    pad = rest[0].shape[1]
    core = core_ref[0]
    for k in range(3):
        total = None
        for h in range(HALVES):
            left = (seconds if k < 2 else cotangents)[h][...]
            left = left.reshape(-1, left.shape[-1])
            term = dot(left, rest[k * HALVES + h][...], 0, 0)
            total = term if total is None else total + term
        total = total.astype(BF16)
        lanes = slice(k * pad, (k + 1) * pad)
        for i in range(total.shape[0] // shard):
            part = total[i * shard : (i + 1) * shard]

            @pl.when(core == i % 2)
            def _(part=part, i=i, lanes=lanes):
                own_ref[i // 2, :, lanes] = part

            @pl.when(core != i % 2)
            def _(part=part, i=i, lanes=lanes):
                other_ref[i // 2, :, lanes] = part


def mlp_grads(core, seconds, g_all, gates, ups, hiddens, shard, tile=384):
    count, width = seconds[0].shape
    pad = gates[0].shape[1]
    n_seq, local, _ = g_all.shape
    rows = local // HALVES
    spec = pl.BlockSpec
    return pl.pallas_call(
        functools.partial(mlp_grads_kernel, shard=shard),
        grid=(width // tile,),
        in_specs=[smem()]
        + [spec((count, tile), lambda r: (0, r))] * HALVES
        + [spec((n_seq, rows, tile), lambda r, h=h: (0, h, r)) for h in range(HALVES)]
        + [spec((count, pad), lambda r: (0, 0))] * (3 * HALVES),
        out_specs=[spec((tile // shard // 2, shard, 3 * pad), lambda r: (r, 0, 0))] * 2,
        out_shape=(shape(width // shard // 2, shard, 3 * pad),) * 2,
        compiler_params=pltpu.CompilerParams(vmem_limit_bytes=VMEM),
        cost_estimate=cost(0.1),
        name="mlp_grads",
    )(core, *seconds, *([g_all] * HALVES), *gates, *ups, *hiddens)


def core_sums_kernel(mine_ref, got_ref, out_ref):
    out_ref[...] = (mine_ref[...].astype(F32) + got_ref[...].astype(F32)).astype(BF16)


def core_sums(mine, got):
    spec = pl.BlockSpec((2,) + mine.shape[1:], lambda i: (i, 0, 0))
    return pl.pallas_call(
        core_sums_kernel,
        grid=(mine.shape[0] // 2,),
        in_specs=[spec] * 2,
        out_specs=spec,
        out_shape=shape(*mine.shape),
        compiler_params=pltpu.CompilerParams(vmem_limit_bytes=VMEM),
        cost_estimate=cost(0.1),
        name="core_sums",
    )(mine, got)


def middle_kernel(
    back0_ref, back1_ref, mid0_ref, mid1_ref, g_ref, gain_ref, w_ref,
    branch_ref, grad_ref, att_ref, gain_grad_ref, mid_out_ref,
    w, sem, *, width,
):
    copy = pltpu.make_async_copy(w_ref.at[:, :width], w, sem)
    copy.start()
    grad = jnp.concatenate(
        [jnp.sum(ref[...].astype(F32), axis=0) for ref in (back0_ref, back1_ref)], axis=0
    )
    middle = jnp.concatenate([mid0_ref[...], mid1_ref[...]], axis=0)
    mid_out_ref[...] = middle
    inverse = lax.rsqrt(jnp.mean(middle * middle, axis=1, keepdims=True) + EPS)
    u = grad * gain_ref[1:2, :]
    pull = jnp.mean(u * middle, axis=1, keepdims=True)
    grad_middle = (
        g_ref[...].astype(F32) + inverse * u - middle * (inverse * inverse * inverse) * pull
    )
    gain_grad_ref[...] = jnp.sum(grad * middle * inverse, axis=0, keepdims=True)
    grad_ref[...] = grad_middle
    branch = grad_middle.astype(BF16)
    branch_ref[...] = branch
    copy.wait()
    att_ref[...] = dot(branch, w[...], 1, 0).T.astype(BF16)


def middle_back(backs, mids, g_own, gain, weights):
    local, width = g_own.shape
    return pl.pallas_call(
        functools.partial(middle_kernel, width=width),
        in_specs=vmem(6) + [pl.BlockSpec(memory_space=pl.ANY)],
        out_shape=(
            shape(local, width),
            shape(local, width, dtype=F32),
            shape(width, local),
            shape(1, width, dtype=F32),
            shape(local, width, dtype=F32),
        ),
        scratch_shapes=[
            pltpu.VMEM((width, width), BF16),
            pltpu.SemaphoreType.DMA(()),
        ],
        compiler_params=pltpu.CompilerParams(vmem_limit_bytes=VMEM),
        cost_estimate=cost(0.1),
        name="middle_back",
    )(*backs, *mids, g_own, gain, weights)


def split_rows(core_ref, rows, shard, own_ref, other_ref):
    core = core_ref[0]
    for i in range(rows.shape[0] // shard):

        def put(ref, i=i):
            ref[i // 2] = rows[i * shard : (i + 1) * shard]

        pl.when(core == i % 2)(functools.partial(put, own_ref))
        pl.when(core != i % 2)(functools.partial(put, other_ref))


def qkv_grads_kernel(
    core_ref, gt_ref, normed_ref, gains_ref, mlp_gain_ref, own_ref, other_ref, *, per, shard,
):
    qkv = dot(gt_ref[...], normed_ref[...], 1, 0)
    width = normed_ref.shape[1]
    gains = dot(gains_ref[:, :HEAD].astype(BF16), owners(width, per), 0, 0)
    row = lax.broadcasted_iota(jnp.int32, gains.shape, 0)
    gains = jnp.where(row == 2, mlp_gain_ref[...], gains)
    rows = jnp.concatenate([qkv, gains], axis=0).T.astype(BF16)
    split_rows(core_ref, rows, shard, own_ref, other_ref)


def qkv_grads(core, gt, normed, gains, mlp_gain, per, shard):
    count, width = normed.shape
    return pl.pallas_call(
        functools.partial(qkv_grads_kernel, per=per, shard=shard),
        in_specs=[smem()] + vmem(4),
        out_shape=(shape(width // shard // 2, shard, gt.shape[0] + HEAD),) * 2,
        compiler_params=pltpu.CompilerParams(vmem_limit_bytes=VMEM),
        cost_estimate=cost(0.1),
        name="qkv_grads",
    )(core, gt, normed, gains, mlp_gain)


def out_grads_kernel(core_ref, branch_ref, *refs, shard):
    att_refs, (own_ref, other_ref) = refs[:-2], refs[-2:]
    att = jnp.concatenate([ref[...] for ref in att_refs], axis=1)
    rows = dot(branch_ref[...], att, 0, 1).astype(BF16)
    split_rows(core_ref, rows, shard, own_ref, other_ref)


def out_grads(core, branch, atts, shard):
    width = branch.shape[1]
    heads = atts[0].shape[0]
    return pl.pallas_call(
        functools.partial(out_grads_kernel, shard=shard),
        in_specs=[smem()] + vmem(1 + len(atts)),
        out_shape=(shape(width // shard // 2, shard, heads),) * 2,
        compiler_params=pltpu.CompilerParams(vmem_limit_bytes=VMEM),
        cost_estimate=cost(0.1),
        name="out_grads",
    )(core, branch, *atts)


def out_blocks_kernel(x_ref, sums_ref, got_ref, out_ref):
    total = (sums_ref[x_ref[0]].astype(F32) + got_ref[...].astype(F32)).astype(BF16)
    part = out_ref.shape[2]
    for j in range(out_ref.shape[0]):
        out_ref[j] = total[:, j * part : (j + 1) * part]


def out_blocks(x_hi, sums, got, n_seq):
    shard, heads = got.shape
    return pl.pallas_call(
        out_blocks_kernel,
        in_specs=[smem()] + vmem(2),
        out_shape=shape(n_seq, shard, heads // n_seq),
        compiler_params=pltpu.CompilerParams(vmem_limit_bytes=VMEM),
        cost_estimate=cost(0.1),
        name="out_blocks",
    )(x_hi, sums, got)


def shards_kernel(
    in_ref, wq_ref, wk_ref, wv_ref, gain_ref,
    gq_ref, gk_ref, gv_ref, go_ref, *gain_refs, q_own, kv_own,
):
    n = in_ref.shape[0]

    def side(start, stop):
        return jnp.concatenate([in_ref[j][:, start:stop] for j in range(n)], axis=1).astype(F32)

    k_at, v_at, end = q_own, q_own + kv_own, q_own + 2 * kv_own
    gq, gk, gv = side(0, k_at), side(k_at, v_at), side(v_at, end)
    gq_ref[...], gk_ref[...], gv_ref[...] = gq, gk, gv
    go_ref[...] = side(end + HEAD, end + HEAD + q_own)
    attn = sum(
        jnp.sum(w[...].astype(F32) * g, axis=1, keepdims=True)
        for w, g in ((wq_ref, gq), (wk_ref, gk), (wv_ref, gv))
    ) / gain_ref[...].astype(F32)
    sums = jnp.sum(in_ref[:, :, 256:384].astype(F32), axis=0)
    lane = lax.broadcasted_iota(jnp.int32, sums.shape, 1)
    gains = jnp.where(lane == 0, attn, sums).T
    at = v_at + kv_own - 256
    for row, ref in zip((0, at, at + 1, at + 2), gain_refs):
        ref[...] = gains[row : row + 1, : ref.shape[1]]


def own_shards(parts, w_query, w_key, w_value, attn_gain, q_own, kv_own, gain_own):
    shard, q_all = w_query.shape
    return pl.pallas_call(
        functools.partial(shards_kernel, q_own=q_own, kv_own=kv_own),
        out_shape=(
            shape(shard, q_all, dtype=F32),
            shape(shard, w_key.shape[1], dtype=F32),
            shape(shard, w_value.shape[1], dtype=F32),
            shape(shard, q_all, dtype=F32),
            shape(1, shard, dtype=F32),
            shape(1, gain_own, dtype=F32),
            shape(1, gain_own, dtype=F32),
            shape(1, shard, dtype=F32),
        ),
        compiler_params=pltpu.CompilerParams(vmem_limit_bytes=VMEM),
        cost_estimate=cost(1),
        name="own_shards",
    )(parts, w_query, w_key, w_value, attn_gain)


def mlp_shards_kernel(x_ref, grads_ref, got_ref, gate_ref, up_ref, down_ref):
    width = gate_ref.shape[1]
    total = grads_ref[x_ref[0]].astype(F32) + got_ref[...].astype(F32)
    for k, ref in enumerate((gate_ref, up_ref, down_ref)):
        ref[...] = total[:, k * PAD : k * PAD + width]


def mlp_shards(x_hi, grads, got, width):
    return pl.pallas_call(
        mlp_shards_kernel,
        in_specs=[smem()] + vmem(2),
        out_shape=(shape(got.shape[0], width, dtype=F32),) * 3,
        compiler_params=pltpu.CompilerParams(vmem_limit_bytes=VMEM),
        cost_estimate=cost(1),
        name="mlp_shards",
    )(x_hi, grads, got)


def shift(size, by):
    return [(i, (i + by) % size) for i in range(size)]


def to_all(block):
    n = lax.axis_size("seq")
    return lax.all_to_all(jnp.broadcast_to(block[None], (n,) + block.shape), "seq", 0, 0, tiled=True)


def exchange(blocks):
    return lax.all_to_all(blocks, "seq", 0, 0, tiled=True)


def total_of(blocks):
    return jnp.sum(blocks.astype(F32), axis=0)


def step_seq(block, dy, dx=0):
    n = lax.axis_size("seq")
    to = [(i, (i + 2 * dy) % n ^ dx) for i in range(n)]
    return lax.ppermute(block, "seq", to)


def gather_pieces(block):
    half = block.shape[0] // 2
    up, down = step_seq(block, 1), step_seq(block, -1)
    beside = step_seq(block, 0, 1)
    beside_up, beside_down = step_seq(beside, 1), step_seq(beside, -1)
    return (
        block,
        beside,
        up,
        down,
        beside_up,
        beside_down,
        step_seq(up[:half], 1),
        step_seq(down[half:], -1),
        step_seq(beside_up[:half], 1),
        step_seq(beside_down[half:], -1),
    )


def along_y(pair):
    return (pair,) + tuple(step_seq(pair, -dy) for dy in STEPS[1:])


def near_of(parts, sign=1):
    return tuple(step_seq(parts[i], sign * STEPS[i]) for i in (1, 2))


def sum_pairs(pairs):
    total = sum(pair.astype(F32) for pair in pairs)
    return total[0] + step_seq(total[1].astype(pairs[0].dtype), 0, 1).astype(F32)


def pairs_for(blocks):
    n = lax.axis_size("seq")
    me = lax.axis_index("seq")
    y, x = me // 2, me % 2
    grid = blocks.reshape((n // 2, 2) + blocks.shape[1:])
    grid = jnp.where(x == 0, grid, grid[:, ::-1])
    pick = functools.partial(lax.dynamic_index_in_dim, grid, axis=0, keepdims=False)
    return [pick((y + dy) % (n // 2)) for dy in STEPS]


def in_order_kernel(me_ref, *refs, n_seq):
    out_ref = refs[-1]
    for dy, ref in zip(STEPS, refs[:-1]):
        for dx in range(2):
            out_ref[block_at(me_ref, dy, dx, n_seq)] = ref[dx]


def in_order(me, pairs, n_seq):
    return pl.pallas_call(
        functools.partial(in_order_kernel, n_seq=n_seq),
        in_specs=[smem()] + vmem(len(pairs)),
        out_shape=shape(n_seq, *pairs[0].shape[1:]),
        compiler_params=pltpu.CompilerParams(vmem_limit_bytes=VMEM),
        cost_estimate=cost(0.1),
        name="in_order",
    )(me, *pairs)


def swap(held, bit):
    n = lax.axis_size("fsdp")
    return lax.ppermute(held, "fsdp", [(i, i ^ bit) for i in range(n)])


def along_z(grid):
    n = lax.axis_size("fsdp")
    z = lax.axis_index("fsdp") // 4
    grid = grid.reshape((n // 4, 2) + grid.shape[1:])
    pick = functools.partial(lax.dynamic_index_in_dim, grid, axis=0, keepdims=False)
    got = [lax.ppermute(pick((z + by) % (n // 4)), "fsdp", shift(n, 4 * by)) for by in range(1, 4)]
    return [pick(z)] + got


def sum_z(pairs):
    x_hi = lax.axis_index("fsdp") // 2 % 2
    pick = functools.partial(lax.dynamic_index_in_dim, axis=0, keepdims=False)
    held = sum(pair.astype(F32) for pair in pairs)
    got = swap(pick(held, 1 - x_hi).astype(pairs[0].dtype), 2)
    return pick(held, x_hi) + got.astype(F32)


def pair(mine, other, low):
    return jnp.concatenate([jnp.where(low, mine, other), jnp.where(low, other, mine)], axis=0)


def gather_fsdp(block, first, second):
    n = lax.axis_size("fsdp")
    me = lax.axis_index("fsdp")
    held = block[None]
    held = pair(held, swap(held, 2), me // 2 % 2 == 0)
    held, _ = lax.optimization_barrier((held, first))
    other = swap(held, 1)
    low = me % 2 == 0
    held = jnp.stack([jnp.where(low, held, other), jnp.where(low, other, held)], axis=1)
    held = held.reshape((1, 4) + block.shape)
    held, _ = lax.optimization_barrier((held, second))
    whole = jnp.zeros((n // 4,) + held.shape[1:], block.dtype)
    z = me // 4
    whole = lax.dynamic_update_slice_in_dim(whole, held, z, 0)
    for by in range(1, n // 4):
        got = lax.ppermute(held, "fsdp", shift(n, 4 * by))
        whole = lax.dynamic_update_slice_in_dim(whole, got, (z - by) % (n // 4), 0)
    return whole.reshape((n * block.shape[0],) + block.shape[1:])


def lanes(array, width):
    return jnp.pad(array, ((0, 0), (0, width - array.shape[1])))


def rows(vector, count):
    return jnp.pad(vector, (0, count - vector.shape[0]))


def on_device(
    tokens,
    segments,
    out_grad,
    attn_gain,
    w_query,
    w_key,
    w_value,
    query_gain,
    key_gain,
    w_out,
    mlp_gain,
    w_gate,
    w_up,
    w_down,
):
    n_seq = lax.axis_size("seq")
    n_fsdp = lax.axis_size("fsdp")
    me = lax.axis_index("seq")
    here = me.astype(jnp.int32).reshape(1)
    core = (lax.axis_index("fsdp") % 2).astype(jnp.int32).reshape(1)
    x_hi = (lax.axis_index("fsdp") // 2 % 2).astype(jnp.int32).reshape(1)
    local, width = tokens.shape[1:]
    shard = attn_gain.shape[0]
    q_all, kv_all = w_query.shape[1], w_key.shape[1]
    q_own, kv_own = q_all // n_seq, kv_all // n_seq
    heads = q_own // HEAD
    qkv_own = q_own + 2 * kv_own
    hidden_own = w_gate.shape[1]
    gain_own = query_gain.shape[0]

    x = tokens[0]
    numbers = lax.pad(
        segments.astype(BF16), jnp.zeros((), BF16), ((0, local - 1, 0), (0, 128 - local, 0))
    )
    x_pieces = gather_pieces(jnp.concatenate([x, numbers], axis=1))

    mlp_pack = jnp.concatenate(
        [w_out.T, lanes(w_gate, PAD), lanes(w_up, PAD), lanes(w_down.T, PAD)], axis=1
    )
    mlp_full = lax.all_gather(mlp_pack, "fsdp", axis=0, tiled=True)

    mlp_pack = jnp.concatenate(
        [w_out.T, lanes(w_gate, PAD), lanes(w_up, PAD), lanes(w_down.T, PAD)], axis=1
    )
    mlp_full = lax.all_gather(mlp_pack, "fsdp", axis=0, tiled=True)

    own = lax.dynamic_slice_in_dim
    head_pack = jnp.concatenate(
        [
            own(w_query, me * q_own, q_own, 1),
            own(w_key, me * kv_own, kv_own, 1),
            own(w_value, me * kv_own, kv_own, 1),
            attn_gain[:, None],
            mlp_gain[:, None],
            rows(query_gain, shard)[:, None],
            rows(key_gain, shard)[:, None],
        ],
        axis=1,
    )
    head_full = gather_fsdp(lanes(head_pack, 384), x_pieces[1], x_pieces[2:4])

    freq = (ROPE_BASE ** (-2.0 * jnp.arange(HEAD // 2, dtype=F32) / HEAD)).reshape(-1, 1)

    after = lax.optimization_barrier
    g_pair = jnp.stack([out_grad[0], step_seq(out_grad[0], 0, 1)])
    g_pair, x_pieces = after((g_pair, x_pieces))
    g_pairs = along_y(g_pair)

    x_all, normed, raw, qt, kt, vt, att, att_parts, lse, pos, gain_rows, gains = attend_forward(
        here, x_pieces, head_full, freq, heads, n_seq, gain_own
    )
    x_all = x_all.reshape(n_seq, local, width)
    att_beside = step_seq(att_parts, 0, 1)
    att_pair, g_pairs = after((jnp.stack([att_parts[0], att_beside[0]]), g_pairs))
    att_first = along_y(att_pair)
    att_sent, att_first = after((att_parts[1], att_first))
    att_second = (to_all(att_sent),)
    g_all = in_order(here, g_pairs, n_seq)
    done = [mlp(here, att_first, x_all, g_all, gain_rows, mlp_full, 0)]
    back_first = exchange(done[0][5])
    att_second, done[0] = after((att_second, done[0]))
    done.append(mlp(here, att_second, x_all, g_all, gain_rows, mlp_full, 1))
    middle_parts, seconds, hiddens, gate_grads, up_grads, back_parts, out_parts, att_own = zip(*done)
    back_sent, back_first = after((back_parts[1], back_first))
    backs = (back_first, exchange(back_sent))
    mine, other = mlp_grads(core, seconds, g_all, gate_grads, up_grads, hiddens, shard)
    mine, other, backs = after((mine, other, backs))
    got = swap(other, 1)

    def sum_fsdp(core_sum):
        parts = lax.psum_scatter(
            core_sum.reshape(n_fsdp // 4, 2, shard, -1),
            "fsdp",
            scatter_dimension=0,
            tiled=True,
            axis_index_groups=[list(range(i, n_fsdp, 4)) for i in range(4)],
        ).reshape(2, shard, -1)
        far = lax.dynamic_index_in_dim(parts, 1 - x_hi[0], 0, keepdims=False)
        return parts, far

    branch, grad_middle, grad_att, grad_mlp_g, middle = middle_back(
        backs, middle_parts, out_grad[0], gain_rows, mlp_full
    )
    grad_heads = exchange(grad_att.reshape(n_seq, q_own, local))
    out_mine, out_other = out_grads(core, branch, att_own, shard)
    out_core = core_sums(out_mine, swap(out_other, 1))
    out_parts, branch = after((out_parts, branch))
    out = pairs_for(jnp.concatenate(out_parts, axis=1))
    out, grad_heads, out_core = after((out, grad_heads, out_core))
    out_sums, out_far = sum_fsdp(out_core)

    out_pairs = (out[0], *near_of(out), step_seq(out[3], STEPS[3]))
    gt, *back, gain_grads = attend_backward(
        here, qt, kt, vt, raw, lse, pos, grad_heads, gains, freq, head_full
    )
    qkv_mine, qkv_other = qkv_grads(core, gt, normed, gain_grads, grad_mlp_g, gain_own, shard)
    mine, got, qkv_mine = after((mine, got, qkv_mine))
    chip_sums = core_sums(mine, got)
    back, qkv_other, chip_sums, out_pairs = after((back, qkv_other, chip_sums, out_pairs))
    mlp_sums, mlp_far = sum_fsdp(chip_sums)
    back_pairs = (back[0], *near_of(back), step_seq(back[3], STEPS[3]))
    z_pairs = along_z(core_sums(qkv_mine, swap(qkv_other, 1)))
    out_owned = exchange(out_blocks(x_hi, out_sums, swap(out_far, 2), n_seq))
    z_pairs, out_owned = after((z_pairs, out_owned))
    att_owned = jnp.concatenate([sum_z(z_pairs), total_of(out_owned)], axis=1).astype(BF16)
    att_owned, back_pairs, mlp_far = after((att_owned, back_pairs, mlp_far))
    mlp_got = swap(mlp_far, 2)
    att_seq = to_all(att_owned)
    grad_normed = sum_pairs(back_pairs)
    layer_out = (middle + sum_pairs(out_pairs)).astype(BF16)
    xf = x.astype(F32)
    inverse_x = lax.rsqrt(jnp.mean(xf * xf, axis=-1, keepdims=True) + EPS)
    ux = grad_normed * gain_rows[:1]
    grad_tokens = (
        grad_middle
        + inverse_x * ux
        - xf * inverse_x**3 * jnp.mean(ux * xf, axis=-1, keepdims=True)
    )

    mlp_owned = mlp_shards(x_hi, mlp_sums, mlp_got, hidden_own)
    att_seq, (gw_gate, gw_up, gw_down) = after((att_seq, mlp_owned))
    gw_query, gw_key, gw_value, gw_out, g_attn, g_query, g_key, g_mlp = own_shards(
        att_seq, w_query, w_key, w_value, attn_gain[:, None], q_own, kv_own, gain_own
    )
    return (
        layer_out[None],
        grad_tokens[None],
        g_attn[0],
        gw_query,
        gw_key,
        gw_value,
        g_query[0],
        g_key[0],
        gw_out.T,
        g_mlp[0],
        gw_gate,
        gw_up,
        gw_down.T,
    )


def solution(mesh):
    in_specs = (
        P("fsdp", "seq", None),
        P("fsdp", "seq"),
        P("fsdp", "seq", None),
        P("fsdp"),
        P("fsdp", None),
        P("fsdp", None),
        P("fsdp", None),
        P("fsdp"),
        P("fsdp"),
        P(None, "fsdp"),
        P("fsdp"),
        P("fsdp", "seq"),
        P("fsdp", "seq"),
        P("seq", "fsdp"),
    )
    out_specs = (
        P("fsdp", "seq", None),
        P("fsdp", "seq", None),
        P("fsdp"),
        P("fsdp", None),
        P("fsdp", None),
        P("fsdp", None),
        P("fsdp"),
        P("fsdp"),
        P(None, "fsdp"),
        P("fsdp"),
        P("fsdp", "seq"),
        P("fsdp", "seq"),
        P("seq", "fsdp"),
    )
    return jax.shard_map(
        on_device, mesh=mesh, in_specs=in_specs, out_specs=out_specs, check_vma=False
    )
```

```python
import functools

import jax
import jax.numpy as jnp
from jax import lax
from jax.experimental import pallas as pl
from jax.experimental.pallas import tpu as pltpu
from jax.sharding import PartitionSpec as P

HEAD = 64
EPS = 1e-05
ROPE_BASE = 1000000.0
F32 = jnp.float32
BF16 = jnp.bfloat16
PAD = 896
HALVES = 2
VMEM = 56 * 2**20


def dot(a, b, ca, cb):
    return lax.dot_general(a, b, (((ca,), (cb,)), ((), ())), preferred_element_type=F32)


def shape(*dims, dtype=BF16):
    return jax.ShapeDtypeStruct(dims, dtype)


def cost(micros):
    return pl.CostEstimate(flops=int(micros * 1.15e9), bytes_accessed=2**10, transcendentals=0)


def angles_of(freq_ref, position):
    turn = freq_ref[...] * position
    return jnp.cos(turn), jnp.sin(turn)


def mask_of(rows, start, index, heads):
    row = lax.broadcasted_iota(jnp.int32, (rows, start.shape[1]), 0).astype(F32)
    allowed = (row >= start) & (row <= index)
    return jnp.concatenate([allowed] * heads, axis=1)


PIECES = (
    (0, 0, 0, 1),
    (0, 1, 0, 1),
    (-1, 0, 0, 1),
    (1, 0, 0, 1),
    (-1, 1, 0, 1),
    (1, 1, 0, 1),
    (2, 0, 0, 2),
    (2, 0, 1, 2),
    (2, 1, 0, 2),
    (2, 1, 1, 2),
)


STEPS = (0, -1, 1, 2)


def block_at(me_ref, dy, dx, n_seq):
    y, x = me_ref[0] // 2, me_ref[0] % 2
    return (y + dy + n_seq // 2) % (n_seq // 2) * 2 + (x + dx) % 2


def first_row(me_ref, piece, n_seq, rows):
    dy, dx, part, parts = piece
    block = block_at(me_ref, dy, dx, n_seq)
    return pl.multiple_of(block * rows + part * (rows // parts), rows // parts)


def owners(width, per):
    lane = lax.broadcasted_iota(jnp.int32, (HEAD, width), 1)
    row = lax.broadcasted_iota(jnp.int32, (HEAD, width), 0)
    shard = width * per // HEAD
    owner, place = lane // shard, lane % shard
    return jnp.where((place < per) & (owner * per + place == row), 1.0, 0.0).astype(BF16)


def forward_kernel(
    me_ref, *refs, pieces, heads, block, n_seq, per,
):
    x_refs, refs = refs[:pieces], refs[pieces:]
    w_ref, freq_ref = refs[:2]
    (
        x_ref, normed_ref, raw_ref, qt_ref, kt_ref, vt_ref, att_ref, parts_ref, lse_ref, pos_ref,
        rows_ref, gains_ref, k_rows, segs_ref,
    ) = refs[2:]
    local = x_refs[0].shape[0]
    width = w_ref.shape[0]
    at = (heads + 2) * HEAD
    slab = w_ref[:, at // 128 * 128 :]
    rows = slab.astype(F32).T
    at = at % 128
    rows_ref[...] = rows[at : at + 8]
    gain = rows[at : at + 1]
    gains_ref[...] = dot(owners(width, per), slab, 1, 0)
    qg, kg = gains_ref[:, at + 2 : at + 3], gains_ref[:, at + 3 : at + 4]
    length = n_seq * local
    q_own = heads * HEAD
    for piece, ref in zip(PIECES, x_refs):
        at = first_row(me_ref, piece, n_seq, local)
        here = pl.ds(at, ref.shape[0])
        x = ref[:, :width]
        x_ref[here, :] = x
        x = x.astype(F32)
        inverse = lax.rsqrt(jnp.mean(x * x, axis=1, keepdims=True) + EPS)
        normed_ref[here, :] = (x * inverse * gain).astype(BF16)
        if piece[2] == 0:
            segs_ref[0:1, pl.ds(pl.multiple_of(at, 128), local)] = ref[
                0:1, width : width + local
            ].astype(F32)
    segs = segs_ref[0:1, :]
    index = lax.broadcasted_iota(jnp.int32, (1, length), 1).astype(F32)
    first = jnp.sum(jnp.where(segs == 0.0, 1.0, 0.0), axis=1, keepdims=True)
    middle = jnp.sum(jnp.where(segs == 1.0, 1.0, 0.0), axis=1, keepdims=True)
    start = jnp.where(segs >= 1.0, first, 0.0) + jnp.where(segs >= 2.0, middle, 0.0)
    position = index - start
    pos_ref[0:1, :] = position
    cosine, sine = angles_of(freq_ref, position)
    raw = dot(normed_ref[...], w_ref[...], 1, 0).T
    raw_ref[...] = raw[: q_own + HEAD]
    for h in range(heads + 1):
        values = raw[h * HEAD : (h + 1) * HEAD]
        inverse = lax.rsqrt(jnp.mean(values * values, axis=0, keepdims=True) + EPS)
        values = values * inverse * (qg if h < heads else kg)
        a, b = values[: HEAD // 2], values[HEAD // 2 :]
        turned = jnp.concatenate([a * cosine - b * sine, b * cosine + a * sine], axis=0)
        if h < heads:
            qt_ref[h * HEAD : (h + 1) * HEAD, :] = turned.astype(BF16)
        else:
            kt_ref[...] = turned.astype(BF16)
            k_rows[...] = turned.T.astype(BF16)
    vt_ref[...] = raw[q_own + HEAD : q_own + 2 * HEAD].astype(BF16)
    part = local // HALVES
    for c in range(length // block):
        stop = (c + 1) * block
        lanes = slice(c * block, stop)
        q = jnp.concatenate(
            [qt_ref[h * HEAD : (h + 1) * HEAD, lanes] for h in range(heads)], axis=1
        )
        scores = dot(k_rows[:stop, :], q, 1, 0) * HEAD**-0.5
        allowed = mask_of(stop, start[:, lanes], index[:, lanes], heads)
        scores = jnp.where(allowed, scores, -1e30)
        peak = jnp.max(scores, axis=0, keepdims=True)
        exps = jnp.exp(scores - peak)
        total = jnp.sum(exps, axis=0, keepdims=True)
        probs = (exps * (1.0 / total)).astype(BF16)
        mixed = dot(vt_ref[:, :stop], probs, 1, 0).astype(BF16)
        lse = peak + jnp.log(total)
        for h in range(heads):
            own = mixed[:, h * block : (h + 1) * block]
            rows = slice(h * HEAD, (h + 1) * HEAD)
            att_ref[rows, lanes] = own
            lse_ref[h : h + 1, lanes] = lse[:, h * block : (h + 1) * block]
            for k in range(HALVES):
                cut = [
                    own[:, t * local + k * part : t * local + (k + 1) * part]
                    for t in range(block // local)
                ]
                at = c * (block // HALVES)
                parts_ref[k, rows, at : at + block // HALVES] = jnp.concatenate(cut, axis=1)


def smem():
    return pl.BlockSpec(memory_space=pltpu.SMEM)


def vmem(count):
    return [pl.BlockSpec(memory_space=pltpu.VMEM)] * count


def attend_forward(me, x_pieces, w_own, freq, heads, n_seq, per, block=256):
    local = x_pieces[0].shape[0]
    width = w_own.shape[0]
    length = n_seq * local
    q_own = heads * HEAD
    return pl.pallas_call(
        functools.partial(
            forward_kernel,
            pieces=len(x_pieces),
            heads=heads,
            block=block,
            n_seq=n_seq,
            per=per,
        ),
        in_specs=[smem()] + vmem(len(x_pieces) + 2),
        out_shape=(
            shape(length, width),
            shape(length, width),
            shape(q_own + HEAD, length, dtype=F32),
            shape(q_own, length),
            shape(HEAD, length),
            shape(HEAD, length),
            shape(q_own, length),
            shape(HALVES, q_own, length // HALVES),
            shape(8, length, dtype=F32),
            shape(8, length, dtype=F32),
            shape(8, width, dtype=F32),
            shape(HEAD, 128, dtype=F32),
        ),
        scratch_shapes=[pltpu.VMEM((length, HEAD), BF16), pltpu.VMEM((8, length), F32)],
        compiler_params=pltpu.CompilerParams(vmem_limit_bytes=VMEM),
        cost_estimate=cost(0.1),
        name="attend_forward",
    )(me, *x_pieces, w_own, freq)


def backward_kernel(
    me_ref, qt_ref, kt_ref, vt_ref, raw_ref, lse_ref, pos_ref, g_ref, gains_ref, freq_ref, w_ref,
    gt_ref, back0_ref, back1_ref, back2_ref, back3_ref, gain_ref,
    k_rows, v_rows, q_rows, g_rows, dk, dv, dq, *, heads, block,
):
    length = kt_ref.shape[1]
    blocks, _, local = g_ref.shape
    q_own = heads * HEAD
    at = (heads + 2) * HEAD % 128 + 2
    qg, kg = gains_ref[:, at : at + 1], gains_ref[:, at + 1 : at + 2]
    position = pos_ref[0:1, :]
    index = lax.broadcasted_iota(jnp.int32, (1, length), 1).astype(F32)
    start = index - position
    cosine, sine = angles_of(freq_ref, position)
    k_rows[...] = kt_ref[...].astype(F32).T.astype(BF16)
    v_rows[...] = vt_ref[...].astype(F32).T.astype(BF16)
    dk[...] = jnp.zeros_like(dk)
    dv[...] = jnp.zeros_like(dv)
    scale = HEAD**-0.5
    per = block // local
    for c in range(length // block):
        stop = (c + 1) * block
        lanes = slice(c * block, stop)
        q = jnp.concatenate(
            [qt_ref[h * HEAD : (h + 1) * HEAD, lanes] for h in range(heads)], axis=1
        )
        g = jnp.concatenate(
            [
                g_ref[c * per + t, h * HEAD : (h + 1) * HEAD, :]
                for h in range(heads)
                for t in range(per)
            ],
            axis=1,
        )
        lse = jnp.concatenate([lse_ref[h : h + 1, lanes] for h in range(heads)], axis=1)
        q_rows[...] = q.astype(F32).T.astype(BF16)
        g_rows[...] = g.astype(F32).T.astype(BF16)
        scores = dot(k_rows[:stop, :], q, 1, 0) * scale
        allowed = mask_of(stop, start[:, lanes], index[:, lanes], heads)
        probs = jnp.where(allowed, jnp.exp(scores - lse), 0.0)
        grad_probs = dot(v_rows[:stop, :], g, 1, 0)
        inner = jnp.sum(probs * grad_probs, axis=0, keepdims=True)
        grad_scores = (probs * (grad_probs - inner)).astype(BF16)
        dv[:stop, :] += dot(probs.astype(BF16), g_rows[...], 1, 0)
        dk[:stop, :] += dot(grad_scores, q_rows[...], 1, 0)
        part = dot(kt_ref[:, :stop], grad_scores, 1, 0) * scale
        for h in range(heads):
            dq[h * HEAD : (h + 1) * HEAD, lanes] = part[:, h * block : (h + 1) * block]

    def back(grad, raw, gain):
        grad = grad.astype(BF16).astype(F32)
        a, b = grad[: HEAD // 2], grad[HEAD // 2 :]
        grad = jnp.concatenate([a * cosine + b * sine, b * cosine - a * sine], axis=0)
        inverse = lax.rsqrt(jnp.mean(raw * raw, axis=0, keepdims=True) + EPS)
        u = grad * gain
        pull = jnp.mean(u * raw, axis=0, keepdims=True)
        out = inverse * u - raw * (inverse * inverse * inverse) * pull
        return out.astype(BF16), jnp.sum(grad * raw * inverse, axis=1, keepdims=True)

    gain_q = jnp.zeros((HEAD, 1), F32)
    for h in range(heads):
        rows = slice(h * HEAD, (h + 1) * HEAD)
        gt_ref[rows, :], more = back(dq[rows, :], raw_ref[rows, :], qg)
        gain_q += more
    k_at = slice(q_own, q_own + HEAD)
    gt_ref[k_at, :], gain_k = back((dk[...] * scale).T, raw_ref[k_at, :], kg)
    gt_ref[q_own + HEAD : q_own + 2 * HEAD, :] = dv[...].T.astype(BF16)
    w = w_ref[:, : q_own + 2 * HEAD]
    for dy, ref in zip(STEPS, (back0_ref, back1_ref, back2_ref, back3_ref)):
        for dx in range(2):
            at = pl.multiple_of(block_at(me_ref, dy, dx, blocks) * local, local)
            ref[dx] = dot(gt_ref[:, pl.ds(at, local)], w, 0, 1).astype(BF16)
    lane = lax.broadcasted_iota(jnp.int32, (HEAD, 128), 1)
    gain_ref[...] = jnp.where(lane == 0, gain_q, jnp.where(lane == 1, gain_k, 0.0))


def attend_backward(me, qt, kt, vt, raw, lse, pos, grads, gains, freq, w_own, block=256):
    blocks, q_own, local = grads.shape
    length = blocks * local
    heads = q_own // HEAD
    rows = q_own + 2 * HEAD
    return pl.pallas_call(
        functools.partial(backward_kernel, heads=heads, block=block),
        out_shape=(
            shape(rows, length),
            *[shape(2, local, w_own.shape[0])] * 4,
            shape(HEAD, 128, dtype=F32),
        ),
        in_specs=[smem()] + vmem(10),
        scratch_shapes=[
            pltpu.VMEM((length, HEAD), BF16),
            pltpu.VMEM((length, HEAD), BF16),
            pltpu.VMEM((heads * block, HEAD), BF16),
            pltpu.VMEM((heads * block, HEAD), BF16),
            pltpu.VMEM((length, HEAD), F32),
            pltpu.VMEM((length, HEAD), F32),
            pltpu.VMEM((q_own, length), F32),
        ],
        compiler_params=pltpu.CompilerParams(vmem_limit_bytes=VMEM),
        cost_estimate=cost(0.1),
        name="attend_backward",
    )(me, qt, kt, vt, raw, lse, pos, grads, gains, freq, w_own)


def mlp_kernel(me_ref, *refs, pieces, width, pad, n_seq):
    att_refs, refs = refs[:pieces], refs[pieces:]
    x_ref, g_ref, gain_ref, w_ref = refs[:4]
    (
        mid_ref, second_ref, hid_ref, gate_grad_ref, up_grad_ref, back_ref, out_ref, own_ref,
        w_out, w_gate, w_up, w_down, sems, att_all,
    ) = refs[4:]
    places = (
        (0, width, w_out),
        (width, pad, w_gate),
        (width + pad, pad, w_up),
        (width + 2 * pad, pad, w_down),
    )
    copies = [
        pltpu.make_async_copy(w_ref.at[:, at : at + n], to, sems.at[i])
        for i, (at, n, to) in enumerate(places)
    ]
    first = pl.program_id(0) == 0

    @pl.when(first)
    def _():
        for copy in copies:
            copy.start()

    def ready(i):
        @pl.when(first)
        def _():
            copies[i].wait()

    n, rows, _ = g_ref.shape
    count = n * rows
    x = x_ref[...].reshape(count, width).astype(F32)
    if pieces == 1:
        att = att_refs[0][...].reshape(width, count)
    else:
        part = width // n_seq
        for dy, ref in zip(STEPS, att_refs):
            for dx in range(2):
                at = pl.multiple_of(block_at(me_ref, dy, dx, n_seq) * part, part)
                att_all[pl.ds(at, part), :] = ref[dx]
        att = att_all[...]
    for i in range(n):

        @pl.when(me_ref[0] == n * pl.program_id(0) + i)
        def _(i=i):
            own_ref[...] = att[:, i * rows : (i + 1) * rows]

    ready(0)
    middle = x + dot(att, w_out[...], 0, 1)
    for i in range(n):

        @pl.when(me_ref[0] == n * pl.program_id(0) + i)
        def _(i=i):
            mid_ref[...] = middle[i * rows : (i + 1) * rows]

    inverse = lax.rsqrt(jnp.mean(middle * middle, axis=1, keepdims=True) + EPS)
    second = (middle * inverse * gain_ref[1:2, :]).astype(BF16)
    second_ref[...] = second
    ready(1)
    gate = dot(second, w_gate[...], 1, 0)
    ready(2)
    up = dot(second, w_up[...], 1, 0)
    sig = lax.logistic(gate)
    act = gate * sig
    hidden = (act * up).astype(BF16)
    hid_ref[...] = hidden
    ready(3)
    grad_hidden = dot(g_ref[...].reshape(count, width), w_down[...], 1, 0)
    gate_grad = (grad_hidden * up * sig * (1.0 + gate * (1.0 - sig))).astype(BF16)
    up_grad = (grad_hidden * act).astype(BF16)
    gate_grad_ref[...] = gate_grad
    up_grad_ref[...] = up_grad
    back = dot(gate_grad, w_gate[...], 1, 1) + dot(up_grad, w_up[...], 1, 1)
    back_ref[...] = back.astype(BF16).reshape(n, rows, width)
    out_ref[...] = dot(hidden, w_down[...], 1, 1).astype(BF16).reshape(n, rows, width)


def mlp(me, att, x_all, g_all, gain, weights, half, per=4):
    count = att[0].shape[-1]
    n_seq, local, width = x_all.shape
    rows = local // HALVES
    pad = (weights.shape[1] - width) // 3
    step = per * rows
    spec = pl.BlockSpec
    flat = spec((step, pad), lambda i: (i, 0))
    stack = spec((per, rows, width), lambda i: (i, 0, 0))
    return pl.pallas_call(
        functools.partial(mlp_kernel, pieces=len(att), width=width, pad=pad, n_seq=n_seq),
        grid=(n_seq // per,),
        in_specs=[smem()]
        + [
            spec(a.shape[:-1] + (step,), lambda i, lead=(0,) * (a.ndim - 1): lead + (i,))
            for a in att
        ]
        + [
            spec((per, rows, width), lambda i: (i, half, 0)),
            spec((per, rows, width), lambda i: (i, half, 0)),
            spec((8, width), lambda i: (0, 0)),
            spec(memory_space=pl.ANY),
        ],
        out_specs=[
            spec((rows, width), lambda i: (0, 0)),
            spec((step, width), lambda i: (i, 0)),
            flat,
            flat,
            flat,
            stack,
            stack,
            spec((width, rows), lambda i: (0, 0)),
        ],
        out_shape=(
            shape(rows, width, dtype=F32),
            shape(count, width),
            shape(count, pad),
            shape(count, pad),
            shape(count, pad),
            shape(n_seq, rows, width),
            shape(n_seq, rows, width),
            shape(width, rows),
        ),
        scratch_shapes=[
            pltpu.VMEM((width, width), BF16),
            pltpu.VMEM((width, pad), BF16),
            pltpu.VMEM((width, pad), BF16),
            pltpu.VMEM((width, pad), BF16),
            pltpu.SemaphoreType.DMA((4,)),
            pltpu.VMEM((width, step), BF16),
        ],
        compiler_params=pltpu.CompilerParams(vmem_limit_bytes=VMEM),
        cost_estimate=cost(1),
        name="mlp_part",
    )(me, *att, x_all, g_all, gain, weights)


def mlp_grads_kernel(core_ref, *refs, shard):
    seconds, cotangents = refs[:HALVES], refs[HALVES : 2 * HALVES]
    rest, own_ref, other_ref = refs[2 * HALVES : -2], refs[-2], refs[-1]
    pad = rest[0].shape[1]
    core = core_ref[0]
    for k in range(3):
        total = None
        for h in range(HALVES):
            left = (seconds if k < 2 else cotangents)[h][...]
            left = left.reshape(-1, left.shape[-1])
            term = dot(left, rest[k * HALVES + h][...], 0, 0)
            total = term if total is None else total + term
        total = total.astype(BF16)
        lanes = slice(k * pad, (k + 1) * pad)
        for i in range(total.shape[0] // shard):
            part = total[i * shard : (i + 1) * shard]

            @pl.when(core == i % 2)
            def _(part=part, i=i, lanes=lanes):
                own_ref[i // 2, :, lanes] = part

            @pl.when(core != i % 2)
            def _(part=part, i=i, lanes=lanes):
                other_ref[i // 2, :, lanes] = part


def mlp_grads(core, seconds, g_all, gates, ups, hiddens, shard, tile=384):
    count, width = seconds[0].shape
    pad = gates[0].shape[1]
    n_seq, local, _ = g_all.shape
    rows = local // HALVES
    spec = pl.BlockSpec
    return pl.pallas_call(
        functools.partial(mlp_grads_kernel, shard=shard),
        grid=(width // tile,),
        in_specs=[smem()]
        + [spec((count, tile), lambda r: (0, r))] * HALVES
        + [spec((n_seq, rows, tile), lambda r, h=h: (0, h, r)) for h in range(HALVES)]
        + [spec((count, pad), lambda r: (0, 0))] * (3 * HALVES),
        out_specs=[spec((tile // shard // 2, shard, 3 * pad), lambda r: (r, 0, 0))] * 2,
        out_shape=(shape(width // shard // 2, shard, 3 * pad),) * 2,
        compiler_params=pltpu.CompilerParams(vmem_limit_bytes=VMEM),
        cost_estimate=cost(0.1),
        name="mlp_grads",
    )(core, *seconds, *([g_all] * HALVES), *gates, *ups, *hiddens)


def core_sums_kernel(mine_ref, got_ref, out_ref):
    out_ref[...] = (mine_ref[...].astype(F32) + got_ref[...].astype(F32)).astype(BF16)


def core_sums(mine, got):
    spec = pl.BlockSpec((2,) + mine.shape[1:], lambda i: (i, 0, 0))
    return pl.pallas_call(
        core_sums_kernel,
        grid=(mine.shape[0] // 2,),
        in_specs=[spec] * 2,
        out_specs=spec,
        out_shape=shape(*mine.shape),
        compiler_params=pltpu.CompilerParams(vmem_limit_bytes=VMEM),
        cost_estimate=cost(0.1),
        name="core_sums",
    )(mine, got)


def core_halves_kernel(mine_ref, low_ref, high_ref, out_ref, *, steps):
    def add(got_ref):
        out_ref[...] = (mine_ref[...].astype(F32) + got_ref[...].astype(F32)).astype(BF16)

    low = pl.program_id(0) < steps
    pl.when(low)(functools.partial(add, low_ref))
    pl.when(jnp.logical_not(low))(functools.partial(add, high_ref))


def core_halves(mine, low, high):
    steps = low.shape[0] // 2
    block = (2,) + mine.shape[1:]
    spec = pl.BlockSpec(block, lambda i: (i, 0, 0))
    return pl.pallas_call(
        functools.partial(core_halves_kernel, steps=steps),
        grid=(2 * steps,),
        in_specs=[
            spec,
            pl.BlockSpec(block, lambda i: (jnp.minimum(i, steps - 1), 0, 0)),
            pl.BlockSpec(block, lambda i: (jnp.maximum(i - steps, 0), 0, 0)),
        ],
        out_specs=spec,
        out_shape=shape(*mine.shape),
        compiler_params=pltpu.CompilerParams(vmem_limit_bytes=VMEM),
        cost_estimate=cost(0.1),
        name="core_halves",
    )(mine, low, high)


def middle_kernel(
    back0_ref, back1_ref, mid0_ref, mid1_ref, g_ref, gain_ref, w_ref,
    branch_ref, grad_ref, att_ref, gain_grad_ref, mid_out_ref,
    w, sem, *, width,
):
    copy = pltpu.make_async_copy(w_ref.at[:, :width], w, sem)
    copy.start()
    grad = jnp.concatenate(
        [jnp.sum(ref[...].astype(F32), axis=0) for ref in (back0_ref, back1_ref)], axis=0
    )
    middle = jnp.concatenate([mid0_ref[...], mid1_ref[...]], axis=0)
    mid_out_ref[...] = middle
    inverse = lax.rsqrt(jnp.mean(middle * middle, axis=1, keepdims=True) + EPS)
    u = grad * gain_ref[1:2, :]
    pull = jnp.mean(u * middle, axis=1, keepdims=True)
    grad_middle = (
        g_ref[...].astype(F32) + inverse * u - middle * (inverse * inverse * inverse) * pull
    )
    gain_grad_ref[...] = jnp.sum(grad * middle * inverse, axis=0, keepdims=True)
    grad_ref[...] = grad_middle
    branch = grad_middle.astype(BF16)
    branch_ref[...] = branch
    copy.wait()
    att_ref[...] = dot(branch, w[...], 1, 0).T.astype(BF16)


def middle_back(backs, mids, g_own, gain, weights):
    local, width = g_own.shape
    return pl.pallas_call(
        functools.partial(middle_kernel, width=width),
        in_specs=vmem(6) + [pl.BlockSpec(memory_space=pl.ANY)],
        out_shape=(
            shape(local, width),
            shape(local, width, dtype=F32),
            shape(width, local),
            shape(1, width, dtype=F32),
            shape(local, width, dtype=F32),
        ),
        scratch_shapes=[
            pltpu.VMEM((width, width), BF16),
            pltpu.SemaphoreType.DMA(()),
        ],
        compiler_params=pltpu.CompilerParams(vmem_limit_bytes=VMEM),
        cost_estimate=cost(0.1),
        name="middle_back",
    )(*backs, *mids, g_own, gain, weights)


def split_rows(core_ref, rows, shard, own_ref, other_ref):
    core = core_ref[0]
    for i in range(rows.shape[0] // shard):

        def put(ref, i=i):
            ref[i // 2] = rows[i * shard : (i + 1) * shard]

        pl.when(core == i % 2)(functools.partial(put, own_ref))
        pl.when(core != i % 2)(functools.partial(put, other_ref))


def qkv_grads_kernel(
    core_ref, gt_ref, normed_ref, gains_ref, mlp_gain_ref, own_ref, other_ref, *, per, shard,
):
    qkv = dot(gt_ref[...], normed_ref[...], 1, 0)
    width = normed_ref.shape[1]
    gains = dot(gains_ref[:, :HEAD].astype(BF16), owners(width, per), 0, 0)
    row = lax.broadcasted_iota(jnp.int32, gains.shape, 0)
    gains = jnp.where(row == 2, mlp_gain_ref[...], gains)
    rows = jnp.concatenate([qkv, gains], axis=0).T.astype(BF16)
    split_rows(core_ref, rows, shard, own_ref, other_ref)


def qkv_grads(core, gt, normed, gains, mlp_gain, per, shard):
    count, width = normed.shape
    return pl.pallas_call(
        functools.partial(qkv_grads_kernel, per=per, shard=shard),
        in_specs=[smem()] + vmem(4),
        out_shape=(shape(width // shard // 2, shard, gt.shape[0] + HEAD),) * 2,
        compiler_params=pltpu.CompilerParams(vmem_limit_bytes=VMEM),
        cost_estimate=cost(0.1),
        name="qkv_grads",
    )(core, gt, normed, gains, mlp_gain)


def out_grads_kernel(core_ref, branch_ref, *refs, shard):
    att_refs, (own_ref, low_ref, high_ref) = refs[:-3], refs[-3:]
    att = jnp.concatenate([ref[...] for ref in att_refs], axis=1)
    rows = dot(branch_ref[...], att, 0, 1).astype(BF16)
    half = low_ref.shape[0]
    split_rows(core_ref, rows[: 2 * half * shard], shard, own_ref.at[:half], low_ref)
    split_rows(core_ref, rows[2 * half * shard :], shard, own_ref.at[half:], high_ref)


def out_grads(core, branch, atts, shard):
    width = branch.shape[1]
    heads = atts[0].shape[0]
    return pl.pallas_call(
        functools.partial(out_grads_kernel, shard=shard),
        in_specs=[smem()] + vmem(1 + len(atts)),
        out_shape=(
            shape(width // shard // 2, shard, heads),
            shape(width // shard // 4, shard, heads),
            shape(width // shard // 4, shard, heads),
        ),
        compiler_params=pltpu.CompilerParams(vmem_limit_bytes=VMEM),
        cost_estimate=cost(0.1),
        name="out_grads",
    )(core, branch, *atts)


def out_blocks_kernel(x_ref, sums_ref, got_ref, out_ref):
    total = (sums_ref[x_ref[0]].astype(F32) + got_ref[...].astype(F32)).astype(BF16)
    part = out_ref.shape[2]
    for j in range(out_ref.shape[0]):
        out_ref[j] = total[:, j * part : (j + 1) * part]


def out_blocks(x_hi, sums, got, n_seq):
    shard, heads = got.shape
    return pl.pallas_call(
        out_blocks_kernel,
        in_specs=[smem()] + vmem(2),
        out_shape=shape(n_seq, shard, heads // n_seq),
        compiler_params=pltpu.CompilerParams(vmem_limit_bytes=VMEM),
        cost_estimate=cost(0.1),
        name="out_blocks",
    )(x_hi, sums, got)


def shards_kernel(
    in_ref, wq_ref, wk_ref, wv_ref, gain_ref,
    gq_ref, gk_ref, gv_ref, go_ref, *gain_refs, q_own, kv_own,
):
    n = in_ref.shape[0]

    def side(start, stop):
        return jnp.concatenate([in_ref[j][:, start:stop] for j in range(n)], axis=1).astype(F32)

    k_at, v_at, end = q_own, q_own + kv_own, q_own + 2 * kv_own
    gq, gk, gv = side(0, k_at), side(k_at, v_at), side(v_at, end)
    gq_ref[...], gk_ref[...], gv_ref[...] = gq, gk, gv
    go_ref[...] = side(end + HEAD, end + HEAD + q_own)
    attn = sum(
        jnp.sum(w[...].astype(F32) * g, axis=1, keepdims=True)
        for w, g in ((wq_ref, gq), (wk_ref, gk), (wv_ref, gv))
    ) / gain_ref[...].astype(F32)
    sums = jnp.sum(in_ref[:, :, 256:384].astype(F32), axis=0)
    lane = lax.broadcasted_iota(jnp.int32, sums.shape, 1)
    gains = jnp.where(lane == 0, attn, sums).T
    at = v_at + kv_own - 256
    for row, ref in zip((0, at, at + 1, at + 2), gain_refs):
        ref[...] = gains[row : row + 1, : ref.shape[1]]


def own_shards(parts, w_query, w_key, w_value, attn_gain, q_own, kv_own, gain_own):
    shard, q_all = w_query.shape
    return pl.pallas_call(
        functools.partial(shards_kernel, q_own=q_own, kv_own=kv_own),
        out_shape=(
            shape(shard, q_all, dtype=F32),
            shape(shard, w_key.shape[1], dtype=F32),
            shape(shard, w_value.shape[1], dtype=F32),
            shape(shard, q_all, dtype=F32),
            shape(1, shard, dtype=F32),
            shape(1, gain_own, dtype=F32),
            shape(1, gain_own, dtype=F32),
            shape(1, shard, dtype=F32),
        ),
        compiler_params=pltpu.CompilerParams(vmem_limit_bytes=VMEM),
        cost_estimate=cost(1),
        name="own_shards",
    )(parts, w_query, w_key, w_value, attn_gain)


def mlp_shards_kernel(x_ref, grads_ref, got_ref, gate_ref, up_ref, down_ref):
    width = gate_ref.shape[1]
    total = grads_ref[x_ref[0]].astype(F32) + got_ref[...].astype(F32)
    for k, ref in enumerate((gate_ref, up_ref, down_ref)):
        ref[...] = total[:, k * PAD : k * PAD + width]


def mlp_shards(x_hi, grads, got, width):
    return pl.pallas_call(
        mlp_shards_kernel,
        in_specs=[smem()] + vmem(2),
        out_shape=(shape(got.shape[0], width, dtype=F32),) * 3,
        compiler_params=pltpu.CompilerParams(vmem_limit_bytes=VMEM),
        cost_estimate=cost(1),
        name="mlp_shards",
    )(x_hi, grads, got)


def shift(size, by):
    return [(i, (i + by) % size) for i in range(size)]


def to_all(block):
    n = lax.axis_size("seq")
    return lax.all_to_all(jnp.broadcast_to(block[None], (n,) + block.shape), "seq", 0, 0, tiled=True)


def exchange(blocks):
    return lax.all_to_all(blocks, "seq", 0, 0, tiled=True)


def total_of(blocks):
    return jnp.sum(blocks.astype(F32), axis=0)


def step_seq(block, dy, dx=0):
    n = lax.axis_size("seq")
    to = [(i, (i + 2 * dy) % n ^ dx) for i in range(n)]
    return lax.ppermute(block, "seq", to)


def gather_pieces(block):
    half = block.shape[0] // 2
    up, down = step_seq(block, 1), step_seq(block, -1)
    beside = step_seq(block, 0, 1)
    beside_up, beside_down = step_seq(beside, 1), step_seq(beside, -1)
    return (
        block,
        beside,
        up,
        down,
        beside_up,
        beside_down,
        step_seq(up[:half], 1),
        step_seq(down[half:], -1),
        step_seq(beside_up[:half], 1),
        step_seq(beside_down[half:], -1),
    )


def along_y(pair):
    return (pair,) + tuple(step_seq(pair, -dy) for dy in STEPS[1:])


def near_of(parts, sign=1):
    return tuple(step_seq(parts[i], sign * STEPS[i]) for i in (1, 2))


def sum_pairs(pairs):
    total = sum(pair.astype(F32) for pair in pairs)
    return total[0] + step_seq(total[1].astype(pairs[0].dtype), 0, 1).astype(F32)


def pairs_for(blocks):
    n = lax.axis_size("seq")
    me = lax.axis_index("seq")
    y, x = me // 2, me % 2
    grid = blocks.reshape((n // 2, 2) + blocks.shape[1:])
    grid = jnp.where(x == 0, grid, grid[:, ::-1])
    pick = functools.partial(lax.dynamic_index_in_dim, grid, axis=0, keepdims=False)
    return [pick((y + dy) % (n // 2)) for dy in STEPS]


def in_order_kernel(me_ref, *refs, n_seq):
    out_ref = refs[-1]
    for dy, ref in zip(STEPS, refs[:-1]):
        for dx in range(2):
            out_ref[block_at(me_ref, dy, dx, n_seq)] = ref[dx]


def in_order(me, pairs, n_seq):
    return pl.pallas_call(
        functools.partial(in_order_kernel, n_seq=n_seq),
        in_specs=[smem()] + vmem(len(pairs)),
        out_shape=shape(n_seq, *pairs[0].shape[1:]),
        compiler_params=pltpu.CompilerParams(vmem_limit_bytes=VMEM),
        cost_estimate=cost(0.1),
        name="in_order",
    )(me, *pairs)


def swap(held, bit):
    n = lax.axis_size("fsdp")
    return lax.ppermute(held, "fsdp", [(i, i ^ bit) for i in range(n)])


def along_z(grid):
    n = lax.axis_size("fsdp")
    z = lax.axis_index("fsdp") // 4
    grid = grid.reshape((n // 4, 2) + grid.shape[1:])
    pick = functools.partial(lax.dynamic_index_in_dim, grid, axis=0, keepdims=False)
    got = [lax.ppermute(pick((z + by) % (n // 4)), "fsdp", shift(n, 4 * by)) for by in range(1, 4)]
    return [pick(z)] + got


def sum_z(pairs):
    x_hi = lax.axis_index("fsdp") // 2 % 2
    pick = functools.partial(lax.dynamic_index_in_dim, axis=0, keepdims=False)
    held = sum(pair.astype(F32) for pair in pairs)
    got = swap(pick(held, 1 - x_hi).astype(pairs[0].dtype), 2)
    return pick(held, x_hi) + got.astype(F32)


def pair(mine, other, low):
    return jnp.concatenate([jnp.where(low, mine, other), jnp.where(low, other, mine)], axis=0)


def gather_fsdp(block, first, second):
    n = lax.axis_size("fsdp")
    me = lax.axis_index("fsdp")
    held = block[None]
    held = pair(held, swap(held, 2), me // 2 % 2 == 0)
    held, _ = lax.optimization_barrier((held, first))
    other = swap(held, 1)
    low = me % 2 == 0
    held = jnp.stack([jnp.where(low, held, other), jnp.where(low, other, held)], axis=1)
    held = held.reshape((1, 4) + block.shape)
    held, _ = lax.optimization_barrier((held, second))
    whole = jnp.zeros((n // 4,) + held.shape[1:], block.dtype)
    z = me // 4
    whole = lax.dynamic_update_slice_in_dim(whole, held, z, 0)
    for by in range(1, n // 4):
        got = lax.ppermute(held, "fsdp", shift(n, 4 * by))
        whole = lax.dynamic_update_slice_in_dim(whole, got, (z - by) % (n // 4), 0)
    return whole.reshape((n * block.shape[0],) + block.shape[1:])


def lanes(array, width):
    return jnp.pad(array, ((0, 0), (0, width - array.shape[1])))


def rows(vector, count):
    return jnp.pad(vector, (0, count - vector.shape[0]))


def on_device(
    tokens,
    segments,
    out_grad,
    attn_gain,
    w_query,
    w_key,
    w_value,
    query_gain,
    key_gain,
    w_out,
    mlp_gain,
    w_gate,
    w_up,
    w_down,
):
    n_seq = lax.axis_size("seq")
    n_fsdp = lax.axis_size("fsdp")
    me = lax.axis_index("seq")
    here = me.astype(jnp.int32).reshape(1)
    core = (lax.axis_index("fsdp") % 2).astype(jnp.int32).reshape(1)
    x_hi = (lax.axis_index("fsdp") // 2 % 2).astype(jnp.int32).reshape(1)
    local, width = tokens.shape[1:]
    shard = attn_gain.shape[0]
    q_all, kv_all = w_query.shape[1], w_key.shape[1]
    q_own, kv_own = q_all // n_seq, kv_all // n_seq
    heads = q_own // HEAD
    qkv_own = q_own + 2 * kv_own
    hidden_own = w_gate.shape[1]
    gain_own = query_gain.shape[0]

    x = tokens[0]
    numbers = lax.pad(
        segments.astype(BF16), jnp.zeros((), BF16), ((0, local - 1, 0), (0, 128 - local, 0))
    )
    x_pieces = gather_pieces(jnp.concatenate([x, numbers], axis=1))

    mlp_pack = jnp.concatenate(
        [w_out.T, lanes(w_gate, PAD), lanes(w_up, PAD), lanes(w_down.T, PAD)], axis=1
    )
    mlp_full = lax.all_gather(mlp_pack, "fsdp", axis=0, tiled=True)

    mlp_pack = jnp.concatenate(
        [w_out.T, lanes(w_gate, PAD), lanes(w_up, PAD), lanes(w_down.T, PAD)], axis=1
    )
    mlp_full = lax.all_gather(mlp_pack, "fsdp", axis=0, tiled=True)

    own = lax.dynamic_slice_in_dim
    head_pack = jnp.concatenate(
        [
            own(w_query, me * q_own, q_own, 1),
            own(w_key, me * kv_own, kv_own, 1),
            own(w_value, me * kv_own, kv_own, 1),
            attn_gain[:, None],
            mlp_gain[:, None],
            rows(query_gain, shard)[:, None],
            rows(key_gain, shard)[:, None],
        ],
        axis=1,
    )
    head_full = gather_fsdp(lanes(head_pack, 384), x_pieces[1], x_pieces[2:4])

    freq = (ROPE_BASE ** (-2.0 * jnp.arange(HEAD // 2, dtype=F32) / HEAD)).reshape(-1, 1)

    after = lax.optimization_barrier
    g_pair = jnp.stack([out_grad[0], step_seq(out_grad[0], 0, 1)])
    g_pair, x_pieces = after((g_pair, x_pieces))
    g_pairs = along_y(g_pair)

    x_all, normed, raw, qt, kt, vt, att, att_parts, lse, pos, gain_rows, gains = attend_forward(
        here, x_pieces, head_full, freq, heads, n_seq, gain_own
    )
    x_all = x_all.reshape(n_seq, local, width)
    att_beside = step_seq(att_parts, 0, 1)
    att_pair, g_pairs = after((jnp.stack([att_parts[0], att_beside[0]]), g_pairs))
    att_first = along_y(att_pair)
    att_sent, att_first = after((att_parts[1], att_first))
    att_second = (to_all(att_sent),)
    g_all = in_order(here, g_pairs, n_seq)
    done = [mlp(here, att_first, x_all, g_all, gain_rows, mlp_full, 0)]
    back_first = exchange(done[0][5])
    att_second, done[0] = after((att_second, done[0]))
    done.append(mlp(here, att_second, x_all, g_all, gain_rows, mlp_full, 1))
    middle_parts, seconds, hiddens, gate_grads, up_grads, back_parts, out_parts, att_own = zip(*done)
    back_sent, back_first = after((back_parts[1], back_first))
    backs = (back_first, exchange(back_sent))
    mine, other = mlp_grads(core, seconds, g_all, gate_grads, up_grads, hiddens, shard)
    mine, other, backs = after((mine, other, backs))
    got = swap(other, 1)

    def sum_fsdp(core_sum):
        parts = lax.psum_scatter(
            core_sum.reshape(n_fsdp // 4, 2, shard, -1),
            "fsdp",
            scatter_dimension=0,
            tiled=True,
            axis_index_groups=[list(range(i, n_fsdp, 4)) for i in range(4)],
        ).reshape(2, shard, -1)
        far = lax.dynamic_index_in_dim(parts, 1 - x_hi[0], 0, keepdims=False)
        return parts, far

    branch, grad_middle, grad_att, grad_mlp_g, middle = middle_back(
        backs, middle_parts, out_grad[0], gain_rows, mlp_full
    )
    grad_heads = exchange(grad_att.reshape(n_seq, q_own, local))
    out_mine, out_low, out_high = out_grads(core, branch, att_own, shard)
    out_core = core_halves(out_mine, swap(out_low, 1), swap(out_high, 1))
    out_parts, branch = after((out_parts, branch))
    out = pairs_for(jnp.concatenate(out_parts, axis=1))
    out, grad_heads, out_core = after((out, grad_heads, out_core))
    out_sums, out_far = sum_fsdp(out_core)

    out_pairs = (out[0], *near_of(out), step_seq(out[3], STEPS[3]))
    gt, *back, gain_grads = attend_backward(
        here, qt, kt, vt, raw, lse, pos, grad_heads, gains, freq, head_full
    )
    qkv_mine, qkv_other = qkv_grads(core, gt, normed, gain_grads, grad_mlp_g, gain_own, shard)
    mine, got, qkv_mine = after((mine, got, qkv_mine))
    chip_sums = core_sums(mine, got)
    back, qkv_other, chip_sums, out_pairs = after((back, qkv_other, chip_sums, out_pairs))
    mlp_sums, mlp_far = sum_fsdp(chip_sums)
    back_pairs = (back[0], *near_of(back), step_seq(back[3], STEPS[3]))
    z_pairs = along_z(core_sums(qkv_mine, swap(qkv_other, 1)))
    out_owned = exchange(out_blocks(x_hi, out_sums, swap(out_far, 2), n_seq))
    z_pairs, out_owned = after((z_pairs, out_owned))
    att_owned = jnp.concatenate([sum_z(z_pairs), total_of(out_owned)], axis=1).astype(BF16)
    att_owned, back_pairs, mlp_far = after((att_owned, back_pairs, mlp_far))
    mlp_got = swap(mlp_far, 2)
    att_seq = to_all(att_owned)
    grad_normed = sum_pairs(back_pairs)
    layer_out = (middle + sum_pairs(out_pairs)).astype(BF16)
    xf = x.astype(F32)
    inverse_x = lax.rsqrt(jnp.mean(xf * xf, axis=-1, keepdims=True) + EPS)
    ux = grad_normed * gain_rows[:1]
    grad_tokens = (
        grad_middle
        + inverse_x * ux
        - xf * inverse_x**3 * jnp.mean(ux * xf, axis=-1, keepdims=True)
    )

    mlp_owned = mlp_shards(x_hi, mlp_sums, mlp_got, hidden_own)
    att_seq, (gw_gate, gw_up, gw_down) = after((att_seq, mlp_owned))
    gw_query, gw_key, gw_value, gw_out, g_attn, g_query, g_key, g_mlp = own_shards(
        att_seq, w_query, w_key, w_value, attn_gain[:, None], q_own, kv_own, gain_own
    )
    return (
        layer_out[None],
        grad_tokens[None],
        g_attn[0],
        gw_query,
        gw_key,
        gw_value,
        g_query[0],
        g_key[0],
        gw_out.T,
        g_mlp[0],
        gw_gate,
        gw_up,
        gw_down.T,
    )


def solution(mesh):
    in_specs = (
        P("fsdp", "seq", None),
        P("fsdp", "seq"),
        P("fsdp", "seq", None),
        P("fsdp"),
        P("fsdp", None),
        P("fsdp", None),
        P("fsdp", None),
        P("fsdp"),
        P("fsdp"),
        P(None, "fsdp"),
        P("fsdp"),
        P("fsdp", "seq"),
        P("fsdp", "seq"),
        P("seq", "fsdp"),
    )
    out_specs = (
        P("fsdp", "seq", None),
        P("fsdp", "seq", None),
        P("fsdp"),
        P("fsdp", None),
        P("fsdp", None),
        P("fsdp", None),
        P("fsdp"),
        P("fsdp"),
        P(None, "fsdp"),
        P("fsdp"),
        P("fsdp", "seq"),
        P("fsdp", "seq"),
        P("seq", "fsdp"),
    )
    return jax.shard_map(
        on_device, mesh=mesh, in_specs=in_specs, out_specs=out_specs, check_vma=False
    )
```
